32 devices in a mesh: dap: 4 (over x, core), dp: 8 (over z, y).
Axes of the slice: x: 2, y: 2, z: 4, core: 2. Of those that a mesh axis runs over, the one named last changes fastest.
Arguments:
- pair_rep: bfloat16 [8, 128, 128, 128], P('dp', 'dap'), may hold values from -6 to 6
- cotangent: bfloat16 [8, 128, 128, 128], P('dp', 'dap'), may hold values from -6 to 6
- tok_mask: int32 [8, 128], P('dp'), may hold values from 0 to 1, as said below
- tok_types: int32 [8, 128], P('dp'), may hold values from 0 to 3
- pair_mask: int32 [8, 128, 128], P('dp', 'dap'), may hold values 0 or 1
- triangle_gain: float32 [128], replicated, may hold values from 0.5 to 1.5
- triangle_input: bfloat16 [128, 512], replicated, may hold values from -0.5 to 0.5
- triangle_gating: bfloat16 [128, 128], replicated, may hold values from -0.5 to 0.5
- product_gain: float32 [128], replicated, may hold values from 0.5 to 1.5
- triangle_output: bfloat16 [128, 128], replicated, may hold values from -0.5 to 0.5
- attend_gain: float32 [128], replicated, may hold values from 0.5 to 1.5
- attend_bias: bfloat16 [128, 4], replicated, may hold values from -0.5 to 0.5
- attend_input: bfloat16 [128, 512], replicated, may hold values from -0.5 to 0.5
- attend_output: bfloat16 [128, 128], replicated, may hold values from -0.5 to 0.5
- type_table: float32 [4, 4, 4], replicated, may hold values from -4 to 4
Outputs:
- pair_out: bfloat16 [8, 128, 128, 128], P('dp', 'dap')
- pair_grad: bfloat16 [8, 128, 128, 128], P('dp', 'dap')
- grad_triangle_gain: float32 [128], replicated
- grad_triangle_input: float32 [128, 512], replicated
- grad_triangle_gating: float32 [128, 128], replicated
- grad_product_gain: float32 [128], replicated
- grad_triangle_output: float32 [128, 128], replicated
- grad_attend_gain: float32 [128], replicated
- grad_attend_bias: float32 [128, 4], replicated
- grad_attend_input: float32 [128, 512], replicated
- grad_attend_output: float32 [128, 128], replicated
- grad_type_table: float32 [4, 4, 4], replicated
The draws below stay inside these ranges and needn't reach their ends.
Inputs may be any that keep to these rules, and one draw needn't show every extreme that they name: `tok_mask`: each crop's real tokens form a leading run of at least 64 tokens.
All inputs are finite; a program needn't handle non-finite values. No bound on the sum of `pair_mask` on one device may be relied on, other than what follows from the above.
Results may differ from the reference program's by a relative error of at most 0.035.
Values may be sent and summed in bfloat16 or wider, within the bound.
No kernel may reach another device: no remote copies, remote signals or barrier semaphores. Data moves between devices by JAX's collectives and lax.ppermute only.
A program may use at most 128 MiB of HBM per device.

```python
from functools import partial
import jax
import jax.numpy as jnp
from jax import lax

C = 128
H = 4
TYPES = 4
N = 128
CROPS = 8
N_DAP = 4
N_DP = 8


def draw_tok_mask(key, part):
    lengths = jax.random.randint(key, (CROPS,), N // 2, N + 1)
    return (jnp.arange(N, dtype=jnp.int32)[None, :] < lengths[:, None]).astype(jnp.int32)


def set_ends(entries, key, least, high):
    dims = entries.shape
    index_at = [jax.random.randint(jax.random.fold_in(key, axis), (), 0, dims[axis]) for axis in range(len(dims))]
    entries = entries.at[tuple(index_at)].set(least)
    longest = dims.index(max(dims))
    index_at[longest] = (index_at[longest] + 1) % dims[longest]
    return entries.at[tuple(index_at)].set(high)


def shard_levels(rng, shape, cuts, least, top_value):
    level = 1.0
    for position, parts in cuts:
        heights = jax.random.uniform(jax.random.fold_in(jax.random.fold_in(rng, 6), position), (parts,), jnp.float32, least / len(cuts), top_value / len(cuts))
        level = level * jnp.repeat(jnp.exp(heights), shape[position] // parts).reshape((-1,) + (1,) * (len(shape) - 1 - position))
    return level


def noise(stream_key, dims, width, most, shards=(), kind=jnp.bfloat16):
    values = jax.random.normal(stream_key, dims, jnp.float32) * width
    if len(shards) > 0:
        values = shard_levels(stream_key, dims, shards, -0.22, 0.18) * values
    return jnp.clip(values, min=-most, max=most).astype(kind)


def setup_inputs(seed: int = 0) -> dict:
    splits = jax.random.split(jax.random.key(seed), 16)
    return {
        "pair_rep": noise(splits[0], (CROPS, N, N, C), 1.0, 6.0, ((0, 8), (1, 4))),
        "cotangent": noise(splits[1], (CROPS, N, N, C), 1.0, 6.0, ((0, 8), (1, 4))),
        "tok_mask": draw_tok_mask(jax.random.fold_in(splits[15], 71), 0),
        "tok_types": set_ends(jax.random.randint(splits[3], (CROPS, N), 0, TYPES), jax.random.fold_in(splits[3], 1), 0, TYPES - 1).astype(jnp.int32),
        "pair_mask": set_ends((jax.random.randint(splits[4], (CROPS, N, N), 0, 8) < 7).astype(jnp.int32), jax.random.fold_in(splits[4], 1), 0, 1),
        "triangle_gain": jnp.clip(1.0 + 0.1 * jax.random.normal(splits[5], (C,), jnp.float32), 0.5, 1.5),
        "triangle_input": noise(splits[6], (C, 4 * C), C ** -0.5, 0.5),
        "triangle_gating": noise(splits[7], (C, C), C ** -0.5, 0.5),
        "product_gain": jnp.clip(1.0 + 0.1 * jax.random.normal(splits[8], (C,), jnp.float32), 0.5, 1.5),
        "triangle_output": noise(splits[9], (C, C), C ** -0.5, 0.5),
        "attend_gain": jnp.clip(1.0 + 0.1 * jax.random.normal(splits[10], (C,), jnp.float32), 0.5, 1.5),
        "attend_bias": noise(splits[11], (C, H), C ** -0.5, 0.5),
        "attend_input": noise(splits[12], (C, 4 * C), C ** -0.5, 0.5),
        "attend_output": noise(splits[13], (C, C), C ** -0.5, 0.5),
        "type_table": noise(splits[14], (H, TYPES, TYPES), 1.0, 4.0, (), jnp.float32),
    }


EPSILON = 1e-05

def layer_norm(values, scales):
    centred = values - lax.optimization_barrier(jnp.mean(values, axis=-1, keepdims=True))
    spread = lax.optimization_barrier(jnp.mean(centred * centred, axis=-1, keepdims=True))
    return centred * lax.rsqrt(spread + EPSILON) * scales

def triangle_first(slab, scales, input_w, gating_w, pair_live):
    channels = slab.shape[-1]
    normed = layer_norm(slab.astype(jnp.float32), scales).astype(jnp.bfloat16)
    projected = jnp.einsum('ijc,cd->ijd', normed.astype(jnp.float32), input_w.astype(jnp.float32))
    masked = pair_live[..., None]
    left_proj = (jax.nn.sigmoid(projected[..., channels:2 * channels]) * projected[..., :channels] * masked).astype(jnp.bfloat16)
    right_proj = (jax.nn.sigmoid(projected[..., 3 * channels:]) * projected[..., 2 * channels:3 * channels] * masked).astype(jnp.bfloat16)
    out_gate = jax.nn.sigmoid(jnp.einsum('ijc,cd->ijd', normed.astype(jnp.float32), gating_w.astype(jnp.float32)))
    return (left_proj, right_proj, out_gate)

def triangle_second(slab, product, out_gate, scales, output_w):
    normed = layer_norm(product, scales).astype(jnp.bfloat16)
    update = out_gate * jnp.einsum('ijc,cd->ijd', normed.astype(jnp.float32), output_w.astype(jnp.float32))
    return (slab.astype(jnp.float32) + update).astype(jnp.bfloat16)

def attend_first(middle, scales, bias_w):
    normed = layer_norm(middle.astype(jnp.float32), scales).astype(jnp.bfloat16)
    bias_rows = jnp.einsum('rjc,ch->hrj', normed.astype(jnp.float32), bias_w.astype(jnp.float32)).astype(jnp.bfloat16)
    return (normed, bias_rows)

def attend_second(middle, normed, bias_all, table, input_w, output_w, one_hot, key_live):
    row_count, length, channels = middle.shape
    head_count = bias_all.shape[0]
    head_size = channels // head_count
    projected = jnp.einsum('ijc,cd->ijd', normed.astype(jnp.float32), input_w.astype(jnp.float32))
    query = projected[..., :channels].astype(jnp.bfloat16).reshape(row_count, length, head_count, head_size)
    keys_all = projected[..., channels:2 * channels].astype(jnp.bfloat16).reshape(row_count, length, head_count, head_size)
    values_all = projected[..., 2 * channels:3 * channels].astype(jnp.bfloat16).reshape(row_count, length, head_count, head_size)
    gate = jax.nn.sigmoid(projected[..., 3 * channels:])
    type_bias = jnp.einsum('ja,hab,kb->hjk', one_hot, table, one_hot)
    scores = jnp.einsum('rjhd,rkhd->rhjk', query.astype(jnp.float32), keys_all.astype(jnp.float32)) / jnp.sqrt(jnp.float32(head_size))
    scores = scores + (bias_all + type_bias)[None]
    exponent = jnp.exp(scores) * key_live[:, None, None, :]
    totals = jnp.maximum(lax.optimization_barrier(jnp.sum(exponent, axis=-1, keepdims=True)), 1.0)
    weights = (exponent / totals).astype(jnp.bfloat16)
    attended = jnp.einsum('rhjk,rkhd->rjhd', weights.astype(jnp.float32), values_all.astype(jnp.float32)).reshape(row_count, length, channels)
    gated = (gate * attended).astype(jnp.bfloat16)
    update = jnp.einsum('ijc,cd->ijd', gated.astype(jnp.float32), output_w.astype(jnp.float32))
    return (middle.astype(jnp.float32) + update).astype(jnp.bfloat16)

def reference(pair_rep, cotangent, tok_mask, tok_types, pair_mask, triangle_gain, triangle_input, triangle_gating, product_gain, triangle_output, attend_gain, attend_bias, attend_input, attend_output, type_table):
    span = N // N_DAP

    def one_crop(inputs):
        slab_all, cot_all, tokens_in, types_in, mask_in = inputs
        tokens = tokens_in.astype(jnp.float32)
        pair_live = mask_in.astype(jnp.float32) * tokens[:, None] * tokens[None, :]
        one_hot = (types_in[:, None] == jnp.arange(TYPES, dtype=jnp.int32)[None, :]).astype(jnp.float32)
        first_backs = []
        left_list = []
        right_list = []
        gate_list = []
        for portion in range(N_DAP):
            lower_row = portion * span
            upper_row = lower_row + span
            outputs, pullback = jax.vjp(partial(triangle_first, pair_live=pair_live[lower_row:upper_row]), slab_all[lower_row:upper_row], triangle_gain, triangle_input, triangle_gating)
            first_backs.append(pullback)
            left_list.append(outputs[0])
            right_list.append(outputs[1])
            gate_list.append(outputs[2])
        right_all = jnp.concatenate(right_list, axis=0)
        second_backs = []
        middle_list = []
        third_backs = []
        normed_list = []
        bias_list = []
        for portion in range(N_DAP):
            lower_row = portion * span
            upper_row = lower_row + span
            product = jnp.einsum('ikc,jkc->ijc', left_list[portion].astype(jnp.float32), right_all.astype(jnp.float32))
            middle, pullback = jax.vjp(triangle_second, slab_all[lower_row:upper_row], product, gate_list[portion], product_gain, triangle_output)
            second_backs.append(pullback)
            middle_list.append(middle)
            outputs, pullback = jax.vjp(attend_first, middle, attend_gain, attend_bias)
            third_backs.append(pullback)
            normed_list.append(outputs[0])
            bias_list.append(outputs[1])
        bias_all = jnp.concatenate(bias_list, axis=1).astype(jnp.float32)
        fourth_backs = []
        out_list = []
        for portion in range(N_DAP):
            lower_row = portion * span
            upper_row = lower_row + span
            result, pullback = jax.vjp(partial(attend_second, one_hot=one_hot, key_live=pair_live[lower_row:upper_row]), middle_list[portion], normed_list[portion], bias_all, type_table, attend_input, attend_output)
            fourth_backs.append(pullback)
            out_list.append(result)
        fourth_grads = [fourth_backs[portion](cot_all[portion * span:(portion + 1) * span]) for portion in range(N_DAP)]
        bias_grad = fourth_grads[0][2]
        for portion in range(1, N_DAP):
            bias_grad = bias_grad + fourth_grads[portion][2]
        bias_grad = bias_grad.astype(jnp.bfloat16)
        grads = [jnp.zeros_like(triangle_gain), jnp.zeros(triangle_input.shape, jnp.float32), jnp.zeros(triangle_gating.shape, jnp.float32), jnp.zeros_like(product_gain), jnp.zeros(triangle_output.shape, jnp.float32), jnp.zeros_like(attend_gain), jnp.zeros(attend_bias.shape, jnp.float32), jnp.zeros(attend_input.shape, jnp.float32), jnp.zeros(attend_output.shape, jnp.float32), jnp.zeros_like(type_table)]
        d_product_list = []
        d_gate_list = []
        d_slab_list = []
        for portion in range(N_DAP):
            lower_row = portion * span
            upper_row = lower_row + span
            d_middle_a, d_normed, unused_bias, d_table, d_att_in, d_att_out = fourth_grads[portion]
            d_middle_b, d_att_gain, d_att_bias = third_backs[portion]((d_normed, bias_grad[:, lower_row:upper_row]))
            d_middle = d_middle_a + d_middle_b
            d_slab_c, d_product, d_gate, d_prod_gain, d_tri_out = second_backs[portion](d_middle)
            d_product_list.append(d_product)
            d_gate_list.append(d_gate)
            d_slab_list.append(d_slab_c)
            grads[3] = grads[3] + d_prod_gain.astype(jnp.float32)
            grads[4] = grads[4] + d_tri_out.astype(jnp.float32)
            grads[5] = grads[5] + d_att_gain.astype(jnp.float32)
            grads[6] = grads[6] + d_att_bias.astype(jnp.float32)
            grads[7] = grads[7] + d_att_in.astype(jnp.float32)
            grads[8] = grads[8] + d_att_out.astype(jnp.float32)
            grads[9] = grads[9] + d_table.astype(jnp.float32)
        d_right_all = jnp.zeros(right_all.shape, jnp.float32)
        for portion in range(N_DAP):
            d_right_all = d_right_all + jnp.einsum('ijc,ikc->jkc', d_product_list[portion], left_list[portion].astype(jnp.float32), precision=lax.Precision.HIGHEST)
        d_right_all = d_right_all.astype(jnp.bfloat16)
        grad_list = []
        for portion in range(N_DAP):
            lower_row = portion * span
            upper_row = lower_row + span
            d_left = jnp.einsum('ijc,jkc->ikc', d_product_list[portion], right_all.astype(jnp.float32), precision=lax.Precision.HIGHEST).astype(jnp.bfloat16)
            d_slab_d, d_tri_gain, d_tri_in, d_tri_gate = first_backs[portion]((d_left, d_right_all[lower_row:upper_row], d_gate_list[portion]))
            grads[0] = grads[0] + d_tri_gain.astype(jnp.float32)
            grads[1] = grads[1] + d_tri_in.astype(jnp.float32)
            grads[2] = grads[2] + d_tri_gate.astype(jnp.float32)
            grad_list.append(d_slab_list[portion] + d_slab_d)
        return (jnp.concatenate(out_list, axis=0), jnp.concatenate(grad_list, axis=0), tuple(grads))
    pair_out, pair_grad, crop_grads = lax.map(one_crop, (pair_rep, cotangent, tok_mask, tok_types, pair_mask))
    factor = jnp.float32((N * N * N_DP) ** (-0.5))
    summed = [lax.optimization_barrier(jnp.sum(member, axis=0)) * factor for member in crop_grads]
    return (pair_out, pair_grad, summed[0], summed[1], summed[2], summed[3], summed[4], summed[5], summed[6], summed[7], summed[8], summed[9])
```

```python
from functools import partial

import jax
import jax.numpy as jnp
from jax import lax
from jax.sharding import PartitionSpec as P

EPSILON = 1e-05


def layer_norm(values, scales):
    centred = values - jnp.mean(values, axis=-1, keepdims=True)
    spread = jnp.mean(centred * centred, axis=-1, keepdims=True)
    return centred * lax.rsqrt(spread + EPSILON) * scales


def triangle_first(slab, scales, input_w, gating_w, pair_live):
    channels = slab.shape[-1]
    normed = layer_norm(slab.astype(jnp.float32), scales).astype(jnp.bfloat16)
    projected = jnp.einsum("ijc,cd->ijd", normed, input_w, preferred_element_type=jnp.float32)
    masked = pair_live[..., None]
    left_proj = (
        jax.nn.sigmoid(projected[..., channels : 2 * channels]) * projected[..., :channels] * masked
    ).astype(jnp.bfloat16)
    right_proj = (
        jax.nn.sigmoid(projected[..., 3 * channels :])
        * projected[..., 2 * channels : 3 * channels]
        * masked
    ).astype(jnp.bfloat16)
    out_gate = jax.nn.sigmoid(
        jnp.einsum("ijc,cd->ijd", normed, gating_w, preferred_element_type=jnp.float32)
    )
    return (left_proj, right_proj, out_gate)


def triangle_second(slab, product, out_gate, scales, output_w):
    normed = layer_norm(product, scales).astype(jnp.bfloat16)
    update = out_gate * jnp.einsum(
        "ijc,cd->ijd", normed, output_w, preferred_element_type=jnp.float32
    )
    return (slab.astype(jnp.float32) + update).astype(jnp.bfloat16)


def attend_first(middle, scales, bias_w):
    normed = layer_norm(middle.astype(jnp.float32), scales).astype(jnp.bfloat16)
    bias_rows = jnp.einsum(
        "rjc,ch->hrj", normed, bias_w, preferred_element_type=jnp.float32
    ).astype(jnp.bfloat16)
    return (normed, bias_rows)


def attend_second(middle, normed, bias_all, table, input_w, output_w, one_hot, key_live):
    row_count, length, channels = middle.shape
    head_count = bias_all.shape[0]
    head_size = channels // head_count
    projected = jnp.einsum("ijc,cd->ijd", normed, input_w, preferred_element_type=jnp.float32)
    query = (
        projected[..., :channels]
        .astype(jnp.bfloat16)
        .reshape(row_count, length, head_count, head_size)
    )
    keys_all = (
        projected[..., channels : 2 * channels]
        .astype(jnp.bfloat16)
        .reshape(row_count, length, head_count, head_size)
    )
    values_all = (
        projected[..., 2 * channels : 3 * channels]
        .astype(jnp.bfloat16)
        .reshape(row_count, length, head_count, head_size)
    )
    gate = jax.nn.sigmoid(projected[..., 3 * channels :])
    type_bias = jnp.einsum("ja,hab,kb->hjk", one_hot, table, one_hot)
    scores = jnp.einsum(
        "rjhd,rkhd->rhjk", query, keys_all, preferred_element_type=jnp.float32
    ) / jnp.sqrt(jnp.float32(head_size))
    scores = scores + (bias_all + type_bias)[None]
    exponent = jnp.exp(scores) * key_live[:, None, None, :]
    totals = jnp.maximum(jnp.sum(exponent, axis=-1, keepdims=True), 1.0)
    weights = (exponent / totals).astype(jnp.bfloat16)
    attended = jnp.einsum(
        "rhjk,rkhd->rjhd", weights, values_all, preferred_element_type=jnp.float32
    ).reshape(row_count, length, channels)
    gated = (gate * attended).astype(jnp.bfloat16)
    update = jnp.einsum("ijc,cd->ijd", gated, output_w, preferred_element_type=jnp.float32)
    return (middle.astype(jnp.float32) + update).astype(jnp.bfloat16)


def swap(value, axis, step):
    count = lax.axis_size(axis)
    return lax.ppermute(value, axis, [(index, index ^ step) for index in range(count)])


def gather_rows(block, axis, dim):
    place = lax.axis_index(axis)
    size = block.shape[dim]
    blocks = {0: block}
    steps = [1 << bit for bit in reversed(range(lax.axis_size(axis).bit_length() - 1))]
    for step in steps:
        for offset, held in list(blocks.items()):
            blocks[offset ^ step] = swap(held, axis, step)
    shape = list(block.shape)
    shape[dim] = size * lax.axis_size(axis)
    whole = jnp.zeros(shape, block.dtype)
    for offset, held in blocks.items():
        whole = lax.dynamic_update_slice_in_dim(whole, held, (place ^ offset) * size, dim)
    return whole


def scatter_rows(parts, axis, dim):
    place = lax.axis_index(axis)
    count = lax.axis_size(axis)
    size = parts.shape[dim] // count
    held = {
        offset: lax.dynamic_slice_in_dim(parts, (place ^ offset) * size, size, dim)
        for offset in range(count)
    }
    step = 1
    while step < count:
        for offset in [o for o in held if o & step]:
            arrived = swap(held.pop(offset).astype(jnp.bfloat16), axis, step)
            held[offset ^ step] = held[offset ^ step] + arrived.astype(jnp.float32)
        step *= 2
    return held[0]


def sum_everywhere(terms, axes):
    flat = [term.astype(jnp.float32).reshape(-1) for term in terms]
    sizes = [part.shape[0] for part in flat]
    packed = jnp.concatenate(flat)
    pad = -packed.shape[0] % 2048
    packed = jnp.pad(packed, (0, pad)).reshape(-1, 128)
    for axis in axes:
        step = 1
        while step < lax.axis_size(axis):
            packed = packed + swap(packed.astype(jnp.bfloat16), axis, step).astype(jnp.float32)
            step *= 2
    packed = packed.reshape(-1)
    out, start = [], 0
    for term, size in zip(terms, sizes):
        out.append(packed[start : start + size].reshape(term.shape))
        start += size
    return out


def per_device(
    pair_rep,
    cotangent,
    tok_mask,
    tok_types,
    pair_mask,
    triangle_gain,
    triangle_input,
    triangle_gating,
    product_gain,
    triangle_output,
    attend_gain,
    attend_bias,
    attend_input,
    attend_output,
    type_table,
):
    slab = pair_rep[0]
    row_count = slab.shape[0]
    length = slab.shape[1]
    tokens = tok_mask[0].astype(jnp.float32)
    first_row = lax.axis_index("dap") * row_count
    row_tokens = lax.dynamic_slice_in_dim(tokens, first_row, row_count)
    pair_live = pair_mask[0].astype(jnp.float32) * row_tokens[:, None] * tokens[None, :]
    one_hot = (
        tok_types[0][:, None] == jnp.arange(type_table.shape[1], dtype=jnp.int32)[None, :]
    ).astype(jnp.float32)
    first_out, first_back = jax.vjp(
        partial(triangle_first, pair_live=pair_live),
        slab,
        triangle_gain,
        triangle_input,
        triangle_gating,
    )
    left_proj, right_proj, out_gate = first_out
    right_all = gather_rows(right_proj, "dap", 0)
    product = jnp.einsum("ikc,jkc->ijc", left_proj, right_all, preferred_element_type=jnp.float32)
    middle, second_back = jax.vjp(
        triangle_second, slab, product, out_gate, product_gain, triangle_output
    )
    third_out, third_back = jax.vjp(attend_first, middle, attend_gain, attend_bias)
    normed, bias_rows = third_out
    bias_all = gather_rows(bias_rows, "dap", 1).astype(jnp.float32)
    pair_out, fourth_back = jax.vjp(
        partial(attend_second, one_hot=one_hot, key_live=pair_live),
        middle,
        normed,
        bias_all,
        type_table,
        attend_input,
        attend_output,
    )
    d_middle_a, d_normed, d_bias_all, d_table, d_att_in, d_att_out = fourth_back(cotangent[0])
    d_bias_rows = scatter_rows(d_bias_all, "dap", 1).astype(jnp.bfloat16)
    d_middle_b, d_att_gain, d_att_bias = third_back((d_normed, d_bias_rows))
    attend_terms = (
        d_att_gain,
        d_att_bias.astype(jnp.float32),
        d_att_in.astype(jnp.float32),
        d_att_out.astype(jnp.float32),
        d_table,
    )
    d_middle = d_middle_a + d_middle_b
    d_slab_c, d_product, d_gate, d_prod_gain, d_tri_out = second_back(d_middle)
    d_left = jnp.einsum(
        "ijc,jkc->ikc", d_product, right_all, preferred_element_type=jnp.float32
    ).astype(jnp.bfloat16)
    d_right_parts = jnp.einsum(
        "ijc,ikc->jkc", d_product, left_proj, preferred_element_type=jnp.float32
    )
    d_right = scatter_rows(d_right_parts, "dap", 0).astype(jnp.bfloat16)
    d_slab_d, d_tri_gain, d_tri_in, d_tri_gate = first_back((d_left, d_right, d_gate))
    d_slab = d_slab_c + d_slab_d
    triangle_terms = (
        d_tri_gain,
        d_tri_in.astype(jnp.float32),
        d_tri_gate.astype(jnp.float32),
        d_prod_gain,
        d_tri_out.astype(jnp.float32),
    )
    triangle_summed = sum_everywhere(triangle_terms, ("dap", "dp"))
    attend_summed = sum_everywhere(attend_terms, ("dap", "dp"))
    factor = (length * length * lax.axis_size("dp")) ** (-0.5)
    return (
        pair_out[None],
        d_slab[None],
        triangle_summed[0] * factor,
        triangle_summed[1] * factor,
        triangle_summed[2] * factor,
        triangle_summed[3] * factor,
        triangle_summed[4] * factor,
        attend_summed[0] * factor,
        attend_summed[1] * factor,
        attend_summed[2] * factor,
        attend_summed[3] * factor,
        attend_summed[4] * factor,
    )


def solution(mesh):
    return jax.shard_map(
        per_device,
        mesh=mesh,
        in_specs=(
            P("dp", "dap", None, None),
            P("dp", "dap", None, None),
            P("dp", None),
            P("dp", None),
            P("dp", "dap", None),
            P(),
            P(),
            P(),
            P(),
            P(),
            P(),
            P(),
            P(),
            P(),
            P(),
        ),
        out_specs=(
            P("dp", "dap", None, None),
            P("dp", "dap", None, None),
            P(),
            P(),
            P(),
            P(),
            P(),
            P(),
            P(),
            P(),
            P(),
            P(),
        ),
        check_vma=False,
    )
```

```python
from functools import partial

import jax
import jax.numpy as jnp
from jax import lax
from jax.experimental import pallas as pl
from jax.experimental.pallas import tpu as pltpu
from jax.sharding import PartitionSpec as P

EPSILON = 1e-05
F32 = jnp.float32
BF16 = jnp.bfloat16
VMEM_LIMIT = 16 * 1024 * 1024
HEAD_ROWS = 16


def mm(left, right):
    return lax.dot_general(left, right, (((1,), (0,)), ((), ())), preferred_element_type=F32)


def mmt(left, right):
    return lax.dot_general(left, right, (((1,), (1,)), ((), ())), preferred_element_type=F32)


def sigmoid(value):
    return 1.0 / (1.0 + jnp.exp(-value))


def identity(size):
    rows = lax.broadcasted_iota(jnp.int32, (size, size), 0)
    columns = lax.broadcasted_iota(jnp.int32, (size, size), 1)
    return (rows == columns).astype(F32).astype(BF16)


def norm_parts(values, axis):
    centred = values - jnp.mean(values, axis=axis, keepdims=True)
    spread = jnp.mean(centred * centred, axis=axis, keepdims=True)
    scale = lax.rsqrt(spread + EPSILON)
    return centred * scale, scale


def norm_back(d_hat, hat, scale, axis):
    first = jnp.mean(d_hat, axis=axis, keepdims=True)
    second = jnp.mean(d_hat * hat, axis=axis, keepdims=True)
    return scale * (d_hat - first - hat * second)


def lockstep(row, indices):
    going = [row(index) for index in indices]
    results = [None] * len(going)
    running = True
    while running:
        for at, one in enumerate(going):
            try:
                next(one)
            except StopIteration as stop:
                results[at] = stop.value
                running = False
    return results


def over_rows(count, width, row, finish=None):
    def some(index, carry):
        results = lockstep(row, [index * width + at for at in range(width)])
        if finish is not None:
            finish(results)
        return carry

    lax.fori_loop(0, count // width, some, 0)


def call(kernel, outs, args, scratch=(), grid=(), in_specs=None, out_specs=None, us=5.0, name=None):
    whole = pl.BlockSpec(memory_space=pltpu.VMEM)
    return pl.pallas_call(
        kernel,
        out_shape=[jax.ShapeDtypeStruct(shape, dtype) for shape, dtype in outs],
        grid=grid,
        in_specs=in_specs or [whole] * len(args),
        out_specs=out_specs or [whole] * len(outs),
        scratch_shapes=list(scratch),
        compiler_params=pltpu.CompilerParams(vmem_limit_bytes=VMEM_LIMIT),
        cost_estimate=pl.CostEstimate(
            flops=int(us * 1.0e9), bytes_accessed=int(us * 3.0e6), transcendentals=0
        ),
        name=name,
    )(*args)


def right_kernel(pair, live, gain, weight, normed_out, right_out, weight_t, lay):
    rows, length, channels = pair.shape
    weight_t[...] = weight[:, 2 * channels : 4 * channels].astype(F32).T.astype(BF16)

    def row(i):
        hat, _ = norm_parts(pair[i].astype(F32), -1)
        yield
        normed = (hat * gain[...]).astype(BF16)
        normed_out[i] = normed
        projected = mmt(weight_t[...], normed)
        yield
        right = sigmoid(projected[channels:]) * projected[:channels] * live[pl.ds(i, 1), :]
        lay[pl.ds(i, channels, stride=rows), :] = right

    over_rows(rows, 4, row)
    right_out[...] = lay[...].reshape(channels, rows, length).astype(BF16)


def left_kernel(parts, *refs):
    normed_parts = refs[:parts]
    live, weight, gating = refs[parts : parts + 3]
    normed_out, left_out, gate_out, weight_t, lay = refs[parts + 3 :]
    rows, length, channels = normed_out.shape
    half = rows // parts
    weight_t[...] = weight[:, : 2 * channels].astype(F32).T.astype(BF16)
    for part in range(parts):

        def row(i, part=part):
            normed = normed_parts[part][i]
            at = i + part * half
            normed_out[at] = normed
            projected = mmt(weight_t[...], normed)
            gate = mm(normed, gating[...])
            yield
            left = sigmoid(projected[channels:]) * projected[:channels] * live[pl.ds(at, 1), :]
            lay[pl.ds(at, channels, stride=rows), :] = left
            gate_out[at] = sigmoid(gate).astype(BF16)

        over_rows(half, 4, row)
    left_out[...] = lay[...].reshape(channels, rows, length).astype(BF16)


def product_kernel(count, place_ref, *refs):
    blocks = refs[: 2 * count]
    (left, pair, gate, gain2_col, gain3, output_w, bias_w) = refs[2 * count : 2 * count + 7]
    (right_all, normed2_out, scale2_out, update_out, middle_out, normed3_out, bias_out) = refs[
        2 * count + 7 : 2 * count + 14
    ]
    product, bias_scr = refs[2 * count + 14 :]
    channels, rows, length = left.shape
    heads = bias_w.shape[1]
    half = rows // 2
    starts = [
        pl.multiple_of((place_ref[0] ^ (index // 2)) * rows + (index % 2) * half, half)
        for index in range(2 * count)
    ]

    def channel(c, carry):
        for start, ref in zip(starts, blocks):
            right_all[c, pl.ds(start, half), :] = ref[c]
        return carry

    lax.fori_loop(0, channels, channel, 0, unroll=4)

    def multiply(c, carry):
        product[pl.ds(c, rows, stride=channels), :] = mmt(left[c], right_all[c])
        return carry

    lax.fori_loop(0, channels, multiply, 0, unroll=8)
    eye = identity(channels)
    gain2 = jnp.broadcast_to(gain2_col[...], (channels, length))
    bias_t = jnp.concatenate(
        [bias_w[...].astype(F32).T, jnp.zeros((HEAD_ROWS - heads, channels), F32)], axis=0
    ).astype(BF16)

    def row(i):
        hat, scale = norm_parts(product[pl.ds(i * channels, channels), :], 0)
        yield
        normed2_t = (hat * gain2).astype(BF16)
        normed2_out[i] = normed2_t
        scale2_out[pl.ds(i, 1), :] = scale
        normed2 = mmt(eye, normed2_t).astype(BF16)
        yield
        update = mm(normed2, output_w[...])
        yield
        update_out[i] = update.astype(BF16)
        middle = (pair[i].astype(F32) + gate[i].astype(F32) * update).astype(BF16)
        middle_out[i] = middle
        hat3, _ = norm_parts(middle.astype(F32), -1)
        yield
        normed3 = (hat3 * gain3[...]).astype(BF16)
        normed3_out[i] = normed3
        bias_scr[pl.ds(i * HEAD_ROWS, HEAD_ROWS), :] = mmt(bias_t, normed3)

    over_rows(rows, 4, row)
    for h in range(heads):
        head = bias_scr[pl.ds(h, rows, stride=HEAD_ROWS), :]
        bias_out[:, h * length : (h + 1) * length] = head.astype(BF16)


def attend_kernel(
    count, block, place_ref, table, *refs
):
    bias_refs = refs[:count]
    (types_row, types_col, live, normed3, middle, cotangent, input_w, output_w) = refs[
        count : count + 8
    ]
    (pair_out, d_projected, d_output, d_table) = refs[count + 8 : count + 12]
    d_bias_outs = refs[count + 12 : 2 * count + 12]
    bias, d_bias, head_mask, weight_t, weight_qg = refs[2 * count + 12 :]
    length, channels = normed3.shape[1:]
    types = table.shape[1]
    heads = table.shape[0] // types
    size = channels // heads
    own = bias_refs[0].shape[0]
    factor = size ** -0.5
    place = place_ref[0]
    step = pl.program_id(0)

    def spans(h):
        return slice(h * length, (h + 1) * length)

    @pl.when(step == 0)
    def _():
        for offset in range(count):
            start = pl.multiple_of((place ^ offset) * own, own)
            bias[pl.ds(start, own), :] = bias_refs[offset][...].astype(F32)
        row_types = types_row[...]
        col_types = types_col[...]
        for h in range(heads):
            total = jnp.zeros((length, length), F32)
            for a in range(types):
                values = jnp.zeros((1, length), F32)
                for b in range(types):
                    values = jnp.where(row_types == b, table[h * types + a, b], values)
                total = jnp.where(col_types == a, values, total)
            bias[:, spans(h)] = bias[:, spans(h)] + total
        d_bias[...] = jnp.zeros_like(d_bias)
        d_output[...] = jnp.zeros_like(d_output)
        rows = lax.broadcasted_iota(jnp.int32, head_mask.shape, 0) // size
        columns = lax.broadcasted_iota(jnp.int32, head_mask.shape, 1) // length
        head_mask[...] = (rows == columns).astype(F32).astype(BF16)
        weight_t[...] = input_w[:, : 3 * channels].astype(F32).T.astype(BF16)
        weight_qg[:, :channels] = input_w[:, :channels]
        weight_qg[:, channels:] = input_w[:, 3 * channels :]

    eye = identity(channels)

    def row(i):
        live_row = live[pl.ds(step * block + i, 1), :]
        live_wide = jnp.concatenate([live_row.astype(BF16)] * heads, axis=1)
        normed = normed3[i]
        projected_t = mmt(weight_t[...], normed)
        projected = mm(normed, weight_qg[...])
        d_gated = mmt(cotangent[i], output_w[...])
        yield
        query_t = (projected_t[:channels] * factor).astype(BF16)
        key_t = projected_t[channels : 2 * channels].astype(BF16)
        value_t = projected_t[2 * channels :].astype(BF16)
        query = (projected[:, :channels] * factor).astype(BF16)
        gate = sigmoid(projected[:, channels:])
        mask = head_mask[...]
        ones = mask * live_wide
        keys = jnp.concatenate([key_t] * heads, axis=1) * mask
        values = jnp.concatenate(
            [jnp.concatenate([value_t] * heads, axis=1) * ones, ones], axis=0
        )
        score = mm(query, keys)
        yield
        expo = jnp.exp(score + bias[...])
        expo_b = expo.astype(BF16)
        sums = mmt(expo_b, values)
        yield
        total = sums[:, channels:]
        inverse = 1.0 / jnp.maximum(total, 1.0)
        attended = sums[:, :channels] * inverse
        gated = (gate * attended).astype(BF16)
        d_attended = d_gated * gate * inverse
        d_gate = d_gated * attended * gate * (1.0 - gate)
        slope = jnp.where(total > 1.0, 1.0, jnp.where(total == 1.0, 0.5, 0.0))
        d_attended_b = d_attended.astype(BF16)
        both = jnp.concatenate(
            [d_attended_b, (-d_attended * attended * slope).astype(BF16)], axis=1
        )
        d_expo = mm(both, values)
        turned = mmt(
            eye, jnp.concatenate([d_attended_b, d_gate.astype(BF16), gated], axis=0)
        ).astype(BF16)
        yield
        update = mm(gated, output_w[...])
        d_score = expo * d_expo
        d_score_b = d_score.astype(BF16)
        d_query_t = mmt(keys, d_score_b) * factor
        d_key_t = mm(query_t, d_score_b)
        d_value_t = mm(turned[:, :length], expo_b)
        yield
        pair_out[i] = (middle[i].astype(F32) + update).astype(BF16)

        def diagonal(full):
            return jnp.concatenate(
                [full[h * size : (h + 1) * size, spans(h)] for h in range(heads)], axis=0
            )

        d_projected[i, :channels] = d_query_t.astype(BF16)
        d_projected[i, channels : 2 * channels] = diagonal(d_key_t).astype(BF16)
        d_projected[i, 2 * channels : 3 * channels] = (diagonal(d_value_t) * live_row).astype(BF16)
        d_projected[i, 3 * channels :] = turned[:, length : 2 * length]
        return turned[:, 2 * length :], cotangent[i], d_score

    def finish(results):
        gated_t, cots, d_scores = zip(*results)
        d_output[...] += mm(jnp.concatenate(gated_t, axis=1), jnp.concatenate(cots, axis=0))
        d_bias[...] += sum(d_scores)

    over_rows(block, 2, row, finish)

    @pl.when(step == pl.num_programs(0) - 1)
    def _():
        for offset in range(count):
            start = pl.multiple_of((place ^ offset) * own, own)
            ref = d_bias_outs[offset]
            ref[...] = d_bias[pl.ds(start, own), :].astype(ref.dtype)
        high = d_bias[...].astype(BF16)
        low = (d_bias[...] - high.astype(F32)).astype(BF16)
        kinds = lax.broadcasted_iota(jnp.int32, (HEAD_ROWS, length), 0)
        picks = (types_row[...] == kinds).astype(F32).astype(BF16)
        by_row = mm(picks, high) + mm(picks, low)
        lanes = lax.broadcasted_iota(jnp.int32, (HEAD_ROWS, channels), 1)
        grad = jnp.zeros((HEAD_ROWS, channels), F32)
        for h in range(heads):
            part = by_row[:, spans(h)]
            for b in range(types):
                one = jnp.sum(jnp.where(types_row[...] == b, part, 0.0), axis=1, keepdims=True)
                grad = jnp.where(lanes == h * types + b, one, grad)
        d_table[...] = grad


def projection_kernel(d_projected, normed3, input_w, d_output, d_table, d_normed, packed, total):
    block = normed3.shape[0]
    wide, length = d_projected.shape[1:]
    channels = normed3.shape[2]
    step = pl.program_id(0)

    @pl.when(step == 0)
    def _():
        total[...] = jnp.zeros_like(total)

    def rows(index, carry):
        at = [4 * index + one for one in range(4)]
        both = jnp.concatenate([d_projected[one] for one in at], axis=1)
        total[...] += mm(both, jnp.concatenate([normed3[one] for one in at], axis=0))
        d_both = mm(input_w[...], both)
        for order, one in enumerate(at):
            d_normed[one] = d_both[:, order * length : (order + 1) * length]
        return carry

    lax.fori_loop(0, block // 4, rows, 0, unroll=2)

    @pl.when(step == pl.num_programs(0) - 1)
    def _():
        packed[:wide] = total[...].astype(BF16)
        packed[wide : wide + channels] = d_output[...].astype(BF16)
        high = d_table[...].astype(BF16)
        packed[wide + channels : wide + channels + HEAD_ROWS] = high
        packed[wide + channels + HEAD_ROWS :] = (d_table[...] - high.astype(F32)).astype(BF16)


def middle_kernel(count, place_ref, *refs):
    arrived = refs[:count]
    (d_normed3, normed3, middle, cotangent, gain3_col, bias_w) = refs[count : count + 6]
    (normed2, scale2, update, gate, gain2_col, output_w) = refs[count + 6 : count + 12]
    (d_middle_out, d_gate_out, d_product_out, grad_out) = refs[count + 12 : count + 16]
    send_outs = refs[count + 16 : 2 * count + 16]
    d_bias, lay = refs[2 * count + 16 :]
    rows, length, channels = middle.shape
    heads = bias_w.shape[1]
    place = place_ref[0]
    eye = identity(channels)
    total = arrived[0][...]
    for ref in arrived[1:]:
        total = total + ref[...].astype(F32)
    d_bias[...] = jnp.zeros_like(d_bias)
    for h in range(heads):
        d_bias[pl.ds(h, rows, stride=HEAD_ROWS), :] = total[:, h * length : (h + 1) * length]
    bias_wide = jnp.concatenate(
        [bias_w[...].astype(F32), jnp.zeros((channels, HEAD_ROWS - heads), F32)], axis=1
    ).astype(BF16)
    gain3 = jnp.broadcast_to(gain3_col[...], (channels, length))
    gain2 = jnp.broadcast_to(gain2_col[...], (channels, length))
    inverse2 = 1.0 / gain2
    grad_out[...] = jnp.zeros_like(grad_out)

    def row(i):
        bias_rows = d_bias[pl.ds(i * HEAD_ROWS, HEAD_ROWS), :].astype(BF16)
        d_normed = d_normed3[i] + mm(bias_wide, bias_rows)
        hat3, scale3 = norm_parts(mmt(eye, middle[i]), 0)
        yield
        d_mid_t = norm_back(d_normed * gain3, hat3, scale3, 0).astype(BF16)
        d_mid_b = mmt(eye, d_mid_t)
        yield
        d_mid = (cotangent[i].astype(F32) + d_mid_b).astype(BF16)
        d_middle_out[i] = d_mid
        gates = gate[i].astype(F32)
        d_mid = d_mid.astype(F32)
        d_up = d_mid * gates
        d_gate_out[i] = (d_up * update[i].astype(F32) * (1.0 - gates)).astype(BF16)
        d_up = d_up.astype(BF16)
        normed2_t = normed2[i]
        d_hat2 = mmt(output_w[...], d_up)
        yield
        hat2 = normed2_t.astype(F32) * inverse2
        lay[pl.ds(i, channels, stride=rows), :] = norm_back(
            d_hat2 * gain2, hat2, scale2[pl.ds(i, 1), :], 0
        )
        return normed2_t, d_up, bias_rows, normed3[i]

    def finish(results):
        normed2_t, d_up, bias_rows, normed = zip(*results)
        grad_out[:channels] += mm(
            jnp.concatenate(normed2_t, axis=1), jnp.concatenate(d_up, axis=0)
        )
        grad_out[channels:] += mm(
            jnp.concatenate(bias_rows, axis=1), jnp.concatenate(normed, axis=0)
        )

    over_rows(rows, 4, row, finish)
    line = lax.broadcasted_iota(jnp.int32, (length, length), 0)
    source = ((line // rows) ^ place) * rows + line % rows
    shuffled = (
        (source == lax.broadcasted_iota(jnp.int32, (length, length), 1)).astype(F32).astype(BF16)
    )

    def group(g, carry):
        block = lay[pl.ds(g * length, length), :].astype(BF16)
        d_product_out[pl.ds(g * length, length), :] = block
        turned = mmt(shuffled, block).astype(BF16)
        for offset in range(count):
            send_outs[offset][g] = turned[offset * rows : (offset + 1) * rows]
        return carry

    lax.fori_loop(0, channels * rows // length, group, 0, unroll=4)


def gate_back(projected, d_out, live_row, channels):
    value, pre = projected[:channels], projected[channels:]
    gate = sigmoid(pre)
    d_value = d_out * live_row * gate
    d_pre = d_value * value * (1.0 - gate)
    return jnp.concatenate([d_value.astype(BF16), d_pre.astype(BF16)], axis=0)


def left_back_kernel(
    right_all, d_product, normed1, live, input_w, d_gate, grad_middle, d_projected_out, packed, lay, grad
):
    rows, length, channels = normed1.shape

    def channel(c, carry):
        lay[pl.ds(c, rows, stride=channels), :] = mm(
            d_product[pl.ds(c * rows, rows), :], right_all[c]
        )
        return carry

    lax.fori_loop(0, channels, channel, 0, unroll=8)
    eye = identity(channels)
    weight_t = input_w[:, : 2 * channels].astype(F32).T.astype(BF16)
    grad[...] = jnp.zeros_like(grad)

    def row(i):
        normed = normed1[i]
        projected = mmt(weight_t, normed)
        d_gate_t = mmt(eye, d_gate[i]).astype(BF16)
        yield
        d_projected = gate_back(
            projected, lay[pl.ds(i * channels, channels), :], live[pl.ds(i, 1), :], channels
        )
        d_projected = jnp.concatenate([d_projected, d_gate_t], axis=0)
        d_projected_out[i] = d_projected
        return d_projected, normed

    def finish(results):
        d_projected, normed = zip(*results)
        grad[...] += mm(jnp.concatenate(d_projected, axis=1), jnp.concatenate(normed, axis=0))

    over_rows(rows, 4, row, finish)
    packed[: 3 * channels] = grad[...].astype(BF16)
    packed[3 * channels :] = grad_middle[...].astype(BF16)


def right_back_kernel(count, place_ref, *refs):
    arrived = refs[:count]
    left_blocks = refs[count : 2 * count]
    normed1, live, input_w, packed_a, packed_b = refs[2 * count : 2 * count + 5]
    d_projected_out = refs[2 * count + 5]
    sends = refs[2 * count + 6 : 3 * count + 6]
    lay, grad, packed = refs[3 * count + 6 :]
    rows, length, channels = normed1.shape
    per = length // rows
    same = (
        lax.broadcasted_iota(jnp.int32, (length, length), 0) // rows
        == lax.broadcasted_iota(jnp.int32, (length, length), 1) // rows
    )
    mask = same.astype(F32).astype(BF16)

    def group(g, carry):
        spread = jnp.concatenate(
            [jnp.concatenate([ref[g]] * per, axis=0) * mask for ref in arrived], axis=1
        )
        lefts = jnp.concatenate(
            [ref[pl.ds(g * per, per)].reshape(length, length) for ref in left_blocks], axis=0
        )
        lay[pl.ds(g * length, length), :] = mm(spread, lefts)
        return carry

    lax.fori_loop(0, channels // per, group, 0, unroll=4)
    weight_t = input_w[:, 2 * channels : 4 * channels].astype(F32).T.astype(BF16)
    grad[...] = jnp.zeros_like(grad)

    def row(i):
        normed = normed1[i]
        projected = mmt(weight_t, normed)
        yield
        d_projected = gate_back(
            projected,
            lay[pl.ds(i, channels, stride=rows), :],
            live[pl.ds(i, 1), :],
            channels,
        )
        d_projected_out[i] = d_projected
        return d_projected, normed

    def finish(results):
        d_projected, normed = zip(*results)
        grad[...] += mm(jnp.concatenate(d_projected, axis=1), jnp.concatenate(normed, axis=0))

    over_rows(rows, 4, row, finish)
    first, second = packed_a.shape[0], packed_b.shape[0]
    packed[:first] = packed_a[...]
    packed[first : first + second] = packed_b[...]
    packed[first + second : first + second + 2 * channels] = grad[...].astype(BF16)
    packed[first + second + 2 * channels :] = jnp.zeros_like(
        packed[first + second + 2 * channels :]
    )
    size = sends[0].shape[0]
    for offset in range(count):
        start = pl.multiple_of((place_ref[0] ^ offset) * size, HEAD_ROWS)
        sends[offset][...] = packed[pl.ds(start, size), :]


def input_back_kernel(d_left, d_right, pair, d_middle, gain_col, input_w, gating, pair_grad):
    rows, length, channels = pair.shape
    eye = identity(channels)
    weight = jnp.concatenate(
        [input_w[:, : 2 * channels], gating[...], input_w[:, 2 * channels :]], axis=1
    )
    gain = jnp.broadcast_to(gain_col[...], (channels, length))

    def row(i):
        hat, scale = norm_parts(mmt(eye, pair[i]), 0)
        d_normed = mm(weight, jnp.concatenate([d_left[i], d_right[i]], axis=0))
        yield
        d_pair = mmt(eye, norm_back(d_normed * gain, hat, scale, 0).astype(BF16))
        yield
        pair_grad[i] = (d_middle[i].astype(F32) + d_pair).astype(BF16)

    over_rows(rows, 4, row)


def finish_kernel(count, factor, place_ref, *refs):
    blocks = refs[:count]
    (input1, gating, output1, bias_w, input3, gain1, gain2, gain3) = refs[count : count + 8]
    (
        gain1_out,
        input1_out,
        gating_out,
        gain2_out,
        output1_out,
        gain3_out,
        bias_out,
        input3_out,
        output3_out,
        table_out,
        packed,
    ) = refs[count + 8 :]
    channels = gating.shape[0]
    heads, types = table_out.shape[:2]
    size = blocks[0].shape[0]
    for offset in range(count):
        start = pl.multiple_of((place_ref[0] ^ offset) * size, HEAD_ROWS)
        packed[pl.ds(start, size), :] = blocks[offset][...].astype(F32) * factor
    at = 0

    def take(rows):
        nonlocal at
        at += rows
        return packed[at - rows : at, :]

    input3_t, output3 = take(4 * channels), take(channels)
    table = take(HEAD_ROWS) + take(HEAD_ROWS)
    left_t, gating_t, output1_grad = take(2 * channels), take(channels), take(channels)
    bias_t, right_t = take(HEAD_ROWS), take(2 * channels)
    input1_t = jnp.concatenate([left_t, right_t], axis=0)

    def dots(weight, grad_t):
        return jnp.sum(weight[...].astype(F32).T * grad_t, axis=0, keepdims=True)

    gain1_out[...] = (dots(input1, input1_t) + dots(gating, gating_t)) / gain1[...]
    output_t = (output1[...].astype(F32) * output1_grad).T
    gain2_out[...] = jnp.sum(output_t, axis=0, keepdims=True) / gain2[...]
    gain3_out[...] = (dots(input3, input3_t) + dots(bias_w, bias_t[:heads])) / gain3[...]
    input1_out[...] = input1_t.T
    gating_out[...] = gating_t.T
    output1_out[...] = output1_grad
    bias_out[...] = bias_t.T[:, :heads]
    input3_out[...] = input3_t.T
    output3_out[...] = output3
    for h in range(heads):
        table_out[h] = table[:types, h * types : (h + 1) * types]


def swap(value, axis, step):
    count = lax.axis_size(axis)
    return lax.ppermute(value, axis, [(index, index ^ step) for index in range(count)])


def gather_blocks(block, axis):
    return gather_near(block, swap(block, axis, lax.axis_size(axis) // 2), axis)


def gather_near(block, far, axis):
    half = lax.axis_size(axis) // 2
    blocks = {0: block, half: far}
    for bit in reversed(range(half.bit_length() - 1)):
        step = 1 << bit
        for offset, held in list(blocks.items()):
            blocks[offset ^ step] = swap(held, axis, step)
    return [blocks[offset] for offset in range(len(blocks))]


def sum_over(value, axis):
    step = 1
    while step < lax.axis_size(axis):
        value = value + swap(value, axis, step)
        step *= 2
    return value


def per_device(
    pair_rep,
    cotangent,
    tok_mask,
    tok_types,
    pair_mask,
    triangle_gain,
    triangle_input,
    triangle_gating,
    product_gain,
    triangle_output,
    attend_gain,
    attend_bias,
    attend_input,
    attend_output,
    type_table,
):
    slab = pair_rep[0]
    cot = cotangent[0]
    rows, length, channels = slab.shape
    heads, types = type_table.shape[:2]
    count = lax.axis_size("dap")
    place = lax.axis_index("dap")
    place_arg = place.reshape(1).astype(jnp.int32)
    tokens = tok_mask[0].astype(F32)
    row_tokens = lax.dynamic_slice_in_dim(tokens, place * rows, rows)
    live = pair_mask[0].astype(F32) * row_tokens[:, None] * tokens[None, :]
    gain1_row, gain3_row = triangle_gain[None, :], attend_gain[None, :]
    gain1_col, gain2_col, gain3_col = (
        triangle_gain[:, None],
        product_gain[:, None],
        attend_gain[:, None],
    )
    vmem = pl.BlockSpec(memory_space=pltpu.VMEM)
    anywhere = pl.BlockSpec(memory_space=pl.ANY)
    smem = pl.BlockSpec(memory_space=pltpu.SMEM)
    cells = (rows, length, channels)
    turned = (rows, channels, length)

    half = rows // 2
    normed1_halves, right_halves = [], []
    for part in range(2):
        normed_part, right_part = call(
            right_kernel,
            [((half, length, channels), BF16), ((channels, half, length), BF16)],
            [slab, live, gain1_row, triangle_input],
            grid=(1,),
            in_specs=[
                pl.BlockSpec((half, length, channels), lambda step, part=part: (part, 0, 0)),
                pl.BlockSpec((half, length), lambda step, part=part: (part, 0)),
                vmem,
                vmem,
            ],
            scratch=[
                pltpu.VMEM((2 * channels, channels), BF16),
                pltpu.VMEM((channels * half, length), F32),
            ],
            us=3.0,
            name="right_projection",
        )
        normed1_halves.append(normed_part)
        right_halves.append(right_part)
    normed1, left, gate = call(
        partial(left_kernel, 2),
        [(cells, BF16), ((channels, rows, length), BF16), (cells, BF16)],
        [*normed1_halves, live, triangle_input, triangle_gating],
        scratch=[
            pltpu.VMEM((2 * channels, channels), BF16),
            pltpu.VMEM((channels * rows, length), F32),
        ],
        us=5.0,
        name="left_projection",
    )
    far = [swap(part, "dap", count // 2) for part in right_halves]
    left, *far = lax.optimization_barrier((left, *far))
    right_halves = [
        gather_near(part, other, "dap") for part, other in zip(right_halves, far)
    ]
    right_blocks = [right_halves[index % 2][index // 2] for index in range(2 * count)]
    right_all, normed2, scale2, update, middle, normed3, bias_rows = call(
        partial(product_kernel, count),
        [
            ((channels, length, length), BF16),
            (turned, BF16),
            ((rows, length), F32),
            (cells, BF16),
            (cells, BF16),
            (cells, BF16),
            ((rows, heads * length), BF16),
        ],
        [place_arg, *right_blocks, left, slab, gate, gain2_col, gain3_row]
        + [triangle_output, attend_bias],
        in_specs=[smem] + [vmem] * (2 * count + 7),
        scratch=[
            pltpu.VMEM((rows * channels, length), F32),
            pltpu.VMEM((rows * HEAD_ROWS, length), F32),
        ],
        us=14.0,
        name="product_and_norms",
    )
    bias_blocks = gather_blocks(bias_rows, "dap")
    left, bias_blocks[-1] = lax.optimization_barrier((left, bias_blocks[-1]))
    left_blocks = gather_blocks(left, "dap")

    block = 8
    steps = rows // block
    by_row = pl.BlockSpec((block, length, channels), lambda step: (step, 0, 0))
    by_row_wide = pl.BlockSpec((block, 4 * channels, length), lambda step: (step, 0, 0))

    def fixed(*shape):
        return pl.BlockSpec(shape, lambda step: (0,) * len(shape))

    attend_outs = call(
        partial(attend_kernel, count, block),
        [
            (cells, BF16),
            ((rows, 4 * channels, length), BF16),
            ((channels, channels), F32),
            ((HEAD_ROWS, channels), F32),
            ((rows, heads * length), F32),
        ]
        + [((rows, heads * length), BF16)] * (count - 1),
        [place_arg, type_table.reshape(heads * types, types), *bias_blocks]
        + [tok_types, tok_types.reshape(length, 1), live, normed3, middle, cot]
        + [attend_input, attend_output],
        grid=(steps,),
        in_specs=[smem, smem]
        + [fixed(rows, heads * length)] * count
        + [fixed(1, length), fixed(length, 1), fixed(rows, length), by_row, by_row, by_row]
        + [fixed(channels, 4 * channels), fixed(channels, channels)],
        out_specs=[by_row, by_row_wide, fixed(channels, channels), fixed(HEAD_ROWS, channels)]
        + [fixed(rows, heads * length)] * count,
        scratch=[
            pltpu.VMEM((length, heads * length), F32),
            pltpu.VMEM((length, heads * length), F32),
            pltpu.VMEM((channels, heads * length), BF16),
            pltpu.VMEM((3 * channels, channels), BF16),
            pltpu.VMEM((channels, 2 * channels), BF16),
        ],
        us=30.0,
        name="attention",
    )
    pair_out, d_projected3, d_output, d_table = attend_outs[:4]
    d_bias_parts = [attend_outs[4]] + [
        swap(attend_outs[4 + offset], "dap", offset) for offset in range(1, count)
    ]
    d_normed3, packed_a = call(
        projection_kernel,
        [(turned, F32), ((4 * channels + channels + 2 * HEAD_ROWS, channels), BF16)],
        [d_projected3, normed3, attend_input, d_output, d_table],
        grid=(steps,),
        in_specs=[by_row_wide, by_row, fixed(channels, 4 * channels)]
        + [fixed(channels, channels), fixed(HEAD_ROWS, channels)],
        out_specs=[
            pl.BlockSpec((block, channels, length), lambda step: (step, 0, 0)),
            fixed(5 * channels + 2 * HEAD_ROWS, channels),
        ],
        scratch=[pltpu.VMEM((4 * channels, channels), F32)],
        us=6.0,
        name="projection_back",
    )
    groups = channels * rows // length
    middle_outs = call(
        partial(middle_kernel, count),
        [
            (cells, BF16),
            (cells, BF16),
            ((channels * rows, length), BF16),
            ((channels + HEAD_ROWS, channels), F32),
        ]
        + [((groups, rows, length), BF16)] * count,
        [place_arg, *d_bias_parts, d_normed3, normed3, middle, cot, gain3_col, attend_bias]
        + [normed2, scale2, update, gate, gain2_col, triangle_output],
        in_specs=[smem] + [vmem] * (count + 12),
        scratch=[
            pltpu.VMEM((rows * HEAD_ROWS, length), F32),
            pltpu.VMEM((channels * rows, length), F32),
        ],
        us=12.0,
        name="middle_back",
    )
    d_middle, d_gate, d_product, grad_middle = middle_outs[:4]
    product_parts = [middle_outs[4]] + [
        swap(middle_outs[4 + offset], "dap", offset) for offset in range(1, count)
    ]
    d_left, packed_b = call(
        left_back_kernel,
        [((rows, 3 * channels, length), BF16), ((4 * channels + HEAD_ROWS, channels), BF16)],
        [right_all, d_product, normed1, live, triangle_input, d_gate, grad_middle],
        scratch=[
            pltpu.VMEM((rows * channels, length), F32),
            pltpu.VMEM((3 * channels, channels), F32),
        ],
        us=10.0,
        name="left_back",
    )
    used = packed_a.shape[0] + packed_b.shape[0] + 2 * channels
    share = -(-used // (count * HEAD_ROWS)) * HEAD_ROWS
    right_outs = call(
        partial(right_back_kernel, count),
        [((rows, 2 * channels, length), BF16)] + [((share, channels), BF16)] * count,
        [place_arg, *product_parts, *left_blocks, normed1, live, triangle_input]
        + [packed_a, packed_b],
        in_specs=[smem] + [vmem] * (2 * count + 5),
        scratch=[
            pltpu.VMEM((channels * rows, length), F32),
            pltpu.VMEM((2 * channels, channels), F32),
            pltpu.VMEM((share * count, channels), BF16),
        ],
        us=7.0,
        name="right_back",
    )
    d_right = right_outs[0]
    grad_share = right_outs[1].astype(F32)
    for offset in range(1, count):
        grad_share = grad_share + swap(right_outs[1 + offset], "dap", offset).astype(F32)
    grad_share = sum_over(grad_share.astype(BF16), "dp")
    grad_blocks = [grad_share] + [
        swap(grad_share, "dap", offset) for offset in range(1, count)
    ]
    (pair_grad,) = call(
        input_back_kernel,
        [(cells, BF16)],
        [d_left, d_right, slab, d_middle, gain1_col, triangle_input, triangle_gating],
        us=6.0,
        name="input_back",
    )
    weights = (triangle_input, triangle_gating, triangle_output, attend_bias, attend_input)
    gains = (gain1_row, product_gain[None, :], gain3_row)
    grads = call(
        partial(finish_kernel, count, (length * length * lax.axis_size("dp")) ** (-0.5)),
        [
            ((1, channels), F32),
            (triangle_input.shape, F32),
            (triangle_gating.shape, F32),
            ((1, channels), F32),
            (triangle_output.shape, F32),
            ((1, channels), F32),
            (attend_bias.shape, F32),
            (attend_input.shape, F32),
            (attend_output.shape, F32),
            (type_table.shape, F32),
        ],
        [place_arg, *grad_blocks, *weights, *gains],
        in_specs=[smem] + [vmem] * (count + 8),
        scratch=[pltpu.VMEM((share * count, channels), F32)],
        us=3.0,
        name="scale_gradients",
    )
    grads = [grad[0] if grad.shape[0] == 1 else grad for grad in grads]
    return (pair_out[None], pair_grad[None], *grads)


def solution(mesh):
    return jax.shard_map(
        per_device,
        mesh=mesh,
        in_specs=(
            P("dp", "dap", None, None),
            P("dp", "dap", None, None),
            P("dp", None),
            P("dp", None),
            P("dp", "dap", None),
        )
        + (P(),) * 10,
        out_specs=(
            P("dp", "dap", None, None),
            P("dp", "dap", None, None),
        )
        + (P(),) * 10,
        check_vma=False,
    )
```

```python
import math
from functools import partial

import jax
import jax.numpy as jnp
from jax import lax
from jax.experimental import pallas as pl
from jax.experimental.pallas import tpu as pltpu
from jax.sharding import PartitionSpec as P

EPSILON = 1e-05
F32 = jnp.float32
BF16 = jnp.bfloat16
VMEM_MARGIN = 4 * 1024 * 1024
W_PRODUCT, W_ATTEND, W_MIDDLE = 8, 4, 8
HEAD_ROWS = 16


def mm(left, right):
    return lax.dot_general(left, right, (((1,), (0,)), ((), ())), preferred_element_type=F32)


def mmt(left, right):
    return lax.dot_general(left, right, (((1,), (1,)), ((), ())), preferred_element_type=F32)


def sigmoid(value):
    return 1.0 / (1.0 + jnp.exp(-value))


def identity(size):
    rows = lax.broadcasted_iota(jnp.int32, (size, size), 0)
    columns = lax.broadcasted_iota(jnp.int32, (size, size), 1)
    return (rows == columns).astype(F32).astype(BF16)


def norm_parts(values, axis):
    centred = values - jnp.mean(values, axis=axis, keepdims=True)
    spread = jnp.mean(centred * centred, axis=axis, keepdims=True)
    scale = lax.rsqrt(spread + EPSILON)
    return centred * scale, scale


def norm_back(d_hat, hat, scale, axis):
    first = jnp.mean(d_hat, axis=axis, keepdims=True)
    second = jnp.mean(d_hat * hat, axis=axis, keepdims=True)
    return scale * (d_hat - first - hat * second)


def lockstep(row, indices):
    going = [row(index) for index in indices]
    results = [None] * len(going)
    running = True
    while running:
        for at, one in enumerate(going):
            try:
                next(one)
            except StopIteration as stop:
                results[at] = stop.value
                running = False
    return results


def over_rows(count, width, row, finish=None, first=0):
    def some(index, carry):
        results = lockstep(row, [first + index * width + at for at in range(width)])
        if finish is not None:
            finish(results)
        return carry

    lax.fori_loop(0, count // width, some, 0)


def split_copies(source, target, sems, parts):
    size = source.shape[0] // parts
    return [
        pltpu.make_async_copy(
            source.at[pl.ds(part * size, size)], target.at[pl.ds(part * size, size)], sems.at[part]
        )
        for part in range(parts)
    ]


def start(copies):
    for copy in copies:
        copy.start()


def wait(copies):
    for copy in copies:
        copy.wait()


def call(kernel, outs, args, scratch=(), grid=(), in_specs=None, out_specs=None, us=5.0, name=None, aliases=None):
    whole = pl.BlockSpec(memory_space=pltpu.VMEM)
    in_specs = in_specs or [whole] * len(args)
    out_specs = out_specs or [whole] * len(outs)
    held = sum(
        math.prod(one.shape) * jnp.dtype(one.dtype).itemsize
        for one in scratch
        if getattr(one, "memory_space", None) == pltpu.VMEM
    )
    args = [
        pltpu.with_memory_space_constraint(arg, pltpu.HBM)
        if spec.memory_space == pltpu.HBM
        else arg
        for arg, spec in zip(args, in_specs)
    ]
    return pl.pallas_call(
        kernel,
        out_shape=[
            pltpu.HBM(shape, dtype)
            if spec.memory_space == pltpu.HBM
            else jax.ShapeDtypeStruct(shape, dtype)
            for (shape, dtype), spec in zip(outs, out_specs)
        ],
        grid=grid,
        in_specs=in_specs,
        out_specs=out_specs,
        scratch_shapes=list(scratch),
        compiler_params=pltpu.CompilerParams(vmem_limit_bytes=held + VMEM_MARGIN),
        cost_estimate=pl.CostEstimate(
            flops=int(us * 1.0e9), bytes_accessed=int(us * 3.0e6), transcendentals=0
        ),
        input_output_aliases=aliases or {},
        name=name,
    )(*args)


def right_kernel(
    part, pair_any, mask_any, tokens_any, gain_any, weight_any, normed_out, right_out, live_out, *scratch
):
    pair, mask, tokens, gain, weight, weight_t, lay, sems = scratch
    rows, length, channels = pair.shape
    place = lax.axis_index("dap")
    span = pl.ds(part * rows, rows)
    sources = [mask_any.at[span], tokens_any, gain_any, weight_any, pair_any.at[span]]
    copies = [
        pltpu.make_async_copy(source, target, sems.at[at])
        for at, (source, target) in enumerate(zip(sources, (mask, tokens, gain, weight, pair)))
    ]
    start(copies)
    wait(copies)
    first = place * (mask_any.shape[0]) + part * rows
    lines = lax.broadcasted_iota(jnp.int32, (rows, length), 0) + first
    lanes = lax.broadcasted_iota(jnp.int32, (rows, length), 1)
    wide = tokens[...].astype(F32)
    own = jnp.sum(jnp.where(lines == lanes, wide, 0.0), axis=1, keepdims=True)
    live_out[...] = mask[...].astype(F32) * own * wide
    weight_t[...] = weight[:, 2 * channels : 4 * channels].astype(F32).T.astype(BF16)

    def row(i):
        hat, _ = norm_parts(pair[i].astype(F32), -1)
        yield
        normed = (hat * gain[...]).astype(BF16)
        normed_out[i] = normed
        projected = mmt(weight_t[...], normed)
        yield
        right = sigmoid(projected[channels:]) * projected[:channels] * live_out[pl.ds(i, 1), :]
        lay[pl.ds(i, channels, stride=rows), :] = right

    over_rows(rows, 8, row)
    right_out[...] = lay[...].reshape(channels, rows, length).astype(BF16)


def gate_factors(projected, live_row, channels):
    value, pre = projected[:channels], projected[channels:]
    gate = sigmoid(pre)
    slope = gate * live_row
    out = slope * value
    factors = jnp.concatenate([slope.astype(BF16), (out * (1.0 - gate)).astype(BF16)], axis=0)
    return out, factors


def left_kernel(parts, *refs):
    normed_parts = refs[:parts]
    live_parts = refs[parts : 2 * parts]
    weight, gating = refs[2 * parts : 2 * parts + 2]
    normed_any, low_out, high_out, gate_any, live, factor_any = refs[2 * parts + 2 : 2 * parts + 8]
    weight_t, lay, gates, factors, sems = refs[2 * parts + 8 :]
    rows, length, channels = gates.shape
    half = rows // parts
    weight_t[...] = weight[:, : 2 * channels].astype(F32).T.astype(BF16)
    outs = []
    for part in range(parts):
        span = pl.ds(part * half, half)
        copy = pltpu.make_async_copy(normed_parts[part], normed_any.at[span], sems.at[0, part])
        copy.start()
        outs.append(copy)
        live[span, :] = live_parts[part][...]

        def row(i, part=part):
            normed = normed_parts[part][i]
            at = i + part * half
            projected = mmt(weight_t[...], normed)
            gate = mm(normed, gating[...])
            yield
            left, factors[at] = gate_factors(projected, live[pl.ds(at, 1), :], channels)
            lay[pl.ds(at, channels, stride=rows), :] = left
            gates[at] = sigmoid(gate)

        over_rows(half, 8, row)
        for index, (source, target) in enumerate(((gates, gate_any), (factors, factor_any))):
            copy = pltpu.make_async_copy(
                source.at[span], target.at[span], sems.at[1 + index, part]
            )
            copy.start()
            outs.append(copy)
    left = lay[...].reshape(channels, rows, length).astype(BF16)
    low_out[...] = left[: channels // 2]
    high_out[...] = left[channels // 2 :]
    wait(outs)


def factor_kernel(parts, *refs):
    normed_parts = refs[:parts]
    live, weight, output_w, cotangent_any, factor_any, d_gated_any = refs[parts : parts + 6]
    cotangent, factors, d_gated, in_sem, sems = refs[parts + 6 :]
    rows, length, channels = cotangent.shape
    half = rows // parts
    arrivals = split_copies(cotangent_any, cotangent, in_sem, parts)
    start(arrivals)
    weight_t = weight[:, 2 * channels : 4 * channels].astype(F32).T.astype(BF16)
    departures = [
        split_copies(factors, factor_any, sems.at[0], parts),
        split_copies(d_gated, d_gated_any, sems.at[1], parts),
    ]
    for part in range(parts):
        arrivals[part].wait()

        def row(i, part=part):
            at = i + part * half
            projected = mmt(weight_t, normed_parts[part][i])
            back = mmt(cotangent[at], output_w[...])
            yield
            _, factors[at] = gate_factors(projected, live[pl.ds(at, 1), :], channels)
            d_gated[at] = back.astype(BF16)

        over_rows(half, 8, row)
        start([copies[part] for copies in departures])
    for copies in departures:
        wait(copies)


def product_kernel(count, *refs):
    blocks = refs[: 2 * count]
    lefts = refs[2 * count : 2 * count + 2]
    (pair_any, gate_any, gain2_col, gain3, output_w, bias_w) = refs[2 * count + 2 : 2 * count + 8]
    row_outs = refs[2 * count + 8 : 2 * count + 12]
    right_any, scale2_out, bias_out = refs[2 * count + 12 : 2 * count + 15]
    product, bias_scr, right_all, pair, gate = refs[2 * count + 15 : 2 * count + 20]
    kept = refs[2 * count + 20 : 2 * count + 24]
    normed2_out, update_out, middle_out, normed3_out = kept
    in_sems, out_sems, right_sem = refs[2 * count + 24 :]
    rows, length, channels = pair.shape
    heads = bias_w.shape[1]
    half = rows // 2
    place = lax.axis_index("dap")
    arrivals = [
        pltpu.make_async_copy(pair_any, pair, in_sems.at[0]),
        pltpu.make_async_copy(gate_any, gate, in_sems.at[1]),
    ]
    start(arrivals)
    starts = [
        pl.multiple_of((place ^ (index // 2)) * rows + (index % 2) * half, half)
        for index in range(2 * count)
    ]

    def channel(c, carry):
        for begin, ref in zip(starts, blocks):
            right_all[c, pl.ds(begin, half), :] = ref[c]
        return carry

    lax.fori_loop(0, channels, channel, 0, unroll=4)
    right_copy = pltpu.make_async_copy(right_all, right_any, right_sem)
    right_copy.start()

    for part, left in enumerate(lefts):

        def multiply(c, carry, left=left, first=part * (channels // 2)):
            product[pl.ds(first + c, rows, stride=channels), :] = mmt(
                left[c], right_all[first + c]
            )
            return carry

        lax.fori_loop(0, channels // 2, multiply, 0, unroll=8)
    eye = identity(channels)
    gain2 = jnp.broadcast_to(gain2_col[...], (channels, length))
    bias_t = jnp.concatenate(
        [bias_w[...].astype(F32).T, jnp.zeros((HEAD_ROWS - heads, channels), F32)], axis=0
    ).astype(BF16)

    def row(i):
        hat, scale = norm_parts(product[pl.ds(i * channels, channels), :], 0)
        yield
        normed2_t = (hat * gain2).astype(BF16)
        normed2_out[i] = normed2_t
        scale2_out[pl.ds(i, 1), :] = scale
        normed2 = mmt(eye, normed2_t).astype(BF16)
        yield
        update = mm(normed2, output_w[...])
        yield
        update_out[i] = update.astype(BF16)
        middle = (pair[i].astype(F32) + gate[i] * update).astype(BF16)
        middle_out[i] = middle
        hat3, _ = norm_parts(middle.astype(F32), -1)
        yield
        normed3 = (hat3 * gain3[...]).astype(BF16)
        normed3_out[i] = normed3
        bias_scr[pl.ds(i * HEAD_ROWS, HEAD_ROWS), :] = mmt(bias_t, normed3)

    wait(arrivals)
    parts = 4
    departures = [
        split_copies(source, target, out_sems.at[at], parts)
        for at, (source, target) in enumerate(zip(kept, row_outs))
    ]
    for part in range(parts):
        over_rows(rows // parts, W_PRODUCT, row, first=part * (rows // parts))
        start([copies[part] for copies in departures])
    for h in range(heads):
        head = bias_scr[pl.ds(h, rows, stride=HEAD_ROWS), :]
        bias_out[:, h * length : (h + 1) * length] = head.astype(BF16)
    for copies in departures:
        wait(copies)
    right_copy.wait()


def project_kernel(factor, normed3_any, weight_any, projected_any, query_any, gate_any, *scratch):
    normed3, weight, weight_t, weight_qg, projected3, queries, gates, sems, out_sems, weight_sem = (
        scratch
    )
    rows, length, channels = normed3.shape
    kept = projected3.shape[1]
    parts = 4
    copy = pltpu.make_async_copy(weight_any, weight, weight_sem)
    copy.start()
    arrivals = split_copies(normed3_any, normed3, sems, parts)
    start(arrivals)
    copy.wait()
    weight_t[...] = weight[:, :kept].astype(F32).T.astype(BF16)
    weight_qg[:, :channels] = weight[:, :channels]
    weight_qg[:, channels:] = weight[:, kept:]

    def row(i):
        normed = normed3[i]
        projected_t = mmt(weight_t[...], normed)
        projected = mm(normed, weight_qg[...])
        yield
        projected3[i, :channels] = (projected_t[:channels] * factor).astype(BF16)
        projected3[i, channels:] = projected_t[channels:].astype(BF16)
        queries[i] = (projected[:, :channels] * factor).astype(BF16)
        gates[i] = sigmoid(projected[:, channels:])

    departures = [
        split_copies(source, target, out_sems.at[at], parts)
        for at, (source, target) in enumerate(
            ((projected3, projected_any), (queries, query_any), (gates, gate_any))
        )
    ]
    for part in range(parts):
        arrivals[part].wait()
        over_rows(rows // parts, 8, row, first=part * (rows // parts))
        start([copies[part] for copies in departures])
    for copies in departures:
        wait(copies)


def attend_kernel(count, table, *refs):
    bias_refs = refs[:count]
    types_row, types_col, live, output_w = refs[count : count + 4]
    row_arrays = refs[count + 4 : count + 10]
    (pair_out_any, d_projected, d_output, d_table) = refs[count + 10 : count + 14]
    d_bias_outs = refs[count + 14 : 2 * count + 14]
    bias, d_bias, head_mask = refs[2 * count + 14 : 2 * count + 17]
    fetched = refs[2 * count + 17 : 2 * count + 23]
    projected, queries, gates, d_gateds, cotangent, middle = fetched
    pair_out, in_sems, out_sems = refs[2 * count + 23 :]
    rows, length, channels = middle.shape
    types = table.shape[1]
    heads = table.shape[0] // types
    size = channels // heads
    own = bias_refs[0].shape[0]
    factor = size ** -0.5
    place = lax.axis_index("dap")
    parts = rows // W_ATTEND
    arrivals = [
        split_copies(source, target, in_sems.at[at], parts)
        for at, (source, target) in enumerate(zip(row_arrays, fetched))
    ]
    for part in range(parts):
        start([copies[part] for copies in arrivals])

    def spans(h):
        return slice(h * length, (h + 1) * length)

    for offset in range(count):
        begin = pl.multiple_of((place ^ offset) * own, own)
        bias[pl.ds(begin, own), :] = bias_refs[offset][...].astype(F32)
    row_types = types_row[...]
    col_types = types_col[...]
    for h in range(heads):
        total = jnp.zeros((length, length), F32)
        for a in range(types):
            values = jnp.zeros((1, length), F32)
            for b in range(types):
                values = jnp.where(row_types == b, table[h * types + a, b], values)
            total = jnp.where(col_types == a, values, total)
        bias[:, spans(h)] = bias[:, spans(h)] + total
    d_bias[...] = jnp.zeros_like(d_bias)
    d_output[...] = jnp.zeros_like(d_output)
    lines = lax.broadcasted_iota(jnp.int32, head_mask.shape, 0) // size
    columns = lax.broadcasted_iota(jnp.int32, head_mask.shape, 1) // length
    head_mask[...] = (lines == columns).astype(F32).astype(BF16)

    eye = identity(channels)

    def row(i):
        live_row = live[pl.ds(i, 1), :]
        live_wide = jnp.concatenate([live_row.astype(BF16)] * heads, axis=1)
        query_t = projected[i, :channels]
        key_t = projected[i, channels : 2 * channels]
        value_t = projected[i, 2 * channels :]
        gate = gates[i]
        d_gated = d_gateds[i].astype(F32)
        mask = head_mask[...]
        ones = mask * live_wide
        keys = jnp.concatenate([key_t] * heads, axis=1) * mask
        values = jnp.concatenate(
            [jnp.concatenate([value_t] * heads, axis=1) * ones, ones], axis=0
        )
        score = mm(queries[i], keys)
        yield
        expo = jnp.exp(score + bias[...])
        expo_b = expo.astype(BF16)
        sums = mmt(expo_b, values)
        yield
        total = sums[:, channels:]
        inverse = 1.0 / jnp.maximum(total, 1.0)
        attended = sums[:, :channels] * inverse
        gated = (gate * attended).astype(BF16)
        d_attended = d_gated * gate * inverse
        d_gate = d_gated * attended * gate * (1.0 - gate)
        slope = jnp.where(total > 1.0, 1.0, jnp.where(total == 1.0, 0.5, 0.0))
        d_attended_b = d_attended.astype(BF16)
        both = jnp.concatenate(
            [d_attended_b, (-d_attended * attended * slope).astype(BF16)], axis=1
        )
        d_expo = mm(both, values)
        turned = mmt(
            eye, jnp.concatenate([d_attended_b, d_gate.astype(BF16), gated], axis=0)
        ).astype(BF16)
        yield
        update = mm(gated, output_w[...])
        d_score = expo * d_expo
        d_score_b = d_score.astype(BF16)
        d_query_t = mmt(keys, d_score_b) * factor
        d_key_t = mm(query_t, d_score_b)
        d_value_t = mm(turned[:, :length], expo_b)
        yield
        pair_out[i] = (middle[i].astype(F32) + update).astype(BF16)

        def diagonal(full):
            return jnp.concatenate(
                [full[h * size : (h + 1) * size, spans(h)] for h in range(heads)], axis=0
            )

        d_projected[i, :channels] = d_query_t.astype(BF16)
        d_projected[i, channels : 2 * channels] = diagonal(d_key_t).astype(BF16)
        d_projected[i, 2 * channels : 3 * channels] = (diagonal(d_value_t) * live_row).astype(BF16)
        d_projected[i, 3 * channels :] = turned[:, length : 2 * length]
        return turned[:, 2 * length :], cotangent[i], d_score

    def finish(results):
        gated_t, cots, d_scores = zip(*results)
        d_output[...] += mm(jnp.concatenate(gated_t, axis=1), jnp.concatenate(cots, axis=0))
        d_bias[...] += sum(d_scores)

    departures = split_copies(pair_out, pair_out_any, out_sems, parts)
    for part in range(parts):
        wait([copies[part] for copies in arrivals])
        over_rows(rows // parts, W_ATTEND, row, finish, first=part * (rows // parts))
        departures[part].start()

    for offset in range(count):
        begin = pl.multiple_of((place ^ offset) * own, own)
        ref = d_bias_outs[offset]
        ref[...] = d_bias[pl.ds(begin, own), :].astype(ref.dtype)
    high = d_bias[...].astype(BF16)
    low = (d_bias[...] - high.astype(F32)).astype(BF16)
    kinds = lax.broadcasted_iota(jnp.int32, (HEAD_ROWS, length), 0)
    picks = (types_row[...] == kinds).astype(F32).astype(BF16)
    by_row = mm(picks, high) + mm(picks, low)
    lanes = lax.broadcasted_iota(jnp.int32, (HEAD_ROWS, channels), 1)
    grad = jnp.zeros((HEAD_ROWS, channels), F32)
    for h in range(heads):
        part = by_row[:, spans(h)]
        for b in range(types):
            one = jnp.sum(jnp.where(types_row[...] == b, part, 0.0), axis=1, keepdims=True)
            grad = jnp.where(lanes == h * types + b, one, grad)
    d_table[...] = grad
    wait(departures)


def projection_kernel(d_projected, normed3, input_w, d_output, d_table, d_normed, packed, total):
    block = normed3.shape[0]
    wide, length = d_projected.shape[1:]
    channels = normed3.shape[2]
    step = pl.program_id(0)

    @pl.when(step == 0)
    def _():
        total[...] = jnp.zeros_like(total)

    def rows(index, carry):
        at = [4 * index + one for one in range(4)]
        both = jnp.concatenate([d_projected[one] for one in at], axis=1)
        total[...] += mm(both, jnp.concatenate([normed3[one] for one in at], axis=0))
        d_both = mm(input_w[...], both)
        for order, one in enumerate(at):
            d_normed[one] = d_both[:, order * length : (order + 1) * length]
        return carry

    lax.fori_loop(0, block // 4, rows, 0, unroll=2)

    @pl.when(step == pl.num_programs(0) - 1)
    def _():
        packed[:wide] = total[...].astype(BF16)
        packed[wide : wide + channels] = d_output[...].astype(BF16)
        high = d_table[...].astype(BF16)
        packed[wide + channels : wide + channels + HEAD_ROWS] = high
        packed[wide + channels + HEAD_ROWS :] = (d_table[...] - high.astype(F32)).astype(BF16)


def middle_kernel(count, *refs):
    arrived = refs[:count]
    (d_normed3, normed3, middle, cotangent, gain3_col, bias_w) = refs[count : count + 6]
    (normed2, scale2, update, gate, gain2_col, output_w) = refs[count + 6 : count + 12]
    (d_middle_any, d_gate_any, d_product_any, grad_out) = refs[count + 12 : count + 16]
    send_any = refs[count + 16 : 2 * count + 16]
    d_bias, lay, d_middle_out, d_gate_out, d_product_out = refs[2 * count + 16 : 2 * count + 21]
    send_outs = refs[2 * count + 21 : 3 * count + 21]
    row_sems, product_sems, send_sems = refs[3 * count + 21 :]
    rows, length, channels = middle.shape
    heads = bias_w.shape[1]
    place = lax.axis_index("dap")
    eye = identity(channels)
    total = arrived[0][...]
    for ref in arrived[1:]:
        total = total + ref[...].astype(F32)
    d_bias[...] = jnp.zeros_like(d_bias)
    for h in range(heads):
        d_bias[pl.ds(h, rows, stride=HEAD_ROWS), :] = total[:, h * length : (h + 1) * length]
    bias_wide = jnp.concatenate(
        [bias_w[...].astype(F32), jnp.zeros((channels, HEAD_ROWS - heads), F32)], axis=1
    ).astype(BF16)
    gain3 = jnp.broadcast_to(gain3_col[...], (channels, length))
    gain2 = jnp.broadcast_to(gain2_col[...], (channels, length))
    inverse2 = 1.0 / gain2
    grad_out[...] = jnp.zeros_like(grad_out)

    def row(i):
        bias_rows = d_bias[pl.ds(i * HEAD_ROWS, HEAD_ROWS), :].astype(BF16)
        d_normed = d_normed3[i] + mm(bias_wide, bias_rows)
        hat3, scale3 = norm_parts(mmt(eye, middle[i]), 0)
        yield
        d_mid_t = norm_back(d_normed * gain3, hat3, scale3, 0).astype(BF16)
        d_mid_b = mmt(eye, d_mid_t)
        yield
        d_mid = (cotangent[i].astype(F32) + d_mid_b).astype(BF16)
        d_middle_out[i] = d_mid
        gates = gate[i]
        d_mid = d_mid.astype(F32)
        d_up = d_mid * gates
        d_gate_out[i] = (d_up * update[i].astype(F32) * (1.0 - gates)).astype(BF16)
        d_up = d_up.astype(BF16)
        normed2_t = normed2[i]
        d_hat2 = mmt(output_w[...], d_up)
        yield
        hat2 = normed2_t.astype(F32) * inverse2
        lay[pl.ds(i, channels, stride=rows), :] = norm_back(
            d_hat2 * gain2, hat2, scale2[pl.ds(i, 1), :], 0
        )
        return normed2_t, d_up, bias_rows, normed3[i]

    def finish(results):
        normed2_t, d_up, bias_rows, normed = zip(*results)
        grad_out[:channels] += mm(
            jnp.concatenate(normed2_t, axis=1), jnp.concatenate(d_up, axis=0)
        )
        grad_out[channels:] += mm(
            jnp.concatenate(bias_rows, axis=1), jnp.concatenate(normed, axis=0)
        )

    over_rows(rows, W_MIDDLE, row, finish)
    departures = [
        pltpu.make_async_copy(d_middle_out, d_middle_any, row_sems.at[0]),
        pltpu.make_async_copy(d_gate_out, d_gate_any, row_sems.at[1]),
    ]
    start(departures)
    line = lax.broadcasted_iota(jnp.int32, (length, length), 0)
    source = ((line // rows) ^ place) * rows + line % rows
    shuffled = (
        (source == lax.broadcasted_iota(jnp.int32, (length, length), 1)).astype(F32).astype(BF16)
    )

    def group(g, carry):
        block = lay[pl.ds(g * length, length), :].astype(BF16)
        d_product_out[pl.ds(g * length, length), :] = block
        turned = mmt(shuffled, block).astype(BF16)
        for offset in range(count):
            send_outs[offset][g] = turned[offset * rows : (offset + 1) * rows]
        return carry

    parts = 4
    copies = [split_copies(d_product_out, d_product_any, product_sems, parts)] + [
        split_copies(source, target, send_sems.at[at], parts)
        for at, (source, target) in enumerate(zip(send_outs, send_any))
    ]
    share = channels * rows // length // parts
    for part in range(parts):
        lax.fori_loop(part * share, (part + 1) * share, group, 0, unroll=4)
        start([one[part] for one in copies])
    for one in copies:
        wait(one)
    wait(departures)


def gate_back(factors, d_out):
    channels = d_out.shape[0]
    d_value = d_out * factors[:channels].astype(F32)
    d_pre = d_out * factors[channels:].astype(F32)
    return jnp.concatenate([d_value.astype(BF16), d_pre.astype(BF16)], axis=0)


def left_back_kernel(
    right_any, d_product_any, normed1_any, factors_any, d_gate_any, grad_middle, *refs
):
    d_projected_any, packed, lay, grad, d_projected_out, sems = refs[:6]
    right_all, d_product, normed1, factors, d_gate, right_sems, product_sems, in_sems = refs[6:]
    rows, length, channels = normed1.shape
    parts = 4
    first_arrivals = [
        split_copies(right_any, right_all, right_sems, parts),
        split_copies(d_product_any, d_product, product_sems, parts),
    ]
    for part in range(parts):
        start([copies[part] for copies in first_arrivals])
    arrivals = [
        pltpu.make_async_copy(normed1_any, normed1, in_sems.at[0]),
        pltpu.make_async_copy(factors_any, factors, in_sems.at[1]),
        pltpu.make_async_copy(d_gate_any, d_gate, in_sems.at[2]),
    ]
    start(arrivals)

    def channel(c, carry):
        lay[pl.ds(c, rows, stride=channels), :] = mm(
            d_product[pl.ds(c * rows, rows), :], right_all[c]
        )
        return carry

    share = channels // parts
    for part in range(parts):
        wait([copies[part] for copies in first_arrivals])
        lax.fori_loop(part * share, (part + 1) * share, channel, 0, unroll=8)
    wait(arrivals)
    eye = identity(channels)
    grad[...] = jnp.zeros_like(grad)

    def row(i):
        normed = normed1[i]
        d_gate_t = mmt(eye, d_gate[i]).astype(BF16)
        d_projected = gate_back(factors[i], lay[pl.ds(i * channels, channels), :])
        yield
        d_projected = jnp.concatenate([d_projected, d_gate_t], axis=0)
        d_projected_out[i] = d_projected
        return d_projected, normed

    def finish(results):
        d_projected, normed = zip(*results)
        grad[...] += mm(jnp.concatenate(d_projected, axis=1), jnp.concatenate(normed, axis=0))

    parts = 4
    departures = split_copies(d_projected_out, d_projected_any, sems, parts)
    for part in range(parts):
        over_rows(rows // parts, 8, row, finish, first=part * (rows // parts))
        departures[part].start()
    packed[: 3 * channels] = grad[...].astype(BF16)
    packed[3 * channels :] = grad_middle[...].astype(BF16)
    wait(departures)


def right_back_kernel(count, *refs):
    arrived = refs[:count]
    left_halves = refs[count : 2 * count], refs[2 * count : 3 * count]
    refs = refs[count:]
    normed1_any, factors_any, packed_a, packed_b = refs[2 * count : 2 * count + 4]
    d_projected_any = refs[2 * count + 4]
    sends = refs[2 * count + 5 : 3 * count + 5]
    lay, grad, packed, d_projected_out, sems, normed1, factors, in_sems = refs[3 * count + 5 :]
    rows, length, channels = normed1.shape
    arrivals = [
        pltpu.make_async_copy(normed1_any, normed1, in_sems.at[0]),
        pltpu.make_async_copy(factors_any, factors, in_sems.at[1]),
    ]
    start(arrivals)
    per = length // rows
    same = (
        lax.broadcasted_iota(jnp.int32, (length, length), 0) // rows
        == lax.broadcasted_iota(jnp.int32, (length, length), 1) // rows
    )
    mask = same.astype(F32).astype(BF16)

    half = channels // per // 2
    for part, left_blocks in enumerate(left_halves):

        def group(g, carry, left_blocks=left_blocks, first=part * half):
            at = first + g
            spread = jnp.concatenate(
                [jnp.concatenate([ref[at]] * per, axis=0) * mask for ref in arrived], axis=1
            )
            lefts = jnp.concatenate(
                [ref[pl.ds(g * per, per)].reshape(length, length) for ref in left_blocks], axis=0
            )
            lay[pl.ds(at * length, length), :] = mm(spread, lefts)
            return carry

        lax.fori_loop(0, half, group, 0, unroll=4)
    wait(arrivals)
    grad[...] = jnp.zeros_like(grad)

    def row(i):
        normed = normed1[i]
        d_projected = gate_back(factors[i], lay[pl.ds(i, channels, stride=rows), :])
        yield
        d_projected_out[i] = d_projected
        return d_projected, normed

    def finish(results):
        d_projected, normed = zip(*results)
        grad[...] += mm(jnp.concatenate(d_projected, axis=1), jnp.concatenate(normed, axis=0))

    parts = 4
    departures = split_copies(d_projected_out, d_projected_any, sems, parts)
    for part in range(parts):
        over_rows(rows // parts, 8, row, finish, first=part * (rows // parts))
        departures[part].start()
    first, second = packed_a.shape[0], packed_b.shape[0]
    packed[:first] = packed_a[...]
    packed[first : first + second] = packed_b[...]
    packed[first + second : first + second + 2 * channels] = grad[...].astype(BF16)
    packed[first + second + 2 * channels :] = jnp.zeros_like(
        packed[first + second + 2 * channels :]
    )
    size = sends[0].shape[0]
    for offset in range(count):
        begin = pl.multiple_of((lax.axis_index("dap") ^ offset) * size, HEAD_ROWS)
        sends[offset][...] = packed[pl.ds(begin, size), :]
    wait(departures)


def input_back_kernel(part, parts, *refs):
    sources = refs[:4]
    gain_col, input_w, gating = refs[4:7]
    pair_grad_any = refs[-8]
    d_left, d_right, pair, d_middle, pair_grad, sems, out_sem = refs[-7:]
    rows, length, channels = pair.shape
    span = pl.ds(part * rows, rows)
    arrivals = [
        pltpu.make_async_copy(source.at[span], target, sems.at[at])
        for at, (source, target) in enumerate(zip(sources, (d_left, d_right, pair, d_middle)))
    ]
    start(arrivals)
    eye = identity(channels)
    weight = jnp.concatenate(
        [input_w[:, : 2 * channels], gating[...], input_w[:, 2 * channels :]], axis=1
    )
    gain = jnp.broadcast_to(gain_col[...], (channels, length))

    def row(i):
        hat, scale = norm_parts(mmt(eye, pair[i]), 0)
        d_normed = mm(weight, jnp.concatenate([d_left[i], d_right[i]], axis=0))
        yield
        d_pair = mmt(eye, norm_back(d_normed * gain, hat, scale, 0).astype(BF16))
        yield
        pair_grad[i] = (d_middle[i].astype(F32) + d_pair).astype(BF16)

    wait(arrivals)
    over_rows(rows, 8, row)
    departure = pltpu.make_async_copy(pair_grad, pair_grad_any.at[span], out_sem)
    departure.start()
    departure.wait()


def finish_kernel(count, factor, *refs):
    blocks = refs[:count]
    (input1, gating, output1, bias_w, input3, gain1, gain2, gain3) = refs[count : count + 8]
    (
        gain1_out,
        input1_out,
        gating_out,
        gain2_out,
        output1_out,
        gain3_out,
        bias_out,
        input3_out,
        output3_out,
        table_out,
        packed,
    ) = refs[count + 8 :]
    channels = gating.shape[0]
    heads, types = table_out.shape[:2]
    size = blocks[0].shape[0]
    for offset in range(count):
        begin = pl.multiple_of((lax.axis_index("dap") ^ offset) * size, HEAD_ROWS)
        packed[pl.ds(begin, size), :] = blocks[offset][...].astype(F32) * factor
    at = 0

    def take(rows):
        nonlocal at
        at += rows
        return packed[at - rows : at, :]

    input3_t, output3 = take(4 * channels), take(channels)
    table = take(HEAD_ROWS) + take(HEAD_ROWS)
    left_t, gating_t, output1_grad = take(2 * channels), take(channels), take(channels)
    bias_t, right_t = take(HEAD_ROWS), take(2 * channels)
    input1_t = jnp.concatenate([left_t, right_t], axis=0)

    def dots(weight, grad_t):
        return jnp.sum(weight[...].astype(F32).T * grad_t, axis=0, keepdims=True)

    gain1_out[...] = (dots(input1, input1_t) + dots(gating, gating_t)) / gain1[...]
    output_t = (output1[...].astype(F32) * output1_grad).T
    gain2_out[...] = jnp.sum(output_t, axis=0, keepdims=True) / gain2[...]
    gain3_out[...] = (dots(input3, input3_t) + dots(bias_w, bias_t[:heads])) / gain3[...]
    input1_out[...] = input1_t.T
    gating_out[...] = gating_t.T
    output1_out[...] = output1_grad
    bias_out[...] = bias_t.T[:, :heads]
    input3_out[...] = input3_t.T
    output3_out[...] = output3
    for h in range(heads):
        table_out[h] = table[:types, h * types : (h + 1) * types]


def swap(value, axis, step):
    count = lax.axis_size(axis)
    return lax.ppermute(value, axis, [(index, index ^ step) for index in range(count)])


def gather_blocks(block, axis):
    return gather_near(block, swap(block, axis, lax.axis_size(axis) // 2), axis)


def gather_near(block, far, axis):
    half = lax.axis_size(axis) // 2
    blocks = {0: block, half: far}
    for bit in reversed(range(half.bit_length() - 1)):
        step = 1 << bit
        for offset, held in list(blocks.items()):
            blocks[offset ^ step] = swap(held, axis, step)
    return [blocks[offset] for offset in range(len(blocks))]


def sum_over(value, axis):
    step = 1
    while step < lax.axis_size(axis):
        value = value + swap(value, axis, step)
        step *= 2
    return value


def per_device(
    pair_rep,
    cotangent,
    tok_mask,
    tok_types,
    pair_mask,
    triangle_gain,
    triangle_input,
    triangle_gating,
    product_gain,
    triangle_output,
    attend_gain,
    attend_bias,
    attend_input,
    attend_output,
    type_table,
):
    slab = pair_rep[0]
    cot = cotangent[0]
    rows, length, channels = slab.shape
    heads, types = type_table.shape[:2]
    count = lax.axis_size("dap")
    gain1_row, gain3_row = triangle_gain[None, :], attend_gain[None, :]
    gain1_col, gain2_col, gain3_col = (
        triangle_gain[:, None],
        product_gain[:, None],
        attend_gain[:, None],
    )
    vmem = pl.BlockSpec(memory_space=pltpu.VMEM)
    anywhere = pl.BlockSpec(memory_space=pltpu.HBM)
    smem = pl.BlockSpec(memory_space=pltpu.SMEM)
    cell_buffer = pltpu.VMEM((rows, length, channels), BF16)
    cells = (rows, length, channels)
    turned = (rows, channels, length)

    half = rows // 2
    normed1_halves, right_halves, live_halves = [], [], []
    for part in range(2):
        normed_part, right_part, live_part = call(
            partial(right_kernel, part),
            [
                ((half, length, channels), BF16),
                ((channels, half, length), BF16),
                ((half, length), F32),
            ],
            [slab, pair_mask[0], tok_mask, gain1_row, triangle_input],
            in_specs=[anywhere] * 5,
            scratch=[
                pltpu.VMEM((half, length, channels), BF16),
                pltpu.VMEM((half, length), jnp.int32),
                pltpu.VMEM((1, length), jnp.int32),
                pltpu.VMEM((1, channels), F32),
                pltpu.VMEM((channels, 4 * channels), BF16),
                pltpu.VMEM((2 * channels, channels), BF16),
                pltpu.VMEM((channels * half, length), F32),
                pltpu.SemaphoreType.DMA((5,)),
            ],
            us=3.0,
            name="right_projection",
        )
        normed1_halves.append(normed_part)
        right_halves.append(right_part)
        live_halves.append(live_part)
    normed1, left_low, left_high, gate, live, left_factors = call(
        partial(left_kernel, 2),
        [
            (cells, BF16),
            ((channels // 2, rows, length), BF16),
            ((channels // 2, rows, length), BF16),
            (cells, F32),
            ((rows, length), F32),
            ((rows, 2 * channels, length), BF16),
        ],
        [*normed1_halves, *live_halves, triangle_input, triangle_gating],
        out_specs=[anywhere, vmem, vmem, anywhere, vmem, anywhere],
        scratch=[
            pltpu.VMEM((2 * channels, channels), BF16),
            pltpu.VMEM((channels * rows, length), F32),
            pltpu.VMEM(cells, F32),
            pltpu.VMEM((rows, 2 * channels, length), BF16),
            pltpu.SemaphoreType.DMA((3, 2)),
        ],
        us=6.0,
        name="left_projection",
    )
    far = [swap(part, "dap", count // 2) for part in right_halves]
    live, far[0] = lax.optimization_barrier((live, far[0]))
    right_factors, d_gated = call(
        partial(factor_kernel, 2),
        [((rows, 2 * channels, length), BF16), (cells, BF16)],
        [*normed1_halves, live, triangle_input, attend_output, cot],
        in_specs=[vmem] * 5 + [anywhere],
        out_specs=[anywhere] * 2,
        scratch=[
            cell_buffer,
            pltpu.VMEM((rows, 2 * channels, length), BF16),
            cell_buffer,
            pltpu.SemaphoreType.DMA((2,)),
            pltpu.SemaphoreType.DMA((2, 2)),
        ],
        us=5.0,
        name="right_factors",
    )
    right_factors, far[1] = lax.optimization_barrier((right_factors, far[1]))
    left_low_sent, _ = lax.optimization_barrier((left_low, far[1]))
    low_far = swap(left_low_sent, "dap", count // 2)
    right_halves = [
        gather_near(part, other, "dap") for part, other in zip(right_halves, far)
    ]
    right_blocks = [right_halves[index % 2][index // 2] for index in range(2 * count)]
    normed2, update, middle, normed3, right_all, scale2, bias_rows = call(
        partial(product_kernel, count),
        [
            (turned, BF16),
            (cells, BF16),
            (cells, BF16),
            (cells, BF16),
            ((channels, length, length), BF16),
            ((rows, length), F32),
            ((rows, heads * length), BF16),
        ],
        [*right_blocks, left_low, left_high, slab, gate, gain2_col, gain3_row, triangle_output, attend_bias],
        in_specs=[vmem] * (2 * count + 2) + [anywhere] * 2 + [vmem] * 4,
        out_specs=[anywhere] * 5 + [vmem] * 2,
        scratch=[
            pltpu.VMEM((rows * channels, length), F32),
            pltpu.VMEM((rows * HEAD_ROWS, length), F32),
            pltpu.VMEM((channels, length, length), BF16),
        ]
        + [cell_buffer, pltpu.VMEM(cells, F32)]
        + [pltpu.VMEM(turned, BF16)]
        + [cell_buffer] * 3
        + [
            pltpu.SemaphoreType.DMA((2,)),
            pltpu.SemaphoreType.DMA((4, 4)),
            pltpu.SemaphoreType.DMA,
        ],
        us=14.0,
        name="product_and_norms",
    )
    normed3, low_far = lax.optimization_barrier((normed3, low_far))
    bias_far = swap(bias_rows, "dap", count // 2)

    block = 8
    steps = rows // block
    by_row = pl.BlockSpec((block, length, channels), lambda step: (step, 0, 0))
    by_row_wide = pl.BlockSpec((block, 4 * channels, length), lambda step: (step, 0, 0))

    def fixed(*shape):
        return pl.BlockSpec(shape, lambda step: (0,) * len(shape))

    projected3, query, gate3 = call(
        partial(project_kernel, (channels // heads) ** -0.5),
        [((rows, 3 * channels, length), BF16), (cells, BF16), (cells, F32)],
        [normed3, attend_input],
        in_specs=[anywhere] * 2,
        scratch=[
            cell_buffer,
            pltpu.VMEM((channels, 4 * channels), BF16),
            pltpu.VMEM((3 * channels, channels), BF16),
            pltpu.VMEM((channels, 2 * channels), BF16),
            pltpu.VMEM((rows, 3 * channels, length), BF16),
            cell_buffer,
            pltpu.VMEM(cells, F32),
            pltpu.SemaphoreType.DMA((4,)),
            pltpu.SemaphoreType.DMA((3, 4)),
            pltpu.SemaphoreType.DMA,
        ],
        out_specs=[anywhere] * 3,
        us=5.0,
        name="attention_projections",
    )
    projected3, bias_far = lax.optimization_barrier((projected3, bias_far))
    bias_blocks = gather_near(bias_rows, bias_far, "dap")
    left_high_sent, _ = lax.optimization_barrier((left_high, bias_far))
    high_far = swap(left_high_sent, "dap", count // 2)
    attend_outs = call(
        partial(attend_kernel, count),
        [
            (cells, BF16),
            ((rows, 4 * channels, length), BF16),
            ((channels, channels), F32),
            ((HEAD_ROWS, channels), F32),
            ((rows, heads * length), F32),
        ]
        + [((rows, heads * length), BF16)] * (count - 1),
        [type_table.reshape(heads * types, types), *bias_blocks]
        + [tok_types, tok_types.reshape(length, 1), live, attend_output]
        + [projected3, query, gate3, d_gated, cot, middle],
        in_specs=[smem] + [vmem] * (count + 4) + [anywhere] * 6,
        out_specs=[anywhere] + [vmem] * (count + 3),
        scratch=[
            pltpu.VMEM((length, heads * length), F32),
            pltpu.VMEM((length, heads * length), F32),
            pltpu.VMEM((channels, heads * length), BF16),
        ]
        + [pltpu.VMEM((rows, 3 * channels, length), BF16), cell_buffer, pltpu.VMEM(cells, F32)]
        + [cell_buffer] * 4
        + [
            pltpu.SemaphoreType.DMA((6, rows // W_ATTEND)),
            pltpu.SemaphoreType.DMA((rows // W_ATTEND,)),
        ],
        us=20.0,
        name="attention",
    )
    pair_out, d_projected3, d_output, d_table = attend_outs[:4]
    d_table, high_far = lax.optimization_barrier((d_table, high_far))
    d_bias_parts = [attend_outs[4]] + [
        swap(attend_outs[4 + offset], "dap", offset) for offset in range(1, count)
    ]
    d_normed3, packed_a = call(
        projection_kernel,
        [(turned, F32), ((4 * channels + channels + 2 * HEAD_ROWS, channels), BF16)],
        [d_projected3, normed3, attend_input, d_output, d_table],
        grid=(steps,),
        in_specs=[by_row_wide, by_row, fixed(channels, 4 * channels)]
        + [fixed(channels, channels), fixed(HEAD_ROWS, channels)],
        out_specs=[
            pl.BlockSpec((block, channels, length), lambda step: (step, 0, 0)),
            fixed(5 * channels + 2 * HEAD_ROWS, channels),
        ],
        scratch=[pltpu.VMEM((4 * channels, channels), F32)],
        us=6.0,
        name="projection_back",
    )
    groups = channels * rows // length
    middle_outs = call(
        partial(middle_kernel, count),
        [
            (cells, BF16),
            (cells, BF16),
            ((channels * rows, length), BF16),
            ((channels + HEAD_ROWS, channels), F32),
        ]
        + [((groups, rows, length), BF16)] * count,
        [*d_bias_parts, d_normed3, normed3, middle, cot, gain3_col, attend_bias]
        + [normed2, scale2, update, gate, gain2_col, triangle_output],
        out_specs=[anywhere] * 3 + [vmem] + [anywhere] * count,
        scratch=[
            pltpu.VMEM((rows * HEAD_ROWS, length), F32),
            pltpu.VMEM((channels * rows, length), F32),
            cell_buffer,
            cell_buffer,
            pltpu.VMEM((channels * rows, length), BF16),
        ]
        + [pltpu.VMEM((groups, rows, length), BF16)] * count
        + [
            pltpu.SemaphoreType.DMA((2,)),
            pltpu.SemaphoreType.DMA((4,)),
            pltpu.SemaphoreType.DMA((count, 4)),
        ],
        us=12.0,
        name="middle_back",
    )
    d_middle, d_gate, d_product, grad_middle = middle_outs[:4]
    d_middle, low_far, high_far = lax.optimization_barrier((d_middle, low_far, high_far))
    left_blocks = gather_near(left_low, low_far, "dap") + gather_near(left_high, high_far, "dap")
    product_parts = [middle_outs[4]] + [
        swap(middle_outs[4 + offset], "dap", offset) for offset in range(1, count)
    ]
    d_left, packed_b = call(
        left_back_kernel,
        [((rows, 3 * channels, length), BF16), ((4 * channels + HEAD_ROWS, channels), BF16)],
        [right_all, d_product, normed1, left_factors, d_gate, grad_middle],
        scratch=[
            pltpu.VMEM((rows * channels, length), F32),
            pltpu.VMEM((3 * channels, channels), F32),
            pltpu.VMEM((rows, 3 * channels, length), BF16),
            pltpu.SemaphoreType.DMA((4,)),
            pltpu.VMEM((channels, length, length), BF16),
            pltpu.VMEM((channels * rows, length), BF16),
            cell_buffer,
            pltpu.VMEM((rows, 2 * channels, length), BF16),
            cell_buffer,
            pltpu.SemaphoreType.DMA((4,)),
            pltpu.SemaphoreType.DMA((4,)),
            pltpu.SemaphoreType.DMA((3,)),
        ],
        in_specs=[anywhere] * 5 + [vmem],
        out_specs=[anywhere, vmem],
        us=10.0,
        name="left_back",
    )
    used = packed_a.shape[0] + packed_b.shape[0] + 2 * channels
    share = -(-used // (count * HEAD_ROWS)) * HEAD_ROWS
    right_outs = call(
        partial(right_back_kernel, count),
        [((rows, 2 * channels, length), BF16)] + [((share, channels), BF16)] * count,
        [*product_parts, *left_blocks, normed1, right_factors, packed_a, packed_b],
        in_specs=[vmem] * (3 * count) + [anywhere] * 2 + [vmem] * 2,
        out_specs=[anywhere] + [vmem] * count,
        scratch=[
            pltpu.VMEM((channels * rows, length), F32),
            pltpu.VMEM((2 * channels, channels), F32),
            pltpu.VMEM((share * count, channels), BF16),
            pltpu.VMEM((rows, 2 * channels, length), BF16),
            pltpu.SemaphoreType.DMA((4,)),
            cell_buffer,
            pltpu.VMEM((rows, 2 * channels, length), BF16),
            pltpu.SemaphoreType.DMA((2,)),
        ],
        us=7.0,
        name="right_back",
    )
    d_right = right_outs[0]
    parts = 4
    some = (rows // parts, length, channels)
    pair_grad = None

    def input_back(part, pair_grad):
        given = [] if pair_grad is None else [pair_grad]
        (pair_grad,) = call(
            partial(input_back_kernel, part, parts),
            [(cells, BF16)],
            [d_left, d_right, slab, d_middle, gain1_col, triangle_input, triangle_gating, *given],
            in_specs=[anywhere] * 4 + [vmem] * 3 + [anywhere] * len(given),
            out_specs=[anywhere],
            scratch=[
                pltpu.VMEM((rows // parts, 3 * channels, length), BF16),
                pltpu.VMEM((rows // parts, 2 * channels, length), BF16),
                pltpu.VMEM(some, BF16),
                pltpu.VMEM(some, BF16),
                pltpu.VMEM(some, BF16),
                pltpu.SemaphoreType.DMA((4,)),
                pltpu.SemaphoreType.DMA,
            ],
            aliases={7: 0} if given else None,
            us=3.0,
            name="input_back",
        )
        return pair_grad

    grad_share = right_outs[1].astype(F32)
    for offset in range(1, count):
        grad_share = grad_share + swap(right_outs[1 + offset], "dap", offset).astype(F32)
    grad_share = grad_share.astype(BF16)
    done = 0
    step = 1
    while step < lax.axis_size("dp"):
        if done < parts - 1:
            pair_grad = input_back(done, pair_grad)
            grad_share, pair_grad = lax.optimization_barrier((grad_share, pair_grad))
            done += 1
        grad_share = grad_share + swap(grad_share, "dp", step)
        step *= 2
    grad_blocks = [grad_share] + [
        swap(grad_share, "dap", offset) for offset in range(1, count)
    ]
    while done < parts:
        pair_grad = input_back(done, pair_grad)
        done += 1
    pair_grad, *grad_blocks = lax.optimization_barrier((pair_grad, *grad_blocks))
    weights = (triangle_input, triangle_gating, triangle_output, attend_bias, attend_input)
    gains = (gain1_row, product_gain[None, :], gain3_row)
    grads = call(
        partial(finish_kernel, count, (length * length * lax.axis_size("dp")) ** (-0.5)),
        [
            ((1, channels), F32),
            (triangle_input.shape, F32),
            (triangle_gating.shape, F32),
            ((1, channels), F32),
            (triangle_output.shape, F32),
            ((1, channels), F32),
            (attend_bias.shape, F32),
            (attend_input.shape, F32),
            (attend_output.shape, F32),
            (type_table.shape, F32),
        ],
        [*grad_blocks, *weights, *gains],
        scratch=[pltpu.VMEM((share * count, channels), F32)],
        us=3.0,
        name="scale_gradients",
    )
    grads = [grad[0] if grad.shape[0] == 1 else grad for grad in grads]
    return (pair_out[None], pair_grad[None], *grads)


def solution(mesh):
    return jax.shard_map(
        per_device,
        mesh=mesh,
        in_specs=(
            P("dp", "dap", None, None),
            P("dp", "dap", None, None),
            P("dp", None),
            P("dp", None),
            P("dp", "dap", None),
        )
        + (P(),) * 10,
        out_specs=(
            P("dp", "dap", None, None),
            P("dp", "dap", None, None),
        )
        + (P(),) * 10,
        check_vma=False,
    )
```

```python
import math
from functools import partial

import jax
import jax.numpy as jnp
from jax import lax
from jax.experimental import pallas as pl
from jax.experimental.pallas import tpu as pltpu
from jax.sharding import PartitionSpec as P

EPSILON = 1e-05
F32 = jnp.float32
BF16 = jnp.bfloat16
VMEM_MARGIN = 4 * 1024 * 1024
W_PRODUCT, W_ATTEND, W_MIDDLE = 8, 4, 8
LOG2_E = math.log2(math.e)
HEAD_ROWS = 16


def mm(left, right):
    return lax.dot_general(left, right, (((1,), (0,)), ((), ())), preferred_element_type=F32)


def mmt(left, right):
    return lax.dot_general(left, right, (((1,), (1,)), ((), ())), preferred_element_type=F32)


def sigmoid(value):
    return 0.5 + 0.5 * jnp.tanh(0.5 * value)


def norm_parts(values, axis):
    centred = values - jnp.mean(values, axis=axis, keepdims=True)
    spread = jnp.mean(centred * centred, axis=axis, keepdims=True)
    scale = lax.rsqrt(spread + EPSILON)
    return centred * scale, scale


def norm_back(d_hat, hat, scale, axis):
    first = jnp.mean(d_hat, axis=axis, keepdims=True)
    second = jnp.mean(d_hat * hat, axis=axis, keepdims=True)
    return scale * (d_hat - first - hat * second)


def lockstep(row, indices):
    going = [row(index) for index in indices]
    results = [None] * len(going)
    running = True
    while running:
        for at, one in enumerate(going):
            try:
                next(one)
            except StopIteration as stop:
                results[at] = stop.value
                running = False
    return results


def over_rows(count, width, row, finish=None, first=0):
    def some(index, carry):
        results = lockstep(row, [first + index * width + at for at in range(width)])
        if finish is not None:
            finish(results)
        return carry

    lax.fori_loop(0, count // width, some, 0)


def side_by_side(first, last, body, most=16):
    unroll = max(one for one in range(1, most + 1) if (last - first) % one == 0)
    lax.fori_loop(first, last, lambda index, carry: body(index), None, unroll=unroll)


def split_copies(source, target, sems, parts):
    size = source.shape[0] // parts
    return [
        pltpu.make_async_copy(
            source.at[pl.ds(part * size, size)], target.at[pl.ds(part * size, size)], sems.at[part]
        )
        for part in range(parts)
    ]


def start(copies):
    for copy in copies:
        copy.start()


def wait(copies):
    for copy in copies:
        copy.wait()


def call(kernel, outs, args, scratch=(), grid=(), in_specs=None, out_specs=None, us=5.0, name=None, aliases=None):
    whole = pl.BlockSpec(memory_space=pltpu.VMEM)
    in_specs = in_specs or [whole] * len(args)
    out_specs = out_specs or [whole] * len(outs)
    held = sum(
        math.prod(one.shape) * jnp.dtype(one.dtype).itemsize
        for one in scratch
        if getattr(one, "memory_space", None) == pltpu.VMEM
    )
    args = [
        pltpu.with_memory_space_constraint(arg, pltpu.HBM)
        if spec.memory_space == pltpu.HBM
        else arg
        for arg, spec in zip(args, in_specs)
    ]
    return pl.pallas_call(
        kernel,
        out_shape=[
            pltpu.HBM(shape, dtype)
            if spec.memory_space == pltpu.HBM
            else jax.ShapeDtypeStruct(shape, dtype)
            for (shape, dtype), spec in zip(outs, out_specs)
        ],
        grid=grid,
        in_specs=in_specs,
        out_specs=out_specs,
        scratch_shapes=list(scratch),
        compiler_params=pltpu.CompilerParams(vmem_limit_bytes=held + VMEM_MARGIN),
        cost_estimate=pl.CostEstimate(
            flops=int(us * 1.0e9), bytes_accessed=int(us * 3.0e6), transcendentals=0
        ),
        input_output_aliases=aliases or {},
        name=name,
    )(*args)


def right_kernel(part, pair_any, mask_any, tokens_any, gain_any, weight_any, *refs):
    normed_any, right_out, live_out = refs[-12:-9]
    pair, mask, tokens, gain, weight, weight_t, lay, normed_out, sems = refs[-9:]
    rows, length, channels = pair.shape
    place = lax.axis_index("dap")
    span = pl.ds(part * rows, rows)
    sources = [mask_any.at[span], tokens_any, gain_any, weight_any, pair_any.at[span]]
    copies = [
        pltpu.make_async_copy(source, target, sems.at[at])
        for at, (source, target) in enumerate(zip(sources, (mask, tokens, gain, weight, pair)))
    ]
    start(copies)
    wait(copies)
    first = place * (mask_any.shape[0]) + part * rows
    lines = lax.broadcasted_iota(jnp.int32, (rows, length), 0) + first
    lanes = lax.broadcasted_iota(jnp.int32, (rows, length), 1)
    wide = tokens[...].astype(F32)
    own = jnp.sum(jnp.where(lines == lanes, wide, 0.0), axis=1, keepdims=True)
    live_out[...] = mask[...].astype(F32) * own * wide
    weight_t[...] = weight[:, 2 * channels : 4 * channels].astype(F32).T.astype(BF16)

    def row(i):
        hat, _ = norm_parts(pair[i].astype(F32), -1)
        yield
        normed = (hat * gain[...]).astype(BF16)
        normed_out[i] = normed
        projected = mmt(weight_t[...], normed)
        yield
        right = sigmoid(projected[channels:]) * projected[:channels] * live_out[pl.ds(i, 1), :]
        lay[pl.ds(i, channels, stride=rows), :] = right

    over_rows(rows, 8, row)
    departure = pltpu.make_async_copy(normed_out, normed_any.at[span], sems.at[5])
    departure.start()
    right_out[...] = lay[...].reshape(channels, rows, length).astype(BF16)
    departure.wait()


def gate_factors(projected, live_row, channels):
    value, pre = projected[:channels], projected[channels:]
    gate = sigmoid(pre)
    slope = gate * live_row
    out = slope * value
    factors = jnp.concatenate([slope.astype(BF16), (out * (1.0 - gate)).astype(BF16)], axis=0)
    return out, factors


def left_kernel(parts, normed_any, *refs):
    live_parts = refs[:parts]
    weight, gating = refs[parts : parts + 2]
    low_out, high_out, gate_any, live, factor_any = refs[parts + 2 : parts + 7]
    weight_t, lay, gates, factors, normed1, in_sems, sems = refs[parts + 7 :]
    arrivals = split_copies(normed_any, normed1, in_sems, parts)
    start(arrivals)
    rows, length, channels = gates.shape
    half = rows // parts
    weight_t[...] = weight[:, : 2 * channels].astype(F32).T.astype(BF16)
    outs = []
    for part in range(parts):
        span = pl.ds(part * half, half)
        live[span, :] = live_parts[part][...]
        arrivals[part].wait()

        def row(i, part=part):
            at = i + part * half
            normed = normed1[at]
            projected = mmt(weight_t[...], normed)
            gate = mm(normed, gating[...])
            yield
            left, factors[at] = gate_factors(projected, live[pl.ds(at, 1), :], channels)
            lay[pl.ds(at, channels, stride=rows), :] = left
            gates[at] = sigmoid(gate)

        over_rows(half, 8, row)
        for index, (source, target) in enumerate(((gates, gate_any), (factors, factor_any))):
            copy = pltpu.make_async_copy(
                source.at[span], target.at[span], sems.at[index, part]
            )
            copy.start()
            outs.append(copy)
    left = lay[...].reshape(channels, rows, length).astype(BF16)
    low = low_out.shape[0]
    low_out[...] = left[:low]
    high_out[...] = left[low:]
    wait(outs)


def factor_kernel(parts, *refs):
    live, weight, output_w, normed_any, cotangent_any, factor_any, d_gated_any = refs[:7]
    normed1, cotangent, factors, d_gated, in_sems, sems = refs[7:]
    rows, length, channels = cotangent.shape
    half = rows // parts
    arrivals = [
        split_copies(normed_any, normed1, in_sems.at[0], parts),
        split_copies(cotangent_any, cotangent, in_sems.at[1], parts),
    ]
    for copies in arrivals:
        start(copies)
    weight_t = weight[:, 2 * channels : 4 * channels].astype(F32).T.astype(BF16)
    departures = [
        split_copies(factors, factor_any, sems.at[0], parts),
        split_copies(d_gated, d_gated_any, sems.at[1], parts),
    ]
    for part in range(parts):
        wait([copies[part] for copies in arrivals])

        def row(i, part=part):
            at = i + part * half
            projected = mmt(weight_t, normed1[at])
            back = mmt(cotangent[at], output_w[...])
            yield
            _, factors[at] = gate_factors(projected, live[pl.ds(at, 1), :], channels)
            d_gated[at] = back.astype(BF16)

        over_rows(half, 8, row)
        start([copies[part] for copies in departures])
    for copies in departures:
        wait(copies)


def product_kernel(count, side, *refs):
    near = count // 2
    blocks = refs[: 2 * near]
    lefts = refs[2 * near : 2 * near + 2]
    (pair_any, gate_any, gain2_col, gain3, output_w, bias_w) = refs[2 * near + 2 : 2 * near + 8]
    rest = refs[2 * near + 8 :]
    if side:
        bias_any, rest = rest[0], rest[5:]
    row_outs = rest[:4]
    right_any, scale2_out, bias_out, product, bias_scr, right_side, pair, gate = rest[4:12]
    kept = rest[12:16]
    normed2_out, update_out, middle_out, normed3_out = kept
    in_sems, out_sems, right_sem, bias_sem, bias_near = rest[16:]
    rows, wide, channels = pair.shape
    length = 2 * wide
    lines = rows // 2
    heads = bias_w.shape[1]
    place = lax.axis_index("dap")
    chip = place // near
    span = pl.ds(pl.multiple_of((chip ^ side) * wide, wide), wide)
    arrivals = [
        pltpu.make_async_copy(pair_any.at[:, span, :], pair, in_sems.at[0]),
        pltpu.make_async_copy(gate_any.at[:, span, :], gate, in_sems.at[1]),
    ]
    start(arrivals)
    if side:
        bias_copy = pltpu.make_async_copy(bias_any, bias_near, bias_sem)
        bias_copy.start()
    size = blocks[0].shape[1]
    starts = [
        pl.multiple_of(((place ^ (index // 2)) % near) * rows + (index % 2) * size, size)
        for index in range(2 * near)
    ]

    def channel(c):
        for begin, ref in zip(starts, blocks):
            right_side[c, pl.ds(begin, size), :] = ref[c]

    side_by_side(0, channels, channel)
    right_copy = pltpu.make_async_copy(right_side, right_any, right_sem)
    right_copy.start()
    for left, first in zip(lefts, (0, lefts[0].shape[0])):

        def multiply(pair_of, left=left, first=first):
            c = 2 * pair_of
            cells = mmt(
                left[pl.ds(c, 2)].reshape(2 * rows, length),
                right_side[pl.ds(first + c, 2)].reshape(length, length),
            )
            for one in range(2):
                mine = cells[one * rows : (one + 1) * rows, one * wide : (one + 1) * wide]
                product[pl.ds(first + c + one, lines, stride=channels), :] = jnp.concatenate(
                    [mine[:lines], mine[lines:]], axis=1
                )

        side_by_side(0, left.shape[0] // 2, multiply)
    gain2 = jnp.broadcast_to(gain2_col[...], (channels, length))
    bias_t = jnp.concatenate(
        [bias_w[...].astype(F32).T, jnp.zeros((HEAD_ROWS - heads, channels), F32)], axis=0
    ).astype(BF16)

    def tile(p):
        hat, scale = norm_parts(product[pl.ds(p * channels, channels), :], 0)
        yield
        normed2_t = (hat * gain2).astype(BF16)
        normed2_out[p] = normed2_t
        scale2_out[pl.ds(p, 1), :] = scale
        normed2 = normed2_t.T
        yield
        update = mm(normed2, output_w[...])
        yield
        update_b = update.astype(BF16)
        gates = jnp.concatenate([gate[p], gate[p + lines]], axis=0)
        pairs = jnp.concatenate([pair[p], pair[p + lines]], axis=0)
        middle = (pairs.astype(F32) + gates * update).astype(BF16)
        hat3, _ = norm_parts(middle.astype(F32), -1)
        yield
        normed3 = (hat3 * gain3[...]).astype(BF16)
        bias_scr[pl.ds(p * HEAD_ROWS, HEAD_ROWS), :] = mmt(bias_t, normed3)
        for out, value in ((update_out, update_b), (middle_out, middle), (normed3_out, normed3)):
            out[p] = value[:wide]
            out[p + lines] = value[wide:]

    wait(arrivals)
    parts = 2
    run = lines // parts
    departures = []
    for part in range(parts):
        over_rows(run, W_PRODUCT, tile, first=part * run)
        some = pl.ds(part * run, run)
        copies = [
            pltpu.make_async_copy(
                normed2_out.at[some], row_outs[0].at[side, some], out_sems.at[0, part]
            )
        ]
        for at in range(1, 4):
            for group in range(2):
                some = pl.ds(group * lines + part * run, run)
                copies.append(
                    pltpu.make_async_copy(
                        kept[at].at[some],
                        row_outs[at].at[some, span, :],
                        out_sems.at[at, 2 * part + group],
                    )
                )
        start(copies)
        departures += copies
    if not side:
        copy = pltpu.make_async_copy(bias_scr, bias_out, bias_sem)
        copy.start()
        departures.append(copy)
    else:
        bias_copy.wait()
        for h in range(heads):
            mine = bias_near[pl.ds(h, lines, stride=HEAD_ROWS), :]
            other = bias_scr[pl.ds(h, lines, stride=HEAD_ROWS), :]
            first = jnp.where(chip == 0, mine, other)
            second = jnp.where(chip == 0, other, mine)
            head = slice(h * length, (h + 1) * length)
            low = jnp.concatenate([first[:, :wide], second[:, :wide]], axis=1)
            high = jnp.concatenate([first[:, wide:], second[:, wide:]], axis=1)
            bias_out[:lines, head] = low.astype(BF16)
            bias_out[lines:, head] = high.astype(BF16)
    wait(departures)
    right_copy.wait()


def project_kernel(factor, normed3_any, weight_any, projected_any, query_any, gate_any, *scratch):
    normed3, weight, weight_t, weight_qg, projected3, queries, gates, sems, out_sems, weight_sem = (
        scratch
    )
    rows, length, channels = normed3.shape
    kept = projected3.shape[1]
    parts = 4
    copy = pltpu.make_async_copy(weight_any, weight, weight_sem)
    copy.start()
    arrivals = split_copies(normed3_any, normed3, sems, parts)
    start(arrivals)
    copy.wait()
    weight_t[...] = weight[:, :kept].astype(F32).T.astype(BF16)
    weight_qg[:, :channels] = weight[:, :channels]
    weight_qg[:, channels:] = weight[:, kept:]

    def row(i):
        normed = normed3[i]
        projected_t = mmt(weight_t[...], normed)
        projected = mm(normed, weight_qg[...])
        yield
        projected3[i, :channels] = (projected_t[:channels] * factor).astype(BF16)
        projected3[i, channels:] = projected_t[channels:].astype(BF16)
        queries[i] = (projected[:, :channels] * (factor * LOG2_E)).astype(BF16)
        gates[i] = sigmoid(projected[:, channels:])

    departures = [
        split_copies(source, target, out_sems.at[at], parts)
        for at, (source, target) in enumerate(
            ((projected3, projected_any), (queries, query_any), (gates, gate_any))
        )
    ]
    for part in range(parts):
        arrivals[part].wait()
        over_rows(rows // parts, 8, row, first=part * (rows // parts))
        start([copies[part] for copies in departures])
    for copies in departures:
        wait(copies)


def attend_kernel(count, table, *refs):
    bias_refs = refs[:count]
    types_row, types_col, live, output_w = refs[count : count + 4]
    row_arrays = refs[count + 4 : count + 10]
    (pair_out_any, d_projected, d_output, d_table) = refs[count + 10 : count + 14]
    d_bias_outs = refs[count + 14 : 2 * count + 14]
    bias, d_bias, head_mask = refs[2 * count + 14 : 2 * count + 17]
    fetched = refs[2 * count + 17 : 2 * count + 23]
    projected, queries, gates, d_gateds, cotangent, middle = fetched
    pair_out, in_sems, out_sems = refs[2 * count + 23 :]
    rows, length, channels = middle.shape
    types = table.shape[1]
    heads = table.shape[0] // types
    size = channels // heads
    own = bias_refs[0].shape[0]
    factor = size ** -0.5
    place = lax.axis_index("dap")
    parts = rows // W_ATTEND
    arrivals = [
        split_copies(source, target, in_sems.at[at], parts)
        for at, (source, target) in enumerate(zip(row_arrays, fetched))
    ]
    for part in range(parts):
        start([copies[part] for copies in arrivals])

    def spans(h):
        return slice(h * length, (h + 1) * length)

    for offset in range(count):
        begin = pl.multiple_of((place ^ offset) * own, own)
        bias[pl.ds(begin, own), :] = bias_refs[offset][...].astype(F32)
    row_types = types_row[...]
    col_types = types_col[...]
    for h in range(heads):
        total = jnp.zeros((length, length), F32)
        for a in range(types):
            values = jnp.zeros((1, length), F32)
            for b in range(types):
                values = jnp.where(row_types == b, table[h * types + a, b], values)
            total = jnp.where(col_types == a, values, total)
        bias[:, spans(h)] = (bias[:, spans(h)] + total) * LOG2_E
    d_bias[...] = jnp.zeros_like(d_bias)
    d_output[...] = jnp.zeros_like(d_output)
    lines = lax.broadcasted_iota(jnp.int32, head_mask.shape, 0) // size
    columns = lax.broadcasted_iota(jnp.int32, head_mask.shape, 1) // length
    head_mask[...] = (lines == columns).astype(F32).astype(BF16)


    def row(i):
        live_row = live[pl.ds(i, 1), :]
        live_wide = jnp.concatenate([live_row.astype(BF16)] * heads, axis=1)
        query_t = projected[i, :channels]
        key_t = projected[i, channels : 2 * channels]
        value_t = projected[i, 2 * channels :]
        gate = gates[i]
        d_gated = d_gateds[i].astype(F32)
        mask = head_mask[...]
        ones = mask * live_wide
        keys = jnp.concatenate([key_t] * heads, axis=1) * mask
        values = jnp.concatenate(
            [jnp.concatenate([value_t] * heads, axis=1) * ones, ones], axis=0
        )
        score = mm(queries[i], keys)
        yield
        expo = jnp.exp2(score + bias[...])
        expo_b = expo.astype(BF16)
        sums = mmt(expo_b, values)
        yield
        total = sums[:, channels:]
        inverse = 1.0 / jnp.maximum(total, 1.0)
        attended = sums[:, :channels] * inverse
        gated = (gate * attended).astype(BF16)
        d_attended = d_gated * gate * inverse
        d_gate = d_gated * attended * gate * (1.0 - gate)
        slope = jnp.where(total > 1.0, 1.0, jnp.where(total == 1.0, 0.5, 0.0))
        d_attended_b = d_attended.astype(BF16)
        both = jnp.concatenate(
            [d_attended_b, (-d_attended * attended * slope).astype(BF16)], axis=1
        )
        d_expo = mm(both, values)
        turned = jnp.concatenate([d_attended_b.T, d_gate.astype(BF16).T, gated.T], axis=1)
        yield
        update = mm(gated, output_w[...])
        d_score = expo * d_expo
        d_score_b = d_score.astype(BF16)
        d_query_t = mmt(keys, d_score_b) * factor
        d_key_t = mm(query_t, d_score_b)
        d_value_t = mm(turned[:, :length], expo_b)
        yield
        pair_out[i] = (middle[i].astype(F32) + update).astype(BF16)

        def diagonal(full):
            return jnp.concatenate(
                [full[h * size : (h + 1) * size, spans(h)] for h in range(heads)], axis=0
            )

        d_projected[i, :channels] = d_query_t.astype(BF16)
        d_projected[i, channels : 2 * channels] = diagonal(d_key_t).astype(BF16)
        d_projected[i, 2 * channels : 3 * channels] = (diagonal(d_value_t) * live_row).astype(BF16)
        d_projected[i, 3 * channels :] = turned[:, length : 2 * length]
        return turned[:, 2 * length :], cotangent[i], d_score

    def finish(results):
        gated_t, cots, d_scores = zip(*results)
        d_output[...] += mm(jnp.concatenate(gated_t, axis=1), jnp.concatenate(cots, axis=0))
        d_bias[...] += sum(d_scores)

    departures = split_copies(pair_out, pair_out_any, out_sems, parts)
    for part in range(parts):
        wait([copies[part] for copies in arrivals])
        over_rows(rows // parts, W_ATTEND, row, finish, first=part * (rows // parts))
        departures[part].start()

    for offset in range(count):
        begin = pl.multiple_of((place ^ offset) * own, own)
        ref = d_bias_outs[offset]
        ref[...] = d_bias[pl.ds(begin, own), :].astype(ref.dtype)
    high = d_bias[...].astype(BF16)
    low = (d_bias[...] - high.astype(F32)).astype(BF16)
    kinds = lax.broadcasted_iota(jnp.int32, (HEAD_ROWS, length), 0)
    picks = (types_row[...] == kinds).astype(F32).astype(BF16)
    by_row = mm(picks, high) + mm(picks, low)
    lanes = lax.broadcasted_iota(jnp.int32, (HEAD_ROWS, channels), 1)
    grad = jnp.zeros((HEAD_ROWS, channels), F32)
    for h in range(heads):
        part = by_row[:, spans(h)]
        for b in range(types):
            one = jnp.sum(jnp.where(types_row[...] == b, part, 0.0), axis=1, keepdims=True)
            grad = jnp.where(lanes == h * types + b, one, grad)
    d_table[...] = grad
    wait(departures)


def projection_kernel(d_projected, normed3, input_w, d_output, d_table, d_normed, packed, total):
    block = normed3.shape[0]
    wide, length = d_projected.shape[1:]
    channels = normed3.shape[2]
    step = pl.program_id(0)

    @pl.when(step == 0)
    def _():
        total[...] = jnp.zeros_like(total)

    def rows(index, carry):
        at = [4 * index + one for one in range(4)]
        both = jnp.concatenate([d_projected[one] for one in at], axis=1)
        total[...] += mm(both, jnp.concatenate([normed3[one] for one in at], axis=0))
        d_both = mm(input_w[...], both)
        for order, one in enumerate(at):
            d_normed[one] = d_both[:, order * length : (order + 1) * length]
        return carry

    lax.fori_loop(0, block // 4, rows, 0, unroll=2)

    @pl.when(step == pl.num_programs(0) - 1)
    def _():
        packed[:wide] = total[...].astype(BF16)
        packed[wide : wide + channels] = d_output[...].astype(BF16)
        high = d_table[...].astype(BF16)
        packed[wide + channels : wide + channels + HEAD_ROWS] = high
        packed[wide + channels + HEAD_ROWS :] = (d_table[...] - high.astype(F32)).astype(BF16)


def middle_kernel(count, *refs):
    arrived = refs[:count]
    (d_normed3, normed3, middle, cotangent, gain3_col, bias_w) = refs[count : count + 6]
    normed2, *scales = refs[count + 6 : count + 9]
    refs = refs[1:]
    (update, gate, gain2_col, output_w) = refs[count + 8 : count + 12]
    (d_middle_any, d_gate_any, d_product_any, grad_out) = refs[count + 12 : count + 16]
    send_any = refs[count + 16 : 2 * count + 16]
    d_bias, lay, d_middle_out, d_gate_out, d_product_out = refs[2 * count + 16 : 2 * count + 21]
    send_outs = refs[2 * count + 21 : 3 * count + 21]
    row_sems, product_sems, send_sems = refs[3 * count + 21 :]
    rows, length, channels = middle.shape
    heads = bias_w.shape[1]
    place = lax.axis_index("dap")
    chip = place // (count // 2)
    lines, wide = rows // 2, length // 2
    total = arrived[0][...]
    for ref in arrived[1:]:
        total = total + ref[...].astype(F32)
    d_bias[...] = jnp.zeros_like(d_bias)
    for h in range(heads):
        d_bias[pl.ds(h, rows, stride=HEAD_ROWS), :] = total[:, h * length : (h + 1) * length]
    bias_wide = jnp.concatenate(
        [bias_w[...].astype(F32), jnp.zeros((channels, HEAD_ROWS - heads), F32)], axis=1
    ).astype(BF16)
    gain3 = jnp.broadcast_to(gain3_col[...], (channels, length))
    gain2 = jnp.broadcast_to(gain2_col[...], (channels, length))
    inverse2 = 1.0 / gain2
    grad_out[...] = jnp.zeros_like(grad_out)

    def row(i):
        bias_rows = d_bias[pl.ds(i * HEAD_ROWS, HEAD_ROWS), :].astype(BF16)
        d_normed = d_normed3[i] + mm(bias_wide, bias_rows)
        hat3, scale3 = norm_parts(middle[i].T.astype(F32), 0)
        yield
        d_mid_t = norm_back(d_normed * gain3, hat3, scale3, 0).astype(BF16)
        d_mid_b = d_mid_t.T.astype(F32)
        yield
        d_mid = (cotangent[i].astype(F32) + d_mid_b).astype(BF16)
        d_middle_out[i] = d_mid
        gates = gate[i]
        d_mid = d_mid.astype(F32)
        d_up = d_mid * gates
        d_gate_out[i] = (d_up * update[i].astype(F32) * (1.0 - gates)).astype(BF16)
        return d_up.astype(BF16), bias_rows, normed3[i]

    def two_rows(p):
        low, high = row(p), row(p + lines)
        for _ in range(2):
            next(low)
            next(high)
            yield
        low, high = [lockstep(lambda one: one, [one])[0] for one in (low, high)]
        tiles = []
        for t in range(2):
            d_up = jnp.concatenate(
                [one[0][t * wide : (t + 1) * wide] for one in (low, high)], axis=0
            )
            tiles.append((normed2[chip ^ t, p], d_up, mmt(output_w[...], d_up)))
        yield
        backs = []
        for t, (normed2_t, _, d_hat2) in enumerate(tiles):
            scale2 = jnp.where(
                chip == t, scales[0][pl.ds(p, 1), :], scales[1][pl.ds(p, 1), :]
            )
            hat2 = normed2_t.astype(F32) * inverse2
            backs.append(norm_back(d_hat2 * gain2, hat2, scale2, 0))
        yield
        for group, i in enumerate((p, p + lines)):
            part = slice(group * wide, (group + 1) * wide)
            lay[pl.ds(i, channels, stride=rows), :] = jnp.concatenate(
                [back[:, part] for back in backs], axis=1
            )
        return tiles, (low[1], high[1]), (low[2], high[2])

    def finish(results):
        tiles, bias_rows, normed = [sum((tuple(one) for one in each), ()) for each in zip(*results)]
        grad_out[:channels] += mm(
            jnp.concatenate([one[0] for one in tiles], axis=1),
            jnp.concatenate([one[1] for one in tiles], axis=0),
        )
        grad_out[channels:] += mm(
            jnp.concatenate(bias_rows, axis=1), jnp.concatenate(normed, axis=0)
        )

    over_rows(lines, W_MIDDLE // 2, two_rows, finish)
    departures = [
        pltpu.make_async_copy(d_middle_out, d_middle_any, row_sems.at[0]),
        pltpu.make_async_copy(d_gate_out, d_gate_any, row_sems.at[1]),
    ]
    start(departures)
    line = lax.broadcasted_iota(jnp.int32, (length, length), 0)
    source = ((line // rows) ^ place) * rows + line % rows
    shuffled = (
        (source == lax.broadcasted_iota(jnp.int32, (length, length), 1)).astype(F32).astype(BF16)
    )

    def group(g):
        block = lay[pl.ds(g * length, length), :].astype(BF16)
        d_product_out[pl.ds(g * length, length), :] = block
        turned = mmt(shuffled, block).astype(BF16)
        for offset in range(count):
            send_outs[offset][g] = turned[offset * rows : (offset + 1) * rows]

    parts = 4
    copies = [split_copies(d_product_out, d_product_any, product_sems, parts)] + [
        split_copies(source, target, send_sems.at[at], parts)
        for at, (source, target) in enumerate(zip(send_outs, send_any))
    ]
    share = channels * rows // length // parts
    for part in range(parts):
        side_by_side(part * share, (part + 1) * share, group)
        start([one[part] for one in copies])
    for one in copies:
        wait(one)
    wait(departures)


def gate_back(factors, d_out):
    channels = d_out.shape[0]
    d_value = d_out * factors[:channels].astype(F32)
    d_pre = d_out * factors[channels:].astype(F32)
    return jnp.concatenate([d_value.astype(BF16), d_pre.astype(BF16)], axis=0)


def left_back_kernel(
    near_any, other_any, d_product_any, normed1_any, factors_any, d_gate_any, grad_middle, input_w, gating, *refs
):
    d_normed_any, packed, lay, grad, d_normed, sems = refs[:6]
    right_all, d_product, normed1, factors, d_gate, right_sems, product_sems, in_sems = refs[6:]
    rows, length, channels = normed1.shape
    parts = 4
    share = channels // parts
    wide = length // 2
    chip = lax.axis_index("dap") // (lax.axis_size("dap") // 2)
    spans = [pl.ds(pl.multiple_of((chip ^ side) * wide, wide), wide) for side in range(2)]
    first_arrivals = [
        [
            pltpu.make_async_copy(
                ref.at[pl.ds(part * share, share)],
                right_all.at[pl.ds(part * share, share), span, :],
                right_sems.at[side, part],
            )
            for part in range(parts)
        ]
        for side, (ref, span) in enumerate(zip((near_any, other_any), spans))
    ] + [
        split_copies(d_product_any, d_product, product_sems, parts),
    ]
    for part in range(parts):
        start([copies[part] for copies in first_arrivals])
    arrivals = [
        pltpu.make_async_copy(normed1_any, normed1, in_sems.at[0]),
        pltpu.make_async_copy(factors_any, factors, in_sems.at[1]),
        pltpu.make_async_copy(d_gate_any, d_gate, in_sems.at[2]),
    ]
    start(arrivals)

    def channel(c):
        lay[pl.ds(c, rows, stride=channels), :] = mm(
            d_product[pl.ds(c * rows, rows), :], right_all[c]
        )

    for part in range(parts):
        wait([copies[part] for copies in first_arrivals])
        side_by_side(part * share, (part + 1) * share, channel)
    wait(arrivals)
    weight = jnp.concatenate([input_w[:, : 2 * channels], gating[...]], axis=1)
    grad[...] = jnp.zeros_like(grad)

    def row(i):
        normed = normed1[i]
        d_gate_t = d_gate[i].T
        d_projected = gate_back(factors[i], lay[pl.ds(i * channels, channels), :])
        yield
        d_projected = jnp.concatenate([d_projected, d_gate_t], axis=0)
        d_normed[i] = mm(weight, d_projected)
        return d_projected, normed

    def finish(results):
        d_projected, normed = zip(*results)
        grad[...] += mm(jnp.concatenate(d_projected, axis=1), jnp.concatenate(normed, axis=0))

    parts = 4
    departures = split_copies(d_normed, d_normed_any, sems, parts)
    for part in range(parts):
        over_rows(rows // parts, 8, row, finish, first=part * (rows // parts))
        departures[part].start()
    packed[: 3 * channels] = grad[...].astype(BF16)
    packed[3 * channels :] = grad_middle[...].astype(BF16)
    wait(departures)


def right_back_kernel(count, *refs):
    arrived = refs[:count]
    left_halves = refs[count : 2 * count], refs[2 * count : 3 * count]
    refs = refs[count:]
    normed1_any, factors_any, packed_a, packed_b = refs[2 * count : 2 * count + 4]
    d_projected_any = refs[2 * count + 4]
    sends = refs[2 * count + 5 : 3 * count + 5]
    lay, grad, packed, d_projected_out, sems, normed1, factors, in_sems = refs[3 * count + 5 :]
    rows, length, channels = normed1.shape
    arrivals = [
        pltpu.make_async_copy(normed1_any, normed1, in_sems.at[0]),
        pltpu.make_async_copy(factors_any, factors, in_sems.at[1]),
    ]
    start(arrivals)
    per = length // rows
    same = (
        lax.broadcasted_iota(jnp.int32, (length, length), 0) // rows
        == lax.broadcasted_iota(jnp.int32, (length, length), 1) // rows
    )
    mask = same.astype(F32).astype(BF16)

    for left_blocks, first in zip(left_halves, (0, left_halves[0][0].shape[0] // per)):

        def group(g, left_blocks=left_blocks, first=first):
            at = first + g
            spread = jnp.concatenate(
                [jnp.concatenate([ref[at]] * per, axis=0) * mask for ref in arrived], axis=1
            )
            lefts = jnp.concatenate(
                [ref[pl.ds(g * per, per)].reshape(length, length) for ref in left_blocks], axis=0
            )
            lay[pl.ds(at * length, length), :] = mm(spread, lefts)

        side_by_side(0, left_blocks[0].shape[0] // per, group)
    wait(arrivals)
    grad[...] = jnp.zeros_like(grad)

    def row(i):
        normed = normed1[i]
        d_projected = gate_back(factors[i], lay[pl.ds(i, channels, stride=rows), :])
        yield
        d_projected_out[i] = d_projected
        return d_projected, normed

    def finish(results):
        d_projected, normed = zip(*results)
        grad[...] += mm(jnp.concatenate(d_projected, axis=1), jnp.concatenate(normed, axis=0))

    parts = 4
    departures = split_copies(d_projected_out, d_projected_any, sems, parts)
    for part in range(parts):
        over_rows(rows // parts, 8, row, finish, first=part * (rows // parts))
        departures[part].start()
    first, second = packed_a.shape[0], packed_b.shape[0]
    packed[:first] = packed_a[...]
    packed[first : first + second] = packed_b[...]
    packed[first + second : first + second + 2 * channels] = grad[...].astype(BF16)
    packed[first + second + 2 * channels :] = jnp.zeros_like(
        packed[first + second + 2 * channels :]
    )
    size = sends[0].shape[0]
    for offset in range(count):
        begin = pl.multiple_of((lax.axis_index("dap") ^ offset) * size, HEAD_ROWS)
        sends[offset][...] = packed[pl.ds(begin, size), :]
    wait(departures)


def input_back_kernel(part, parts, *refs):
    sources = refs[:4]
    gain_col, input_w = refs[4:6]
    pair_grad_any = refs[-8]
    d_left, d_right, pair, d_middle, pair_grad, sems, out_sem = refs[-7:]
    rows, length, channels = pair.shape
    span = pl.ds(part * rows, rows)
    arrivals = [
        pltpu.make_async_copy(source.at[span], target, sems.at[at])
        for at, (source, target) in enumerate(zip(sources, (d_left, d_right, pair, d_middle)))
    ]
    start(arrivals)
    weight = input_w[:, 2 * channels :]
    gain = jnp.broadcast_to(gain_col[...], (channels, length))

    def row(i):
        hat, scale = norm_parts(pair[i].T.astype(F32), 0)
        d_normed = d_left[i] + mm(weight, d_right[i])
        yield
        d_pair = norm_back(d_normed * gain, hat, scale, 0).astype(BF16).T.astype(F32)
        yield
        pair_grad[i] = (d_middle[i].astype(F32) + d_pair).astype(BF16)

    wait(arrivals)
    over_rows(rows, 8, row)
    departure = pltpu.make_async_copy(pair_grad, pair_grad_any.at[span], out_sem)
    departure.start()
    departure.wait()


def finish_kernel(count, factor, *refs):
    blocks = refs[:count]
    (input1, gating, output1, bias_w, input3, gain1, gain2, gain3) = refs[count : count + 8]
    (
        gain1_out,
        input1_out,
        gating_out,
        gain2_out,
        output1_out,
        gain3_out,
        bias_out,
        input3_out,
        output3_out,
        table_out,
        packed,
    ) = refs[count + 8 :]
    channels = gating.shape[0]
    heads, types = table_out.shape[:2]
    size = blocks[0].shape[0]
    for offset in range(count):
        begin = pl.multiple_of((lax.axis_index("dap") ^ offset) * size, HEAD_ROWS)
        packed[pl.ds(begin, size), :] = blocks[offset][...].astype(F32) * factor
    at = 0

    def take(rows):
        nonlocal at
        at += rows
        return packed[at - rows : at, :]

    input3_t, output3 = take(4 * channels), take(channels)
    table = take(HEAD_ROWS) + take(HEAD_ROWS)
    left_t, gating_t, output1_grad = take(2 * channels), take(channels), take(channels)
    bias_t, right_t = take(HEAD_ROWS), take(2 * channels)
    input1_t = jnp.concatenate([left_t, right_t], axis=0)

    def dots(weight, grad_t):
        return jnp.sum(weight[...].astype(F32).T * grad_t, axis=0, keepdims=True)

    gain1_out[...] = (dots(input1, input1_t) + dots(gating, gating_t)) / gain1[...]
    output_t = (output1[...].astype(F32) * output1_grad).T
    gain2_out[...] = jnp.sum(output_t, axis=0, keepdims=True) / gain2[...]
    gain3_out[...] = (dots(input3, input3_t) + dots(bias_w, bias_t[:heads])) / gain3[...]
    input1_out[...] = input1_t.T
    gating_out[...] = gating_t.T
    output1_out[...] = output1_grad
    bias_out[...] = bias_t[:heads]
    input3_out[...] = input3_t.T
    output3_out[...] = output3
    for h in range(heads):
        table_out[h] = table[:types, h * types : (h + 1) * types]


def swap(value, axis, step):
    count = lax.axis_size(axis)
    return lax.ppermute(value, axis, [(index, index ^ step) for index in range(count)])


def gather_blocks(block, axis):
    return gather_near(block, swap(block, axis, lax.axis_size(axis) // 2), axis)


def gather_near(block, far, axis):
    return near_blocks(block, axis) + near_blocks(far, axis)


def near_blocks(block, axis):
    half = lax.axis_size(axis) // 2
    blocks = {0: block}
    for bit in reversed(range(half.bit_length() - 1)):
        step = 1 << bit
        for offset, held in list(blocks.items()):
            blocks[offset ^ step] = swap(held, axis, step)
    return [blocks[offset] for offset in range(len(blocks))]


def sum_over(value, axis):
    step = 1
    while step < lax.axis_size(axis):
        value = value + swap(value, axis, step)
        step *= 2
    return value


def per_device(
    pair_rep,
    cotangent,
    tok_mask,
    tok_types,
    pair_mask,
    triangle_gain,
    triangle_input,
    triangle_gating,
    product_gain,
    triangle_output,
    attend_gain,
    attend_bias,
    attend_input,
    attend_output,
    type_table,
):
    slab = pair_rep[0]
    cot = cotangent[0]
    rows, length, channels = slab.shape
    heads, types = type_table.shape[:2]
    count = lax.axis_size("dap")
    gain1_row, gain3_row = triangle_gain[None, :], attend_gain[None, :]
    gain1_col, gain2_col, gain3_col = (
        triangle_gain[:, None],
        product_gain[:, None],
        attend_gain[:, None],
    )
    vmem = pl.BlockSpec(memory_space=pltpu.VMEM)
    anywhere = pl.BlockSpec(memory_space=pltpu.HBM)
    smem = pl.BlockSpec(memory_space=pltpu.SMEM)
    cell_buffer = pltpu.VMEM((rows, length, channels), BF16)
    cells = (rows, length, channels)
    turned = (rows, channels, length)

    half = rows // 2
    normed1, right_halves, live_halves = None, [], []
    for part in range(2):
        given = [] if normed1 is None else [normed1]
        normed1, right_part, live_part = call(
            partial(right_kernel, part),
            [
                (cells, BF16),
                ((channels, half, length), BF16),
                ((half, length), F32),
            ],
            [slab, pair_mask[0], tok_mask, gain1_row, triangle_input, *given],
            in_specs=[anywhere] * (5 + len(given)),
            out_specs=[anywhere, vmem, vmem],
            aliases={5: 0} if given else None,
            scratch=[
                pltpu.VMEM((half, length, channels), BF16),
                pltpu.VMEM((half, length), jnp.int32),
                pltpu.VMEM((1, length), jnp.int32),
                pltpu.VMEM((1, channels), F32),
                pltpu.VMEM((channels, 4 * channels), BF16),
                pltpu.VMEM((2 * channels, channels), BF16),
                pltpu.VMEM((channels * half, length), F32),
                pltpu.VMEM((half, length, channels), BF16),
                pltpu.SemaphoreType.DMA((6,)),
            ],
            us=3.0,
            name="right_projection",
        )
        right_halves.append(right_part)
        live_halves.append(live_part)
    low_count = 5 * channels // 16
    left_low, left_high, gate, live, left_factors = call(
        partial(left_kernel, 2),
        [
            ((low_count, rows, length), BF16),
            ((channels - low_count, rows, length), BF16),
            (cells, F32),
            ((rows, length), F32),
            ((rows, 2 * channels, length), BF16),
        ],
        [normed1, *live_halves, triangle_input, triangle_gating],
        in_specs=[anywhere] + [vmem] * 4,
        out_specs=[vmem, vmem, anywhere, vmem, anywhere],
        scratch=[
            pltpu.VMEM((2 * channels, channels), BF16),
            pltpu.VMEM((channels * rows, length), F32),
            pltpu.VMEM(cells, F32),
            pltpu.VMEM((rows, 2 * channels, length), BF16),
            cell_buffer,
            pltpu.SemaphoreType.DMA((2,)),
            pltpu.SemaphoreType.DMA((2, 2)),
        ],
        us=6.0,
        name="left_projection",
    )
    far = [swap(part, "dap", count // 2) for part in right_halves]
    live, far[0] = lax.optimization_barrier((live, far[0]))
    right_factors, d_gated = call(
        partial(factor_kernel, 2),
        [((rows, 2 * channels, length), BF16), (cells, BF16)],
        [live, triangle_input, attend_output, normed1, cot],
        in_specs=[vmem] * 3 + [anywhere] * 2,
        out_specs=[anywhere] * 2,
        scratch=[
            cell_buffer,
            cell_buffer,
            pltpu.VMEM((rows, 2 * channels, length), BF16),
            cell_buffer,
            pltpu.SemaphoreType.DMA((2, 2)),
            pltpu.SemaphoreType.DMA((2, 2)),
        ],
        us=5.0,
        name="right_factors",
    )
    lines, wide = rows // 2, length // 2

    def product_side(side, halves, given=()):
        blocks = [halves[index % 2][index // 2] for index in range(count)]
        return call(
            partial(product_kernel, count, side),
            [
                ((2, lines, channels, length), BF16),
                (cells, BF16),
                (cells, BF16),
                (cells, BF16),
                ((channels, wide, length), BF16),
                ((lines, length), F32),
                ((rows, heads * length), BF16) if side else ((lines * HEAD_ROWS, length), F32),
            ],
            [*blocks, left_low, left_high, slab, gate, gain2_col, gain3_row]
            + [triangle_output, attend_bias, *given],
            in_specs=[vmem] * (count + 2)
            + [anywhere] * 2
            + [vmem] * 4
            + [anywhere] * (5 if side else 0),
            out_specs=[anywhere] * 5 + [vmem, vmem if side else anywhere],
            scratch=[
                pltpu.VMEM((lines * channels, length), F32),
                pltpu.VMEM((lines * HEAD_ROWS, length), F32),
                pltpu.VMEM((channels, wide, length), BF16),
                pltpu.VMEM((rows, wide, channels), BF16),
                pltpu.VMEM((rows, wide, channels), F32),
                pltpu.VMEM((lines, channels, length), BF16),
            ]
            + [pltpu.VMEM((rows, wide, channels), BF16)] * 3
            + [
                pltpu.SemaphoreType.DMA((2,)),
                pltpu.SemaphoreType.DMA((4, 4)),
                pltpu.SemaphoreType.DMA,
                pltpu.SemaphoreType.DMA,
                pltpu.VMEM((lines * HEAD_ROWS, length), F32),
            ],
            aliases={count + 9 + at: at for at in range(4)} if side else None,
            us=7.0,
            name="product_other" if side else "product_near",
        )

    *shared, right_near, scale2_near, bias_near = product_side(
        0, [near_blocks(part, "dap") for part in right_halves]
    )
    shared[0], d_gated, far[1] = lax.optimization_barrier((shared[0], d_gated, far[1]))
    left_low_sent, _ = lax.optimization_barrier((left_low, far[1]))
    low_far = swap(left_low_sent, "dap", count // 2)
    *shared, right_other, scale2_other, bias_rows = product_side(
        1, [near_blocks(part, "dap") for part in far], [bias_near, *shared]
    )
    normed2, update, middle, normed3 = shared
    right_sides = [right_near, right_other]
    normed3, low_far = lax.optimization_barrier((normed3, low_far))
    bias_blocks = [bias_rows] + [
        swap(bias_rows, "dap", offset) for offset in reversed(range(1, count))
    ][::-1]

    block = 8
    steps = rows // block
    by_row = pl.BlockSpec((block, length, channels), lambda step: (step, 0, 0))
    by_row_wide = pl.BlockSpec((block, 4 * channels, length), lambda step: (step, 0, 0))

    def fixed(*shape):
        return pl.BlockSpec(shape, lambda step: (0,) * len(shape))

    projected3, query, gate3 = call(
        partial(project_kernel, (channels // heads) ** -0.5),
        [((rows, 3 * channels, length), BF16), (cells, BF16), (cells, F32)],
        [normed3, attend_input],
        in_specs=[anywhere] * 2,
        scratch=[
            cell_buffer,
            pltpu.VMEM((channels, 4 * channels), BF16),
            pltpu.VMEM((3 * channels, channels), BF16),
            pltpu.VMEM((channels, 2 * channels), BF16),
            pltpu.VMEM((rows, 3 * channels, length), BF16),
            cell_buffer,
            pltpu.VMEM(cells, F32),
            pltpu.SemaphoreType.DMA((4,)),
            pltpu.SemaphoreType.DMA((3, 4)),
            pltpu.SemaphoreType.DMA,
        ],
        out_specs=[anywhere] * 3,
        us=5.0,
        name="attention_projections",
    )
    projected3, *bias_blocks = lax.optimization_barrier((projected3, *bias_blocks))
    left_high_sent, _ = lax.optimization_barrier((left_high, bias_blocks[-1]))
    high_far = swap(left_high_sent, "dap", count // 2)
    attend_outs = call(
        partial(attend_kernel, count),
        [
            (cells, BF16),
            ((rows, 4 * channels, length), BF16),
            ((channels, channels), F32),
            ((HEAD_ROWS, channels), F32),
            ((rows, heads * length), F32),
        ]
        + [((rows, heads * length), BF16)] * (count - 1),
        [type_table.reshape(heads * types, types), *bias_blocks]
        + [tok_types, tok_types.reshape(length, 1), live, attend_output]
        + [projected3, query, gate3, d_gated, cot, middle],
        in_specs=[smem] + [vmem] * (count + 4) + [anywhere] * 6,
        out_specs=[anywhere] + [vmem] * (count + 3),
        scratch=[
            pltpu.VMEM((length, heads * length), F32),
            pltpu.VMEM((length, heads * length), F32),
            pltpu.VMEM((channels, heads * length), BF16),
        ]
        + [pltpu.VMEM((rows, 3 * channels, length), BF16), cell_buffer, pltpu.VMEM(cells, F32)]
        + [cell_buffer] * 4
        + [
            pltpu.SemaphoreType.DMA((6, rows // W_ATTEND)),
            pltpu.SemaphoreType.DMA((rows // W_ATTEND,)),
        ],
        us=20.0,
        name="attention",
    )
    pair_out, d_projected3, d_output, d_table = attend_outs[:4]
    d_bias_parts = [attend_outs[4]] + [
        swap(attend_outs[4 + offset], "dap", offset) for offset in range(1, count)
    ]
    d_bias_parts[1], high_far = lax.optimization_barrier((d_bias_parts[1], high_far))
    d_normed3, packed_a = call(
        projection_kernel,
        [(turned, F32), ((4 * channels + channels + 2 * HEAD_ROWS, channels), BF16)],
        [d_projected3, normed3, attend_input, d_output, d_table],
        grid=(steps,),
        in_specs=[by_row_wide, by_row, fixed(channels, 4 * channels)]
        + [fixed(channels, channels), fixed(HEAD_ROWS, channels)],
        out_specs=[
            pl.BlockSpec((block, channels, length), lambda step: (step, 0, 0)),
            fixed(5 * channels + 2 * HEAD_ROWS, channels),
        ],
        scratch=[pltpu.VMEM((4 * channels, channels), F32)],
        us=0.5,
        name="projection_back",
    )
    groups = channels * rows // length
    middle_outs = call(
        partial(middle_kernel, count),
        [
            (cells, BF16),
            (cells, BF16),
            ((channels * rows, length), BF16),
            ((channels + HEAD_ROWS, channels), F32),
        ]
        + [((groups, rows, length), BF16)] * count,
        [*d_bias_parts, d_normed3, normed3, middle, cot, gain3_col, attend_bias]
        + [normed2, scale2_near, scale2_other, update, gate, gain2_col, triangle_output],
        out_specs=[anywhere] * 3 + [vmem] + [anywhere] * count,
        scratch=[
            pltpu.VMEM((rows * HEAD_ROWS, length), F32),
            pltpu.VMEM((channels * rows, length), F32),
            cell_buffer,
            cell_buffer,
            pltpu.VMEM((channels * rows, length), BF16),
        ]
        + [pltpu.VMEM((groups, rows, length), BF16)] * count
        + [
            pltpu.SemaphoreType.DMA((2,)),
            pltpu.SemaphoreType.DMA((4,)),
            pltpu.SemaphoreType.DMA((count, 4)),
        ],
        us=12.0,
        name="middle_back",
    )
    d_middle, d_gate, d_product, grad_middle = middle_outs[:4]
    d_middle, low_far, high_far = lax.optimization_barrier((d_middle, low_far, high_far))
    left_blocks = gather_near(left_low, low_far, "dap") + gather_near(left_high, high_far, "dap")
    product_parts = [middle_outs[4]] + [
        swap(middle_outs[4 + offset], "dap", offset) for offset in range(1, count)
    ]
    d_left, packed_b = call(
        left_back_kernel,
        [(turned, F32), ((4 * channels + HEAD_ROWS, channels), BF16)],
        [*right_sides, d_product, normed1, left_factors, d_gate, grad_middle]
        + [triangle_input, triangle_gating],
        scratch=[
            pltpu.VMEM((rows * channels, length), F32),
            pltpu.VMEM((3 * channels, channels), F32),
            pltpu.VMEM(turned, F32),
            pltpu.SemaphoreType.DMA((4,)),
            pltpu.VMEM((channels, length, length), BF16),
            pltpu.VMEM((channels * rows, length), BF16),
            cell_buffer,
            pltpu.VMEM((rows, 2 * channels, length), BF16),
            cell_buffer,
            pltpu.SemaphoreType.DMA((2, 4)),
            pltpu.SemaphoreType.DMA((4,)),
            pltpu.SemaphoreType.DMA((3,)),
        ],
        in_specs=[anywhere] * 6 + [vmem] * 3,
        out_specs=[anywhere, vmem],
        us=10.0,
        name="left_back",
    )
    used = packed_a.shape[0] + packed_b.shape[0] + 2 * channels
    share = -(-used // (count * HEAD_ROWS)) * HEAD_ROWS
    right_outs = call(
        partial(right_back_kernel, count),
        [((rows, 2 * channels, length), BF16)] + [((share, channels), BF16)] * count,
        [*product_parts, *left_blocks, normed1, right_factors, packed_a, packed_b],
        in_specs=[vmem] * (3 * count) + [anywhere] * 2 + [vmem] * 2,
        out_specs=[anywhere] + [vmem] * count,
        scratch=[
            pltpu.VMEM((channels * rows, length), F32),
            pltpu.VMEM((2 * channels, channels), F32),
            pltpu.VMEM((share * count, channels), BF16),
            pltpu.VMEM((rows, 2 * channels, length), BF16),
            pltpu.SemaphoreType.DMA((4,)),
            cell_buffer,
            pltpu.VMEM((rows, 2 * channels, length), BF16),
            pltpu.SemaphoreType.DMA((2,)),
        ],
        us=7.0,
        name="right_back",
    )
    d_right = right_outs[0]
    parts = 4
    some = (rows // parts, length, channels)
    pair_grad = None

    def input_back(part, pair_grad):
        given = [] if pair_grad is None else [pair_grad]
        (pair_grad,) = call(
            partial(input_back_kernel, part, parts),
            [(cells, BF16)],
            [d_left, d_right, slab, d_middle, gain1_col, triangle_input, *given],
            in_specs=[anywhere] * 4 + [vmem] * 2 + [anywhere] * len(given),
            out_specs=[anywhere],
            scratch=[
                pltpu.VMEM((rows // parts, channels, length), F32),
                pltpu.VMEM((rows // parts, 2 * channels, length), BF16),
                pltpu.VMEM(some, BF16),
                pltpu.VMEM(some, BF16),
                pltpu.VMEM(some, BF16),
                pltpu.SemaphoreType.DMA((4,)),
                pltpu.SemaphoreType.DMA,
            ],
            aliases={6: 0} if given else None,
            us=3.0,
            name="input_back",
        )
        return pair_grad

    shares = dict(enumerate(right_outs[1:]))
    step = 1
    done = 0
    while step < count:
        if 2 * step == count:
            pair_grad = input_back(done, pair_grad)
            done += 1
        for offset in [one for one in shares if one & step]:
            arrived = swap(shares.pop(offset), "dap", step)
            shares[offset ^ step] = shares[offset ^ step] + arrived
        step *= 2
    grad_share, pair_grad = lax.optimization_barrier((shares[0], pair_grad))
    step = 1
    while step < lax.axis_size("dp"):
        if step > 1 and done < parts - 1:
            pair_grad = input_back(done, pair_grad)
            grad_share, pair_grad = lax.optimization_barrier((grad_share, pair_grad))
            done += 1
        grad_share = grad_share + swap(grad_share, "dp", step)
        step *= 2
    grad_far = swap(grad_share, "dap", count // 2)
    while done < parts:
        pair_grad = input_back(done, pair_grad)
        done += 1
    pair_grad, grad_far = lax.optimization_barrier((pair_grad, grad_far))
    grad_blocks = gather_near(grad_share, grad_far, "dap")
    weights = (triangle_input, triangle_gating, triangle_output, attend_bias, attend_input)
    gains = (gain1_row, product_gain[None, :], gain3_row)
    grads = call(
        partial(finish_kernel, count, (length * length * lax.axis_size("dp")) ** (-0.5)),
        [
            ((1, channels), F32),
            (triangle_input.shape, F32),
            (triangle_gating.shape, F32),
            ((1, channels), F32),
            (triangle_output.shape, F32),
            ((1, channels), F32),
            (attend_bias.shape[::-1], F32),
            (attend_input.shape, F32),
            (attend_output.shape, F32),
            (type_table.shape, F32),
        ],
        [*grad_blocks, *weights, *gains],
        scratch=[pltpu.VMEM((share * count, channels), F32)],
        us=3.0,
        name="scale_gradients",
    )
    grads = [grad[0] if grad.shape[0] == 1 else grad for grad in grads]
    grads[6] = grads[6].T
    return (pair_out[None], pair_grad[None], *grads)


def solution(mesh):
    return jax.shard_map(
        per_device,
        mesh=mesh,
        in_specs=(
            P("dp", "dap", None, None),
            P("dp", "dap", None, None),
            P("dp", None),
            P("dp", None),
            P("dp", "dap", None),
        )
        + (P(),) * 10,
        out_specs=(
            P("dp", "dap", None, None),
            P("dp", "dap", None, None),
        )
        + (P(),) * 10,
        check_vma=False,
    )
```

```python
import math
from functools import partial

import jax
import jax.numpy as jnp
from jax import lax
from jax.experimental import pallas as pl
from jax.experimental.pallas import tpu as pltpu
from jax.sharding import PartitionSpec as P

EPSILON = 1e-05
F32 = jnp.float32
BF16 = jnp.bfloat16
VMEM_MARGIN = 4 * 1024 * 1024
W_PRODUCT, W_ATTEND, W_MIDDLE = 8, 4, 8
LOG2_E = math.log2(math.e)
HEAD_ROWS = 16


def mm(left, right):
    return lax.dot_general(left, right, (((1,), (0,)), ((), ())), preferred_element_type=F32)


def mmt(left, right):
    return lax.dot_general(left, right, (((1,), (1,)), ((), ())), preferred_element_type=F32)


def sigmoid(value):
    return 0.5 + 0.5 * jnp.tanh(0.5 * value)


def norm_parts(values, axis):
    centred = values - jnp.mean(values, axis=axis, keepdims=True)
    spread = jnp.mean(centred * centred, axis=axis, keepdims=True)
    scale = lax.rsqrt(spread + EPSILON)
    return centred * scale, scale


def norm_back(d_hat, hat, scale, axis):
    first = jnp.mean(d_hat, axis=axis, keepdims=True)
    second = jnp.mean(d_hat * hat, axis=axis, keepdims=True)
    return scale * (d_hat - first - hat * second)


def lockstep(row, indices):
    going = [row(index) for index in indices]
    results = [None] * len(going)
    running = True
    while running:
        for at, one in enumerate(going):
            try:
                next(one)
            except StopIteration as stop:
                results[at] = stop.value
                running = False
    return results


def over_rows(count, width, row, finish=None, first=0):
    def some(index, carry):
        results = lockstep(row, [first + index * width + at for at in range(width)])
        if finish is not None:
            finish(results)
        return carry

    lax.fori_loop(0, count // width, some, 0)


def side_by_side(first, last, body, most=16):
    unroll = max(one for one in range(1, most + 1) if (last - first) % one == 0)
    lax.fori_loop(first, last, lambda index, carry: body(index), None, unroll=unroll)


def split_copies(source, target, sems, parts):
    size = source.shape[0] // parts
    return [
        pltpu.make_async_copy(
            source.at[pl.ds(part * size, size)], target.at[pl.ds(part * size, size)], sems.at[part]
        )
        for part in range(parts)
    ]


def start(copies):
    for copy in copies:
        copy.start()


def wait(copies):
    for copy in copies:
        copy.wait()


def call(kernel, outs, args, scratch=(), grid=(), in_specs=None, out_specs=None, us=5.0, name=None, aliases=None):
    whole = pl.BlockSpec(memory_space=pltpu.VMEM)
    in_specs = in_specs or [whole] * len(args)
    out_specs = out_specs or [whole] * len(outs)
    held = sum(
        math.prod(one.shape) * jnp.dtype(one.dtype).itemsize
        for one in scratch
        if getattr(one, "memory_space", None) == pltpu.VMEM
    )
    args = [
        pltpu.with_memory_space_constraint(arg, pltpu.HBM)
        if spec.memory_space == pltpu.HBM
        else arg
        for arg, spec in zip(args, in_specs)
    ]
    return pl.pallas_call(
        kernel,
        out_shape=[
            pltpu.HBM(shape, dtype)
            if spec.memory_space == pltpu.HBM
            else jax.ShapeDtypeStruct(shape, dtype)
            for (shape, dtype), spec in zip(outs, out_specs)
        ],
        grid=grid,
        in_specs=in_specs,
        out_specs=out_specs,
        scratch_shapes=list(scratch),
        compiler_params=pltpu.CompilerParams(vmem_limit_bytes=held + VMEM_MARGIN),
        cost_estimate=pl.CostEstimate(
            flops=int(us * 1.0e9), bytes_accessed=int(us * 3.0e6), transcendentals=0
        ),
        input_output_aliases=aliases or {},
        name=name,
    )(*args)


def right_kernel(part, pair_any, mask_any, tokens_any, gain_any, weight_any, *refs):
    normed_any, right_out, live_out = refs[-12:-9]
    pair, mask, tokens, gain, weight, weight_t, lay, normed_out, sems = refs[-9:]
    rows, length, channels = pair.shape
    place = lax.axis_index("dap")
    span = pl.ds(part * rows, rows)
    sources = [mask_any.at[span], tokens_any, gain_any, weight_any, pair_any.at[span]]
    copies = [
        pltpu.make_async_copy(source, target, sems.at[at])
        for at, (source, target) in enumerate(zip(sources, (mask, tokens, gain, weight, pair)))
    ]
    start(copies)
    wait(copies)
    first = place * (mask_any.shape[0]) + part * rows
    lines = lax.broadcasted_iota(jnp.int32, (rows, length), 0) + first
    lanes = lax.broadcasted_iota(jnp.int32, (rows, length), 1)
    wide = tokens[...].astype(F32)
    own = jnp.sum(jnp.where(lines == lanes, wide, 0.0), axis=1, keepdims=True)
    live_out[...] = mask[...].astype(F32) * own * wide
    weight_t[...] = weight[:, 2 * channels : 4 * channels].astype(F32).T.astype(BF16)

    def row(i):
        hat, _ = norm_parts(pair[i].astype(F32), -1)
        yield
        normed = (hat * gain[...]).astype(BF16)
        normed_out[i] = normed
        projected = mmt(weight_t[...], normed)
        yield
        right = sigmoid(projected[channels:]) * projected[:channels] * live_out[pl.ds(i, 1), :]
        lay[pl.ds(i, channels, stride=rows), :] = right

    over_rows(rows, 8, row)
    departure = pltpu.make_async_copy(normed_out, normed_any.at[span], sems.at[5])
    departure.start()
    right_out[...] = lay[...].reshape(channels, rows, length).astype(BF16)
    departure.wait()


def gate_factors(projected, live_row, channels):
    value, pre = projected[:channels], projected[channels:]
    gate = sigmoid(pre)
    slope = gate * live_row
    out = slope * value
    factors = jnp.concatenate([slope.astype(BF16), (out * (1.0 - gate)).astype(BF16)], axis=0)
    return out, factors


def left_kernel(parts, normed_any, *refs):
    live_parts = refs[:parts]
    weight, gating = refs[parts : parts + 2]
    high_out, gate_any, live, factor_any, low_any = refs[parts + 2 : parts + 7]
    weight_t, lay, gates, factors, normed1, in_sems, sems, low_sem, low_out = refs[parts + 7 :]
    arrivals = split_copies(normed_any, normed1, in_sems, parts)
    start(arrivals)
    rows, length, channels = gates.shape
    half = rows // parts
    weight_t[...] = weight[:, : 2 * channels].astype(F32).T.astype(BF16)
    outs = []
    for part in range(parts):
        span = pl.ds(part * half, half)
        live[span, :] = live_parts[part][...]
        arrivals[part].wait()

        def row(i, part=part):
            at = i + part * half
            normed = normed1[at]
            projected = mmt(weight_t[...], normed)
            gate = mm(normed, gating[...])
            yield
            left, factors[at] = gate_factors(projected, live[pl.ds(at, 1), :], channels)
            lay[pl.ds(at, channels, stride=rows), :] = left
            gates[at] = sigmoid(gate)

        over_rows(half, 8, row)
        for index, (source, target) in enumerate(((gates, gate_any), (factors, factor_any))):
            copy = pltpu.make_async_copy(
                source.at[span], target.at[span], sems.at[index, part]
            )
            copy.start()
            outs.append(copy)
    left = lay[...].reshape(channels, rows, length).astype(BF16)
    low = low_out.shape[0]
    low_out[...] = left[:low]
    copy = pltpu.make_async_copy(low_out, low_any, low_sem)
    copy.start()
    outs.append(copy)
    high_out[...] = left[low:]
    wait(outs)


def factor_kernel(parts, *refs):
    live, weight, output_w, normed_any, cotangent_any, factor_any, d_gated_any = refs[:7]
    normed1, cotangent, factors, d_gated, in_sems, sems = refs[7:]
    rows, length, channels = cotangent.shape
    half = rows // parts
    arrivals = [
        split_copies(normed_any, normed1, in_sems.at[0], parts),
        split_copies(cotangent_any, cotangent, in_sems.at[1], parts),
    ]
    for copies in arrivals:
        start(copies)
    weight_t = weight[:, 2 * channels : 4 * channels].astype(F32).T.astype(BF16)
    departures = [
        split_copies(factors, factor_any, sems.at[0], parts),
        split_copies(d_gated, d_gated_any, sems.at[1], parts),
    ]
    for part in range(parts):
        wait([copies[part] for copies in arrivals])

        def row(i, part=part):
            at = i + part * half
            projected = mmt(weight_t, normed1[at])
            back = mmt(cotangent[at], output_w[...])
            yield
            _, factors[at] = gate_factors(projected, live[pl.ds(at, 1), :], channels)
            d_gated[at] = back.astype(BF16)

        over_rows(half, 8, row)
        start([copies[part] for copies in departures])
    for copies in departures:
        wait(copies)


def product_kernel(count, side, *refs):
    near = count // 2
    blocks = refs[: 2 * near]
    low_any, high = refs[2 * near : 2 * near + 2]
    (pair_any, gate_any, gain2_col, gain3, output_w, bias_w) = refs[2 * near + 2 : 2 * near + 8]
    rest = refs[2 * near + 8 :]
    if side:
        bias_any, rest = rest[0], rest[5:]
    row_outs = rest[:4]
    right_any, scale2_out, bias_out, product, bias_scr, right_side, pair, gate = rest[4:12]
    kept = rest[12:16]
    normed2_out, update_out, middle_out, normed3_out = kept
    in_sems, out_sems, right_sem, bias_sem, bias_near, low = rest[16:]
    rows, wide, channels = pair.shape
    length = 2 * wide
    lines = rows // 2
    heads = bias_w.shape[1]
    place = lax.axis_index("dap")
    chip = place // near
    span = pl.ds(pl.multiple_of((chip ^ side) * wide, wide), wide)
    low_copy = pltpu.make_async_copy(low_any, low, in_sems.at[2])
    low_copy.start()
    arrivals = [
        pltpu.make_async_copy(pair_any.at[:, span, :], pair, in_sems.at[0]),
        pltpu.make_async_copy(gate_any.at[:, span, :], gate, in_sems.at[1]),
    ]
    start(arrivals)
    if side:
        bias_copy = pltpu.make_async_copy(bias_any, bias_near, bias_sem)
        bias_copy.start()
    size = blocks[0].shape[1]
    starts = [
        pl.multiple_of(((place ^ (index // 2)) % near) * rows + (index % 2) * size, size)
        for index in range(2 * near)
    ]

    def channel(c):
        for begin, ref in zip(starts, blocks):
            right_side[c, pl.ds(begin, size), :] = ref[c]

    side_by_side(0, channels, channel)
    right_copy = pltpu.make_async_copy(right_side, right_any, right_sem)
    right_copy.start()
    for left, first in ((high, low.shape[0]), (low, 0)):
        if first == 0:
            low_copy.wait()

        def multiply(pair_of, left=left, first=first):
            c = 2 * pair_of
            cells = mmt(
                left[pl.ds(c, 2)].reshape(2 * rows, length),
                right_side[pl.ds(first + c, 2)].reshape(length, length),
            )
            for one in range(2):
                mine = cells[one * rows : (one + 1) * rows, one * wide : (one + 1) * wide]
                product[pl.ds(first + c + one, lines, stride=channels), :] = jnp.concatenate(
                    [mine[:lines], mine[lines:]], axis=1
                )

        side_by_side(0, left.shape[0] // 2, multiply)
    gain2 = jnp.broadcast_to(gain2_col[...], (channels, length))
    bias_t = jnp.concatenate(
        [bias_w[...].astype(F32).T, jnp.zeros((HEAD_ROWS - heads, channels), F32)], axis=0
    ).astype(BF16)

    def tile(p):
        hat, scale = norm_parts(product[pl.ds(p * channels, channels), :], 0)
        yield
        normed2_t = (hat * gain2).astype(BF16)
        normed2_out[p] = normed2_t
        scale2_out[pl.ds(p, 1), :] = scale
        normed2 = normed2_t.T
        yield
        update = mm(normed2, output_w[...])
        yield
        update_b = update.astype(BF16)
        gates = jnp.concatenate([gate[p], gate[p + lines]], axis=0)
        pairs = jnp.concatenate([pair[p], pair[p + lines]], axis=0)
        middle = (pairs.astype(F32) + gates * update).astype(BF16)
        hat3, _ = norm_parts(middle.astype(F32), -1)
        yield
        normed3 = (hat3 * gain3[...]).astype(BF16)
        bias_scr[pl.ds(p * HEAD_ROWS, HEAD_ROWS), :] = mmt(bias_t, normed3)
        for out, value in ((update_out, update_b), (middle_out, middle), (normed3_out, normed3)):
            out[p] = value[:wide]
            out[p + lines] = value[wide:]

    wait(arrivals)
    parts = 2
    run = lines // parts
    departures = []
    for part in range(parts):
        over_rows(run, W_PRODUCT, tile, first=part * run)
        some = pl.ds(part * run, run)
        copies = [
            pltpu.make_async_copy(
                normed2_out.at[some], row_outs[0].at[side, some], out_sems.at[0, part]
            )
        ]
        for at in range(1, 4):
            for group in range(2):
                some = pl.ds(group * lines + part * run, run)
                copies.append(
                    pltpu.make_async_copy(
                        kept[at].at[some],
                        row_outs[at].at[some, span, :],
                        out_sems.at[at, 2 * part + group],
                    )
                )
        start(copies)
        departures += copies
    if not side:
        copy = pltpu.make_async_copy(bias_scr, bias_out, bias_sem)
        copy.start()
        departures.append(copy)
    else:
        bias_copy.wait()
        for h in range(heads):
            mine = bias_near[pl.ds(h, lines, stride=HEAD_ROWS), :]
            other = bias_scr[pl.ds(h, lines, stride=HEAD_ROWS), :]
            first = jnp.where(chip == 0, mine, other)
            second = jnp.where(chip == 0, other, mine)
            head = slice(h * length, (h + 1) * length)
            low = jnp.concatenate([first[:, :wide], second[:, :wide]], axis=1)
            high = jnp.concatenate([first[:, wide:], second[:, wide:]], axis=1)
            bias_out[:lines, head] = low.astype(BF16)
            bias_out[lines:, head] = high.astype(BF16)
    wait(departures)
    right_copy.wait()


def project_kernel(factor, normed3_any, weight_any, projected_any, query_any, gate_any, *scratch):
    normed3, weight, weight_t, weight_qg, projected3, queries, gates, sems, out_sems, weight_sem = (
        scratch
    )
    rows, length, channels = normed3.shape
    kept = projected3.shape[1]
    parts = 4
    copy = pltpu.make_async_copy(weight_any, weight, weight_sem)
    copy.start()
    arrivals = split_copies(normed3_any, normed3, sems, parts)
    start(arrivals)
    copy.wait()
    weight_t[...] = weight[:, :kept].astype(F32).T.astype(BF16)
    weight_qg[:, :channels] = weight[:, :channels]
    weight_qg[:, channels:] = weight[:, kept:]

    def row(i):
        normed = normed3[i]
        projected_t = mmt(weight_t[...], normed)
        projected = mm(normed, weight_qg[...])
        yield
        projected3[i, :channels] = (projected_t[:channels] * factor).astype(BF16)
        projected3[i, channels:] = projected_t[channels:].astype(BF16)
        queries[i] = (projected[:, :channels] * (factor * LOG2_E)).astype(BF16)
        gates[i] = sigmoid(projected[:, channels:])

    departures = [
        split_copies(source, target, out_sems.at[at], parts)
        for at, (source, target) in enumerate(
            ((projected3, projected_any), (queries, query_any), (gates, gate_any))
        )
    ]
    for part in range(parts):
        arrivals[part].wait()
        over_rows(rows // parts, 8, row, first=part * (rows // parts))
        start([copies[part] for copies in departures])
    for copies in departures:
        wait(copies)


def attend_kernel(count, table, *refs):
    bias_refs = refs[:count]
    types_row, types_col, live = refs[count : count + 3]
    row_arrays = refs[count + 3 : count + 7]
    gated_any, d_projected, d_table = refs[count + 7 : count + 10]
    d_bias_outs = refs[count + 10 : 2 * count + 10]
    bias, d_bias, head_mask = refs[2 * count + 10 : 2 * count + 13]
    fetched = refs[2 * count + 13 : 2 * count + 17]
    projected, queries, gates, d_gateds = fetched
    gated_all, in_sems, out_sems = refs[2 * count + 17 :]
    rows, length, channels = queries.shape
    types = table.shape[1]
    heads = table.shape[0] // types
    size = channels // heads
    own = bias_refs[0].shape[0]
    factor = size ** -0.5
    place = lax.axis_index("dap")
    parts = rows // W_ATTEND
    arrivals = [
        split_copies(source, target, in_sems.at[at], parts)
        for at, (source, target) in enumerate(zip(row_arrays, fetched))
    ]
    for part in range(parts):
        start([copies[part] for copies in arrivals])

    def spans(h):
        return slice(h * length, (h + 1) * length)

    for offset in range(count):
        begin = pl.multiple_of((place ^ offset) * own, own)
        bias[pl.ds(begin, own), :] = bias_refs[offset][...].astype(F32)
    row_types = types_row[...]
    col_types = types_col[...]
    for h in range(heads):
        total = jnp.zeros((length, length), F32)
        for a in range(types):
            values = jnp.zeros((1, length), F32)
            for b in range(types):
                values = jnp.where(row_types == b, table[h * types + a, b], values)
            total = jnp.where(col_types == a, values, total)
        bias[:, spans(h)] = (bias[:, spans(h)] + total) * LOG2_E
    d_bias[...] = jnp.zeros_like(d_bias)
    lines = lax.broadcasted_iota(jnp.int32, head_mask.shape, 0) // size
    columns = lax.broadcasted_iota(jnp.int32, head_mask.shape, 1) // length
    head_mask[...] = (lines == columns).astype(F32).astype(BF16)


    def row(i):
        live_row = live[pl.ds(i, 1), :]
        live_wide = jnp.concatenate([live_row.astype(BF16)] * heads, axis=1)
        query_t = projected[i, :channels]
        key_t = projected[i, channels : 2 * channels]
        value_t = projected[i, 2 * channels :]
        gate = gates[i]
        d_gated = d_gateds[i].astype(F32)
        mask = head_mask[...]
        ones = mask * live_wide
        keys = jnp.concatenate([key_t] * heads, axis=1) * mask
        values = jnp.concatenate(
            [jnp.concatenate([value_t] * heads, axis=1) * ones, ones], axis=0
        )
        score = mm(queries[i], keys)
        yield
        expo = jnp.exp2(score + bias[...])
        expo_b = expo.astype(BF16)
        sums = mmt(expo_b, values)
        yield
        total = sums[:, channels:]
        inverse = 1.0 / jnp.maximum(total, 1.0)
        attended = sums[:, :channels] * inverse
        gated_all[i] = (gate * attended).astype(BF16)
        d_attended = d_gated * gate * inverse
        d_gate = d_gated * attended * gate * (1.0 - gate)
        slope = jnp.where(total > 1.0, 1.0, jnp.where(total == 1.0, 0.5, 0.0))
        d_attended_b = d_attended.astype(BF16)
        both = jnp.concatenate(
            [d_attended_b, (-d_attended * attended * slope).astype(BF16)], axis=1
        )
        d_expo = mm(both, values)
        turned = jnp.concatenate([d_attended_b.T, d_gate.astype(BF16).T], axis=1)
        yield
        d_score = expo * d_expo
        d_score_b = d_score.astype(BF16)
        d_query_t = mmt(keys, d_score_b) * factor
        d_key_t = mm(query_t, d_score_b)
        d_value_t = mm(turned[:, :length], expo_b)
        yield

        def diagonal(full):
            return jnp.concatenate(
                [full[h * size : (h + 1) * size, spans(h)] for h in range(heads)], axis=0
            )

        d_projected[i, :channels] = d_query_t.astype(BF16)
        d_projected[i, channels : 2 * channels] = diagonal(d_key_t).astype(BF16)
        d_projected[i, 2 * channels : 3 * channels] = (diagonal(d_value_t) * live_row).astype(BF16)
        d_projected[i, 3 * channels :] = turned[:, length:]
        return d_score

    def finish(results):
        d_bias[...] += sum(results)

    departures = split_copies(gated_all, gated_any, out_sems, parts)
    for part in range(parts):
        wait([copies[part] for copies in arrivals])
        over_rows(rows // parts, W_ATTEND, row, finish, first=part * (rows // parts))
        departures[part].start()

    for offset in range(count):
        begin = pl.multiple_of((place ^ offset) * own, own)
        ref = d_bias_outs[offset]
        ref[...] = d_bias[pl.ds(begin, own), :].astype(ref.dtype)
    high = d_bias[...].astype(BF16)
    low = (d_bias[...] - high.astype(F32)).astype(BF16)
    kinds = lax.broadcasted_iota(jnp.int32, (HEAD_ROWS, length), 0)
    picks = (types_row[...] == kinds).astype(F32).astype(BF16)
    by_row = mm(picks, high) + mm(picks, low)
    lanes = lax.broadcasted_iota(jnp.int32, (HEAD_ROWS, channels), 1)
    grad = jnp.zeros((HEAD_ROWS, channels), F32)
    for h in range(heads):
        part = by_row[:, spans(h)]
        for b in range(types):
            one = jnp.sum(jnp.where(types_row[...] == b, part, 0.0), axis=1, keepdims=True)
            grad = jnp.where(lanes == h * types + b, one, grad)
    d_table[...] = grad
    wait(departures)


def output_kernel(gated_any, middle_any, cotangent_any, output_w, pair_out_any, d_output, *scratch):
    gated, middle, cotangent, pair_out, in_sems, out_sems = scratch
    rows, length, channels = gated.shape
    parts = 4
    arrivals = [
        split_copies(source, target, in_sems.at[at], parts)
        for at, (source, target) in enumerate(
            ((gated_any, gated), (cotangent_any, cotangent), (middle_any, middle))
        )
    ]
    for part in range(parts):
        start([copies[part] for copies in arrivals])
    departures = split_copies(pair_out, pair_out_any, out_sems, parts)
    d_output[...] = jnp.zeros_like(d_output)
    size = rows // parts
    for part in range(parts):
        wait([copies[part] for copies in arrivals])
        some = pl.ds(part * size, size)
        flat = gated[some].reshape(size * length, channels)
        update = mm(flat, output_w[...]).reshape(size, length, channels)
        pair_out[some] = (middle[some].astype(F32) + update).astype(BF16)
        departures[part].start()
        d_output[...] += mm(flat.T, cotangent[some].reshape(size * length, channels))
    wait(departures)


def projection_kernel(d_projected, normed3, input_w, d_table, d_normed, packed, total):
    block = normed3.shape[0]
    wide, length = d_projected.shape[1:]
    channels = normed3.shape[2]
    step = pl.program_id(0)

    @pl.when(step == 0)
    def _():
        total[...] = jnp.zeros_like(total)

    def rows(index, carry):
        at = [4 * index + one for one in range(4)]
        both = jnp.concatenate([d_projected[one] for one in at], axis=1)
        total[...] += mm(both, jnp.concatenate([normed3[one] for one in at], axis=0))
        d_both = mm(input_w[...], both)
        for order, one in enumerate(at):
            d_normed[one] = d_both[:, order * length : (order + 1) * length]
        return carry

    lax.fori_loop(0, block // 4, rows, 0, unroll=2)

    @pl.when(step == pl.num_programs(0) - 1)
    def _():
        packed[:wide] = total[...].astype(BF16)
        packed[wide : wide + channels] = jnp.zeros((channels, channels), BF16)
        high = d_table[...].astype(BF16)
        packed[wide + channels : wide + channels + HEAD_ROWS] = high
        packed[wide + channels + HEAD_ROWS :] = (d_table[...] - high.astype(F32)).astype(BF16)


def middle_kernel(count, *refs):
    arrived = refs[:count]
    (d_normed3, normed3, middle, cotangent, gain3_col, bias_w) = refs[count : count + 6]
    normed2, *scales = refs[count + 6 : count + 9]
    refs = refs[1:]
    (update, gate, gain2_col, output_w) = refs[count + 8 : count + 12]
    (d_middle_any, d_gate_any, d_product_any, grad_out) = refs[count + 12 : count + 16]
    send_any = refs[count + 16 : 2 * count + 16]
    d_bias, lay, d_middle_out, d_gate_out, d_product_out = refs[2 * count + 16 : 2 * count + 21]
    send_outs = refs[2 * count + 21 : 3 * count + 21]
    row_sems, product_sems, send_sems = refs[3 * count + 21 :]
    rows, length, channels = middle.shape
    heads = bias_w.shape[1]
    place = lax.axis_index("dap")
    chip = place // (count // 2)
    lines, wide = rows // 2, length // 2
    total = arrived[0][...]
    for ref in arrived[1:]:
        total = total + ref[...].astype(F32)
    d_bias[...] = jnp.zeros_like(d_bias)
    for h in range(heads):
        d_bias[pl.ds(h, rows, stride=HEAD_ROWS), :] = total[:, h * length : (h + 1) * length]
    bias_wide = jnp.concatenate(
        [bias_w[...].astype(F32), jnp.zeros((channels, HEAD_ROWS - heads), F32)], axis=1
    ).astype(BF16)
    gain3 = jnp.broadcast_to(gain3_col[...], (channels, length))
    gain2 = jnp.broadcast_to(gain2_col[...], (channels, length))
    inverse2 = 1.0 / gain2
    grad_out[...] = jnp.zeros_like(grad_out)

    def row(i):
        bias_rows = d_bias[pl.ds(i * HEAD_ROWS, HEAD_ROWS), :].astype(BF16)
        d_normed = d_normed3[i] + mm(bias_wide, bias_rows)
        hat3, scale3 = norm_parts(middle[i].T.astype(F32), 0)
        yield
        d_mid_t = norm_back(d_normed * gain3, hat3, scale3, 0).astype(BF16)
        d_mid_b = d_mid_t.T.astype(F32)
        yield
        d_mid = (cotangent[i].astype(F32) + d_mid_b).astype(BF16)
        d_middle_out[i] = d_mid
        gates = gate[i]
        d_mid = d_mid.astype(F32)
        d_up = d_mid * gates
        d_gate_out[i] = (d_up * update[i].astype(F32) * (1.0 - gates)).astype(BF16)
        return d_up.astype(BF16), bias_rows, normed3[i]

    def two_rows(p):
        low, high = row(p), row(p + lines)
        for _ in range(2):
            next(low)
            next(high)
            yield
        low, high = [lockstep(lambda one: one, [one])[0] for one in (low, high)]
        tiles = []
        for t in range(2):
            d_up = jnp.concatenate(
                [one[0][t * wide : (t + 1) * wide] for one in (low, high)], axis=0
            )
            tiles.append((normed2[chip ^ t, p], d_up, mmt(output_w[...], d_up)))
        yield
        backs = []
        for t, (normed2_t, _, d_hat2) in enumerate(tiles):
            scale2 = jnp.where(
                chip == t, scales[0][pl.ds(p, 1), :], scales[1][pl.ds(p, 1), :]
            )
            hat2 = normed2_t.astype(F32) * inverse2
            backs.append(norm_back(d_hat2 * gain2, hat2, scale2, 0))
        yield
        for group, i in enumerate((p, p + lines)):
            part = slice(group * wide, (group + 1) * wide)
            lay[pl.ds(i, channels, stride=rows), :] = jnp.concatenate(
                [back[:, part] for back in backs], axis=1
            )
        return tiles, (low[1], high[1]), (low[2], high[2])

    def finish(results):
        tiles, bias_rows, normed = [sum((tuple(one) for one in each), ()) for each in zip(*results)]
        grad_out[:channels] += mm(
            jnp.concatenate([one[0] for one in tiles], axis=1),
            jnp.concatenate([one[1] for one in tiles], axis=0),
        )
        grad_out[channels:] += mm(
            jnp.concatenate(bias_rows, axis=1), jnp.concatenate(normed, axis=0)
        )

    over_rows(lines, W_MIDDLE // 2, two_rows, finish)
    departures = [
        pltpu.make_async_copy(d_middle_out, d_middle_any, row_sems.at[0]),
        pltpu.make_async_copy(d_gate_out, d_gate_any, row_sems.at[1]),
    ]
    start(departures)
    line = lax.broadcasted_iota(jnp.int32, (length, length), 0)
    source = ((line // rows) ^ place) * rows + line % rows
    shuffled = (
        (source == lax.broadcasted_iota(jnp.int32, (length, length), 1)).astype(F32).astype(BF16)
    )

    def group(g):
        block = lay[pl.ds(g * length, length), :].astype(BF16)
        d_product_out[pl.ds(g * length, length), :] = block
        turned = mmt(shuffled, block).astype(BF16)
        for offset in range(count):
            send_outs[offset][g] = turned[offset * rows : (offset + 1) * rows]

    parts = 4
    copies = [split_copies(d_product_out, d_product_any, product_sems, parts)] + [
        split_copies(source, target, send_sems.at[at], parts)
        for at, (source, target) in enumerate(zip(send_outs, send_any))
    ]
    share = channels * rows // length // parts
    for part in range(parts):
        side_by_side(part * share, (part + 1) * share, group)
        start([one[part] for one in copies])
    for one in copies:
        wait(one)
    wait(departures)


def gate_back(factors, d_out):
    channels = d_out.shape[0]
    d_value = d_out * factors[:channels].astype(F32)
    d_pre = d_out * factors[channels:].astype(F32)
    return jnp.concatenate([d_value.astype(BF16), d_pre.astype(BF16)], axis=0)


def left_back_kernel(
    near_any, other_any, d_product_any, normed1_any, factors_any, d_gate_any, grad_middle, input_w, gating, *refs
):
    d_normed_any, packed, lay, grad, d_normed, sems = refs[:6]
    right_all, d_product, normed1, factors, d_gate, right_sems, product_sems, in_sems = refs[6:]
    rows, length, channels = normed1.shape
    parts = 4
    share = channels // parts
    wide = length // 2
    chip = lax.axis_index("dap") // (lax.axis_size("dap") // 2)
    spans = [pl.ds(pl.multiple_of((chip ^ side) * wide, wide), wide) for side in range(2)]
    first_arrivals = [
        [
            pltpu.make_async_copy(
                ref.at[pl.ds(part * share, share)],
                right_all.at[pl.ds(part * share, share), span, :],
                right_sems.at[side, part],
            )
            for part in range(parts)
        ]
        for side, (ref, span) in enumerate(zip((near_any, other_any), spans))
    ] + [
        split_copies(d_product_any, d_product, product_sems, parts),
    ]
    for part in range(parts):
        start([copies[part] for copies in first_arrivals])
    arrivals = [
        pltpu.make_async_copy(normed1_any, normed1, in_sems.at[0]),
        pltpu.make_async_copy(factors_any, factors, in_sems.at[1]),
        pltpu.make_async_copy(d_gate_any, d_gate, in_sems.at[2]),
    ]
    start(arrivals)

    def channel(c):
        lay[pl.ds(c, rows, stride=channels), :] = mm(
            d_product[pl.ds(c * rows, rows), :], right_all[c]
        )

    for part in range(parts):
        wait([copies[part] for copies in first_arrivals])
        side_by_side(part * share, (part + 1) * share, channel)
    wait(arrivals)
    weight = jnp.concatenate([input_w[:, : 2 * channels], gating[...]], axis=1)
    grad[...] = jnp.zeros_like(grad)

    def row(i):
        normed = normed1[i]
        d_gate_t = d_gate[i].T
        d_projected = gate_back(factors[i], lay[pl.ds(i * channels, channels), :])
        yield
        d_projected = jnp.concatenate([d_projected, d_gate_t], axis=0)
        d_normed[i] = mm(weight, d_projected)
        return d_projected, normed

    def finish(results):
        d_projected, normed = zip(*results)
        grad[...] += mm(jnp.concatenate(d_projected, axis=1), jnp.concatenate(normed, axis=0))

    parts = 4
    departures = split_copies(d_normed, d_normed_any, sems, parts)
    for part in range(parts):
        over_rows(rows // parts, 8, row, finish, first=part * (rows // parts))
        departures[part].start()
    packed[: 3 * channels] = grad[...].astype(BF16)
    packed[3 * channels :] = grad_middle[...].astype(BF16)
    wait(departures)


def right_back_kernel(count, *refs):
    arrived = refs[:count]
    left_halves = refs[count : 2 * count], refs[2 * count : 3 * count]
    refs = refs[count:]
    normed1_any, factors_any, packed_a, packed_b, d_output = refs[2 * count : 2 * count + 5]
    d_projected_any = refs[2 * count + 5]
    sends = refs[2 * count + 6 : 3 * count + 6]
    lay, grad, packed, d_projected_out, sems, normed1, factors, in_sems = refs[3 * count + 6 :]
    rows, length, channels = normed1.shape
    arrivals = [
        pltpu.make_async_copy(normed1_any, normed1, in_sems.at[0]),
        pltpu.make_async_copy(factors_any, factors, in_sems.at[1]),
    ]
    start(arrivals)
    per = length // rows
    same = (
        lax.broadcasted_iota(jnp.int32, (length, length), 0) // rows
        == lax.broadcasted_iota(jnp.int32, (length, length), 1) // rows
    )
    mask = same.astype(F32).astype(BF16)

    for left_blocks, first in zip(left_halves, (0, left_halves[0][0].shape[0] // per)):

        def group(g, left_blocks=left_blocks, first=first):
            at = first + g
            spread = jnp.concatenate(
                [jnp.concatenate([ref[at]] * per, axis=0) * mask for ref in arrived], axis=1
            )
            lefts = jnp.concatenate(
                [ref[pl.ds(g * per, per)].reshape(length, length) for ref in left_blocks], axis=0
            )
            lay[pl.ds(at * length, length), :] = mm(spread, lefts)

        side_by_side(0, left_blocks[0].shape[0] // per, group)
    wait(arrivals)
    grad[...] = jnp.zeros_like(grad)

    def row(i):
        normed = normed1[i]
        d_projected = gate_back(factors[i], lay[pl.ds(i, channels, stride=rows), :])
        yield
        d_projected_out[i] = d_projected
        return d_projected, normed

    def finish(results):
        d_projected, normed = zip(*results)
        grad[...] += mm(jnp.concatenate(d_projected, axis=1), jnp.concatenate(normed, axis=0))

    parts = 4
    departures = split_copies(d_projected_out, d_projected_any, sems, parts)
    for part in range(parts):
        over_rows(rows // parts, 8, row, finish, first=part * (rows // parts))
        departures[part].start()
    first, second = packed_a.shape[0], packed_b.shape[0]
    packed[:first] = packed_a[...]
    packed[4 * channels : 5 * channels] = d_output[...].astype(BF16)
    packed[first : first + second] = packed_b[...]
    packed[first + second : first + second + 2 * channels] = grad[...].astype(BF16)
    packed[first + second + 2 * channels :] = jnp.zeros_like(
        packed[first + second + 2 * channels :]
    )
    size = sends[0].shape[0]
    for offset in range(count):
        begin = pl.multiple_of((lax.axis_index("dap") ^ offset) * size, HEAD_ROWS)
        sends[offset][...] = packed[pl.ds(begin, size), :]
    wait(departures)


def input_back_kernel(part, parts, *refs):
    sources = refs[:4]
    gain_col, input_w = refs[4:6]
    pair_grad_any = refs[-8]
    d_left, d_right, pair, d_middle, pair_grad, sems, out_sem = refs[-7:]
    rows, length, channels = pair.shape
    span = pl.ds(part * rows, rows)
    arrivals = [
        pltpu.make_async_copy(source.at[span], target, sems.at[at])
        for at, (source, target) in enumerate(zip(sources, (d_left, d_right, pair, d_middle)))
    ]
    start(arrivals)
    weight = input_w[:, 2 * channels :]
    gain = jnp.broadcast_to(gain_col[...], (channels, length))

    def row(i):
        hat, scale = norm_parts(pair[i].T.astype(F32), 0)
        d_normed = d_left[i] + mm(weight, d_right[i])
        yield
        d_pair = norm_back(d_normed * gain, hat, scale, 0).astype(BF16).T.astype(F32)
        yield
        pair_grad[i] = (d_middle[i].astype(F32) + d_pair).astype(BF16)

    wait(arrivals)
    over_rows(rows, 8, row)
    departure = pltpu.make_async_copy(pair_grad, pair_grad_any.at[span], out_sem)
    departure.start()
    departure.wait()


def finish_kernel(count, factor, *refs):
    blocks = refs[:count]
    (input1, gating, output1, bias_w, input3, gain1, gain2, gain3) = refs[count : count + 8]
    (
        gain1_out,
        input1_out,
        gating_out,
        gain2_out,
        output1_out,
        gain3_out,
        bias_out,
        input3_out,
        output3_out,
        table_out,
        packed,
    ) = refs[count + 8 :]
    channels = gating.shape[0]
    heads, types = table_out.shape[:2]
    size = blocks[0].shape[0]
    for offset in range(count):
        begin = pl.multiple_of((lax.axis_index("dap") ^ offset) * size, HEAD_ROWS)
        packed[pl.ds(begin, size), :] = blocks[offset][...].astype(F32) * factor
    at = 0

    def take(rows):
        nonlocal at
        at += rows
        return packed[at - rows : at, :]

    input3_t, output3 = take(4 * channels), take(channels)
    table = take(HEAD_ROWS) + take(HEAD_ROWS)
    left_t, gating_t, output1_grad = take(2 * channels), take(channels), take(channels)
    bias_t, right_t = take(HEAD_ROWS), take(2 * channels)
    input1_t = jnp.concatenate([left_t, right_t], axis=0)

    def dots(weight, grad_t):
        return jnp.sum(weight[...].astype(F32).T * grad_t, axis=0, keepdims=True)

    gain1_out[...] = (dots(input1, input1_t) + dots(gating, gating_t)) / gain1[...]
    output_t = (output1[...].astype(F32) * output1_grad).T
    gain2_out[...] = jnp.sum(output_t, axis=0, keepdims=True) / gain2[...]
    gain3_out[...] = (dots(input3, input3_t) + dots(bias_w, bias_t[:heads])) / gain3[...]
    input1_out[...] = input1_t.T
    gating_out[...] = gating_t.T
    output1_out[...] = output1_grad
    bias_out[...] = bias_t[:heads]
    input3_out[...] = input3_t.T
    output3_out[...] = output3
    for h in range(heads):
        table_out[h] = table[:types, h * types : (h + 1) * types]


def swap(value, axis, step):
    count = lax.axis_size(axis)
    return lax.ppermute(value, axis, [(index, index ^ step) for index in range(count)])


def gather_blocks(block, axis):
    return gather_near(block, swap(block, axis, lax.axis_size(axis) // 2), axis)


def gather_near(block, far, axis):
    return near_blocks(block, axis) + near_blocks(far, axis)


def near_blocks(block, axis):
    half = lax.axis_size(axis) // 2
    blocks = {0: block}
    for bit in reversed(range(half.bit_length() - 1)):
        step = 1 << bit
        for offset, held in list(blocks.items()):
            blocks[offset ^ step] = swap(held, axis, step)
    return [blocks[offset] for offset in range(len(blocks))]


def sum_over(value, axis):
    step = 1
    while step < lax.axis_size(axis):
        value = value + swap(value, axis, step)
        step *= 2
    return value


def per_device(
    pair_rep,
    cotangent,
    tok_mask,
    tok_types,
    pair_mask,
    triangle_gain,
    triangle_input,
    triangle_gating,
    product_gain,
    triangle_output,
    attend_gain,
    attend_bias,
    attend_input,
    attend_output,
    type_table,
):
    slab = pair_rep[0]
    cot = cotangent[0]
    rows, length, channels = slab.shape
    heads, types = type_table.shape[:2]
    count = lax.axis_size("dap")
    gain1_row, gain3_row = triangle_gain[None, :], attend_gain[None, :]
    gain1_col, gain2_col, gain3_col = (
        triangle_gain[:, None],
        product_gain[:, None],
        attend_gain[:, None],
    )
    vmem = pl.BlockSpec(memory_space=pltpu.VMEM)
    anywhere = pl.BlockSpec(memory_space=pltpu.HBM)
    smem = pl.BlockSpec(memory_space=pltpu.SMEM)
    cell_buffer = pltpu.VMEM((rows, length, channels), BF16)
    cells = (rows, length, channels)
    turned = (rows, channels, length)

    half = rows // 2
    normed1, right_halves, live_halves = None, [], []
    for part in range(2):
        given = [] if normed1 is None else [normed1]
        normed1, right_part, live_part = call(
            partial(right_kernel, part),
            [
                (cells, BF16),
                ((channels, half, length), BF16),
                ((half, length), F32),
            ],
            [slab, pair_mask[0], tok_mask, gain1_row, triangle_input, *given],
            in_specs=[anywhere] * (5 + len(given)),
            out_specs=[anywhere, vmem, vmem],
            aliases={5: 0} if given else None,
            scratch=[
                pltpu.VMEM((half, length, channels), BF16),
                pltpu.VMEM((half, length), jnp.int32),
                pltpu.VMEM((1, length), jnp.int32),
                pltpu.VMEM((1, channels), F32),
                pltpu.VMEM((channels, 4 * channels), BF16),
                pltpu.VMEM((2 * channels, channels), BF16),
                pltpu.VMEM((channels * half, length), F32),
                pltpu.VMEM((half, length, channels), BF16),
                pltpu.SemaphoreType.DMA((6,)),
            ],
            us=3.0,
            name="right_projection",
        )
        right_halves.append(right_part)
        live_halves.append(live_part)
    low_count = 5 * channels // 16
    left_high, gate, live, left_factors, left_low = call(
        partial(left_kernel, 2),
        [
            ((channels - low_count, rows, length), BF16),
            (cells, F32),
            ((rows, length), F32),
            ((rows, 2 * channels, length), BF16),
            ((low_count, rows, length), BF16),
        ],
        [normed1, *live_halves, triangle_input, triangle_gating],
        in_specs=[anywhere] + [vmem] * 4,
        out_specs=[vmem, anywhere, vmem, anywhere, anywhere],
        scratch=[
            pltpu.VMEM((2 * channels, channels), BF16),
            pltpu.VMEM((channels * rows, length), F32),
            pltpu.VMEM(cells, F32),
            pltpu.VMEM((rows, 2 * channels, length), BF16),
            cell_buffer,
            pltpu.SemaphoreType.DMA((2,)),
            pltpu.SemaphoreType.DMA((2, 2)),
            pltpu.SemaphoreType.DMA,
            pltpu.VMEM((low_count, rows, length), BF16),
        ],
        us=6.0,
        name="left_projection",
    )
    far = [swap(part, "dap", count // 2) for part in right_halves]
    live, far[0] = lax.optimization_barrier((live, far[0]))
    right_factors, d_gated = call(
        partial(factor_kernel, 2),
        [((rows, 2 * channels, length), BF16), (cells, BF16)],
        [live, triangle_input, attend_output, normed1, cot],
        in_specs=[vmem] * 3 + [anywhere] * 2,
        out_specs=[anywhere] * 2,
        scratch=[
            cell_buffer,
            cell_buffer,
            pltpu.VMEM((rows, 2 * channels, length), BF16),
            cell_buffer,
            pltpu.SemaphoreType.DMA((2, 2)),
            pltpu.SemaphoreType.DMA((2, 2)),
        ],
        us=5.0,
        name="right_factors",
    )
    lines, wide = rows // 2, length // 2

    def product_side(side, halves, given=()):
        blocks = [halves[index % 2][index // 2] for index in range(count)]
        return call(
            partial(product_kernel, count, side),
            [
                ((2, lines, channels, length), BF16),
                (cells, BF16),
                (cells, BF16),
                (cells, BF16),
                ((channels, wide, length), BF16),
                ((lines, length), F32),
                ((rows, heads * length), BF16) if side else ((lines * HEAD_ROWS, length), F32),
            ],
            [*blocks, left_low, left_high, slab, gate, gain2_col, gain3_row]
            + [triangle_output, attend_bias, *given],
            in_specs=[vmem] * count
            + [anywhere, vmem]
            + [anywhere] * 2
            + [vmem] * 4
            + [anywhere] * (5 if side else 0),
            out_specs=[anywhere] * 5 + [vmem, vmem if side else anywhere],
            scratch=[
                pltpu.VMEM((lines * channels, length), F32),
                pltpu.VMEM((lines * HEAD_ROWS, length), F32),
                pltpu.VMEM((channels, wide, length), BF16),
                pltpu.VMEM((rows, wide, channels), BF16),
                pltpu.VMEM((rows, wide, channels), F32),
                pltpu.VMEM((lines, channels, length), BF16),
            ]
            + [pltpu.VMEM((rows, wide, channels), BF16)] * 3
            + [
                pltpu.SemaphoreType.DMA((3,)),
                pltpu.SemaphoreType.DMA((4, 4)),
                pltpu.SemaphoreType.DMA,
                pltpu.SemaphoreType.DMA,
                pltpu.VMEM((lines * HEAD_ROWS, length), F32),
                pltpu.VMEM(left_low.shape, BF16),
            ],
            aliases={count + 9 + at: at for at in range(4)} if side else None,
            us=7.0,
            name="product_other" if side else "product_near",
        )

    *shared, right_near, scale2_near, bias_near = product_side(
        0, [near_blocks(part, "dap") for part in right_halves]
    )
    shared[0], d_gated, far[1] = lax.optimization_barrier((shared[0], d_gated, far[1]))
    left_low_sent, _ = lax.optimization_barrier((left_low, far[1]))
    low_far = swap(left_low_sent, "dap", count // 2)
    *shared, right_other, scale2_other, bias_rows = product_side(
        1, [near_blocks(part, "dap") for part in far], [bias_near, *shared]
    )
    normed2, update, middle, normed3 = shared
    right_sides = [right_near, right_other]
    normed3, low_far = lax.optimization_barrier((normed3, low_far))
    bias_blocks = [bias_rows] + [
        swap(bias_rows, "dap", offset) for offset in reversed(range(1, count))
    ][::-1]

    block = 8
    steps = rows // block
    by_row = pl.BlockSpec((block, length, channels), lambda step: (step, 0, 0))
    by_row_wide = pl.BlockSpec((block, 4 * channels, length), lambda step: (step, 0, 0))

    def fixed(*shape):
        return pl.BlockSpec(shape, lambda step: (0,) * len(shape))

    projected3, query, gate3 = call(
        partial(project_kernel, (channels // heads) ** -0.5),
        [((rows, 3 * channels, length), BF16), (cells, BF16), (cells, F32)],
        [normed3, attend_input],
        in_specs=[anywhere] * 2,
        scratch=[
            cell_buffer,
            pltpu.VMEM((channels, 4 * channels), BF16),
            pltpu.VMEM((3 * channels, channels), BF16),
            pltpu.VMEM((channels, 2 * channels), BF16),
            pltpu.VMEM((rows, 3 * channels, length), BF16),
            cell_buffer,
            pltpu.VMEM(cells, F32),
            pltpu.SemaphoreType.DMA((4,)),
            pltpu.SemaphoreType.DMA((3, 4)),
            pltpu.SemaphoreType.DMA,
        ],
        out_specs=[anywhere] * 3,
        us=5.0,
        name="attention_projections",
    )
    projected3, *bias_blocks = lax.optimization_barrier((projected3, *bias_blocks))
    left_high_sent, _ = lax.optimization_barrier((left_high, bias_blocks[-1]))
    high_far = swap(left_high_sent, "dap", count // 2)
    attend_outs = call(
        partial(attend_kernel, count),
        [
            (cells, BF16),
            ((rows, 4 * channels, length), BF16),
            ((HEAD_ROWS, channels), F32),
            ((rows, heads * length), F32),
        ]
        + [((rows, heads * length), BF16)] * (count - 1),
        [type_table.reshape(heads * types, types), *bias_blocks]
        + [tok_types, tok_types.reshape(length, 1), live]
        + [projected3, query, gate3, d_gated],
        in_specs=[smem] + [vmem] * (count + 3) + [anywhere] * 4,
        out_specs=[anywhere] + [vmem] * (count + 2),
        scratch=[
            pltpu.VMEM((length, heads * length), F32),
            pltpu.VMEM((length, heads * length), F32),
            pltpu.VMEM((channels, heads * length), BF16),
        ]
        + [pltpu.VMEM((rows, 3 * channels, length), BF16), cell_buffer, pltpu.VMEM(cells, F32)]
        + [cell_buffer] * 2
        + [
            pltpu.SemaphoreType.DMA((4, rows // W_ATTEND)),
            pltpu.SemaphoreType.DMA((rows // W_ATTEND,)),
        ],
        us=20.0,
        name="attention",
    )
    gated, d_projected3, d_table = attend_outs[:3]
    d_bias_parts = [attend_outs[3]] + [
        swap(attend_outs[3 + offset], "dap", offset) for offset in range(1, count)
    ]
    d_bias_parts[1], high_far = lax.optimization_barrier((d_bias_parts[1], high_far))
    d_normed3, packed_a = call(
        projection_kernel,
        [(turned, F32), ((4 * channels + channels + 2 * HEAD_ROWS, channels), BF16)],
        [d_projected3, normed3, attend_input, d_table],
        grid=(steps,),
        in_specs=[by_row_wide, by_row, fixed(channels, 4 * channels)]
        + [fixed(HEAD_ROWS, channels)],
        out_specs=[
            pl.BlockSpec((block, channels, length), lambda step: (step, 0, 0)),
            fixed(5 * channels + 2 * HEAD_ROWS, channels),
        ],
        scratch=[pltpu.VMEM((4 * channels, channels), F32)],
        us=0.5,
        name="projection_back",
    )
    groups = channels * rows // length
    middle_outs = call(
        partial(middle_kernel, count),
        [
            (cells, BF16),
            (cells, BF16),
            ((channels * rows, length), BF16),
            ((channels + HEAD_ROWS, channels), F32),
        ]
        + [((groups, rows, length), BF16)] * count,
        [*d_bias_parts, d_normed3, normed3, middle, cot, gain3_col, attend_bias]
        + [normed2, scale2_near, scale2_other, update, gate, gain2_col, triangle_output],
        out_specs=[anywhere] * 3 + [vmem] + [anywhere] * count,
        scratch=[
            pltpu.VMEM((rows * HEAD_ROWS, length), F32),
            pltpu.VMEM((channels * rows, length), F32),
            cell_buffer,
            cell_buffer,
            pltpu.VMEM((channels * rows, length), BF16),
        ]
        + [pltpu.VMEM((groups, rows, length), BF16)] * count
        + [
            pltpu.SemaphoreType.DMA((2,)),
            pltpu.SemaphoreType.DMA((4,)),
            pltpu.SemaphoreType.DMA((count, 4)),
        ],
        us=12.0,
        name="middle_back",
    )
    d_middle, d_gate, d_product, grad_middle = middle_outs[:4]
    d_middle, low_far, high_far = lax.optimization_barrier((d_middle, low_far, high_far))
    left_blocks = gather_near(left_low, low_far, "dap") + gather_near(left_high, high_far, "dap")
    product_parts = [middle_outs[4]] + [
        swap(middle_outs[4 + offset], "dap", offset) for offset in range(1, count)
    ]
    d_left, packed_b = call(
        left_back_kernel,
        [(turned, F32), ((4 * channels + HEAD_ROWS, channels), BF16)],
        [*right_sides, d_product, normed1, left_factors, d_gate, grad_middle]
        + [triangle_input, triangle_gating],
        scratch=[
            pltpu.VMEM((rows * channels, length), F32),
            pltpu.VMEM((3 * channels, channels), F32),
            pltpu.VMEM(turned, F32),
            pltpu.SemaphoreType.DMA((4,)),
            pltpu.VMEM((channels, length, length), BF16),
            pltpu.VMEM((channels * rows, length), BF16),
            cell_buffer,
            pltpu.VMEM((rows, 2 * channels, length), BF16),
            cell_buffer,
            pltpu.SemaphoreType.DMA((2, 4)),
            pltpu.SemaphoreType.DMA((4,)),
            pltpu.SemaphoreType.DMA((3,)),
        ],
        in_specs=[anywhere] * 6 + [vmem] * 3,
        out_specs=[anywhere, vmem],
        us=10.0,
        name="left_back",
    )
    gated, d_left = lax.optimization_barrier((gated, d_left))
    pair_out, d_output = call(
        output_kernel,
        [(cells, BF16), ((channels, channels), F32)],
        [gated, middle, cot, attend_output],
        in_specs=[anywhere] * 3 + [vmem],
        out_specs=[anywhere, vmem],
        scratch=[cell_buffer] * 4
        + [pltpu.SemaphoreType.DMA((3, 4)), pltpu.SemaphoreType.DMA((4,))],
        us=0.1,
        name="attention_output",
    )
    used = packed_a.shape[0] + packed_b.shape[0] + 2 * channels
    share = -(-used // (count * HEAD_ROWS)) * HEAD_ROWS
    right_outs = call(
        partial(right_back_kernel, count),
        [((rows, 2 * channels, length), BF16)] + [((share, channels), BF16)] * count,
        [*product_parts, *left_blocks, normed1, right_factors, packed_a, packed_b]
        + [d_output],
        in_specs=[vmem] * (3 * count) + [anywhere] * 2 + [vmem] * 3,
        out_specs=[anywhere] + [vmem] * count,
        scratch=[
            pltpu.VMEM((channels * rows, length), F32),
            pltpu.VMEM((2 * channels, channels), F32),
            pltpu.VMEM((share * count, channels), BF16),
            pltpu.VMEM((rows, 2 * channels, length), BF16),
            pltpu.SemaphoreType.DMA((4,)),
            cell_buffer,
            pltpu.VMEM((rows, 2 * channels, length), BF16),
            pltpu.SemaphoreType.DMA((2,)),
        ],
        us=7.0,
        name="right_back",
    )
    d_right = right_outs[0]
    parts = 4
    some = (rows // parts, length, channels)
    pair_grad = None

    def input_back(part, pair_grad):
        given = [] if pair_grad is None else [pair_grad]
        (pair_grad,) = call(
            partial(input_back_kernel, part, parts),
            [(cells, BF16)],
            [d_left, d_right, slab, d_middle, gain1_col, triangle_input, *given],
            in_specs=[anywhere] * 4 + [vmem] * 2 + [anywhere] * len(given),
            out_specs=[anywhere],
            scratch=[
                pltpu.VMEM((rows // parts, channels, length), F32),
                pltpu.VMEM((rows // parts, 2 * channels, length), BF16),
                pltpu.VMEM(some, BF16),
                pltpu.VMEM(some, BF16),
                pltpu.VMEM(some, BF16),
                pltpu.SemaphoreType.DMA((4,)),
                pltpu.SemaphoreType.DMA,
            ],
            aliases={6: 0} if given else None,
            us=3.0,
            name="input_back",
        )
        return pair_grad

    shares = dict(enumerate(right_outs[1:]))
    step = 1
    done = 0
    while step < count:
        if 2 * step == count:
            pair_grad = input_back(done, pair_grad)
            done += 1
        for offset in [one for one in shares if one & step]:
            arrived = swap(shares.pop(offset), "dap", step)
            shares[offset ^ step] = shares[offset ^ step] + arrived
        step *= 2
    grad_share, pair_grad = lax.optimization_barrier((shares[0], pair_grad))
    step = 1
    while step < lax.axis_size("dp"):
        if step > 1 and done < parts - 1:
            pair_grad = input_back(done, pair_grad)
            grad_share, pair_grad = lax.optimization_barrier((grad_share, pair_grad))
            done += 1
        grad_share = grad_share + swap(grad_share, "dp", step)
        step *= 2
    grad_far = swap(grad_share, "dap", count // 2)
    while done < parts:
        pair_grad = input_back(done, pair_grad)
        done += 1
    pair_grad, grad_far = lax.optimization_barrier((pair_grad, grad_far))
    grad_blocks = gather_near(grad_share, grad_far, "dap")
    weights = (triangle_input, triangle_gating, triangle_output, attend_bias, attend_input)
    gains = (gain1_row, product_gain[None, :], gain3_row)
    grads = call(
        partial(finish_kernel, count, (length * length * lax.axis_size("dp")) ** (-0.5)),
        [
            ((1, channels), F32),
            (triangle_input.shape, F32),
            (triangle_gating.shape, F32),
            ((1, channels), F32),
            (triangle_output.shape, F32),
            ((1, channels), F32),
            (attend_bias.shape[::-1], F32),
            (attend_input.shape, F32),
            (attend_output.shape, F32),
            (type_table.shape, F32),
        ],
        [*grad_blocks, *weights, *gains],
        scratch=[pltpu.VMEM((share * count, channels), F32)],
        us=3.0,
        name="scale_gradients",
    )
    grads = [grad[0] if grad.shape[0] == 1 else grad for grad in grads]
    grads[6] = grads[6].T
    return (pair_out[None], pair_grad[None], *grads)


def solution(mesh):
    return jax.shard_map(
        per_device,
        mesh=mesh,
        in_specs=(
            P("dp", "dap", None, None),
            P("dp", "dap", None, None),
            P("dp", None),
            P("dp", None),
            P("dp", "dap", None),
        )
        + (P(),) * 10,
        out_specs=(
            P("dp", "dap", None, None),
            P("dp", "dap", None, None),
        )
        + (P(),) * 10,
        check_vma=False,
    )
```
